128 devices in a mesh: dp: 16 (over x, y_hi, core), label: 8 (over z, y_lo).
Axes of the slice: x: 4, y: 4 (y_hi: 2, y_lo: 2; y = y_hi * 2 + y_lo), z: 4, core: 2. Of those that a mesh axis runs over, the one named last changes fastest.
Arguments:
- documents: bfloat16 [2048, 768], P('dp'), as said below
- labels: bfloat16 [262144, 768], P(('dp', 'label')), as said below
- target_owner: int32 [2048, 17, 1], P(('dp', 'label')), may hold values from 0 to 127; in each aligned block of 272 rows (0 to 271, 272 to 543, ..., all dimensions but the last counted through in order) at most 8 rows name the same one
- target_row: int32 [2048, 17], P(('dp', 'label')), may hold values from 0 to 2047
Outputs:
- doc_loss: float32 [2048], P(('dp', 'label'))
- doc_grad: float32 [2048, 768], P(('dp', 'label'))
- label_grad: float32 [262144, 768], P(('dp', 'label'))
The draws below stay inside these ranges and needn't reach their ends.
Inputs may be any that keep to these rules, and one draw needn't show every extreme that they name: `target_owner`: within the rows of one device (aligned blocks of 16 documents with all their 17 columns) no owner is named more than 8 times, and in some block one owner is named exactly 8 times. The listed label is row target_owner * 2048 + target_row of the cache. `documents`: embedding rows. `labels`: embedding rows.
All inputs are finite; a program needn't handle non-finite values.
Results may differ from the reference program's by a relative error of at most 0.0029.
Values may be sent and summed in bfloat16 or wider, within the bound.
A program may use at most 128 MiB of HBM per device.

```python
import math
import jax
import jax.numpy as jnp
import numpy as np
from jax import lax

D = 768
NEG = 16
LAB_DEV = 2048
DOCS = 2048
LABELS = 262144
DOC_SUB = 16
CAP = 8
DEVICES = 128


def draw_documents(key, part):
    key = jax.random.fold_in(key, 1)
    values = jax.random.normal(key, (DOCS, D), jnp.float32)
    return values.astype(jnp.bfloat16)


def draw_labels(key, part):
    key = jax.random.fold_in(key, 2)
    values = jax.random.normal(key, (LABELS, D), jnp.float32)
    return values.astype(jnp.bfloat16)


def set_ends(values, own_key, low, largest):
    longest = values.shape.index(max(values.shape))
    spots = []
    for shift in (0, 1):
        where = [jax.random.randint(jax.random.fold_in(own_key, axis), (), 0, length) for axis, length in enumerate(values.shape)]
        where[longest] = (where[longest] + shift) % values.shape[longest]
        spots.append(tuple(where))
    return values.at[spots[0]].set(low).at[spots[1]].set(largest)


def routed_block(key, own, number, rows, number_of, top, limit, lean):
    ranking = jax.random.permutation(key, number_of)
    crowded, usual = portions_of(number_of, rows * top, limit, lean, True), portions_of(number_of, rows * top, limit, lean, False)
    places = jnp.arange(number_of)

    def named(sizes, turn):
        used = int((sizes > 0).sum())
        fixed = max(1, used // 4)
        passed = fixed + (places - fixed + turn * (used - fixed)) % max(1, number_of - fixed)
        return jnp.zeros((number_of,), jnp.int32).at[ranking[jnp.where(places < fixed, places, passed)]].set(jnp.asarray(sizes, jnp.int32))

    sizes = jnp.where(number % 4 == 0, named(crowded, number // 4), named(usual, number - number // 4 - 1))
    mixed = jax.random.permutation(jax.random.fold_in(own, 3), number_of)
    giver, sink = mixed[0:number_of // 2 * 2:2], mixed[1:number_of // 2 * 2:2]
    room = jnp.minimum(sizes[giver] - 1, limit - sizes[sink]) // 2
    room = jnp.where((giver == ranking[0]) | (sink == ranking[0]) | (sizes[sink] == 0), 0, jnp.maximum(room, 0))
    passed = jax.random.randint(jax.random.fold_in(own, 4), (number_of // 2,), 0, 1 << 20) % (room + 1)
    sizes = sizes.at[giver].add(-passed).at[sink].add(passed)
    items = jnp.searchsorted(jnp.cumsum(sizes), jnp.arange(rows * top), side="right").astype(jnp.int32)
    grid = items.reshape(top, rows).T
    grid = grid[jax.random.permutation(jax.random.fold_in(own, 1), rows)]
    turn = jax.random.randint(jax.random.fold_in(own, 2), (rows, 1), 0, top)
    return jnp.take_along_axis(grid, (jnp.arange(top)[None, :] + turn) % top, axis=1)


def portions_of(number_of, total, bound, skew, full):
    loads = [(1 << 20) // math.isqrt(rank ** skew) + 1 for rank in range(1, number_of + 1)]
    largest = bound if full else min(bound, max(-(-total // number_of), total * loads[0] // sum(loads)))
    least = 1 if total - largest >= number_of - 1 else 0
    holding, rest = [largest] + [least] * (number_of - 1), total - largest - least * (number_of - 1)
    while rest > 0:
        movable = [i for i in range(1, number_of) if holding[i] < largest] or [i for i in range(1, number_of) if holding[i] < bound]
        mass, remaining = sum([loads[i] for i in movable]), rest
        for i in movable:
            addition = min(bound - holding[i], max(1, remaining * loads[i] // mass), rest)
            holding[i] = holding[i] + addition
            rest = rest - addition
    return np.array(holding)


def setup_inputs(seed: int = 0) -> dict:
    streams_of = jax.random.split(jax.random.key(seed), 5)
    documents = draw_documents(jax.random.fold_in(streams_of[4], 71), 0)
    labels = draw_labels(jax.random.fold_in(streams_of[4], 71), 0)
    target_owner_keys = jax.random.split(jax.random.fold_in(streams_of[2], 1), DOCS * (NEG + 1) // (DOC_SUB * (NEG + 1)))
    target_owner_turns = jax.random.permutation(jax.random.fold_in(streams_of[2], 3), DOCS * (NEG + 1) // (DOC_SUB * (NEG + 1)))
    target_owner = jax.vmap(lambda own, number: routed_block(jax.random.fold_in(streams_of[2], 2), own, number, DOC_SUB * (NEG + 1), DEVICES, 1, CAP, 2))(target_owner_keys, target_owner_turns).reshape((DOCS, NEG + 1, 1))
    target_row = set_ends(jax.random.randint(streams_of[3], (DOCS, NEG + 1), 0, LAB_DEV), jax.random.fold_in(streams_of[3], 1), 0, LAB_DEV - 1).astype(jnp.int32)
    return {"documents": documents, "labels": labels, "target_owner": target_owner, "target_row": target_row}


def reference(documents, labels, target_owner, target_row):
    score_factor = 4.0 / math.sqrt(D)
    blocks = labels.reshape(LABELS // LAB_DEV, LAB_DEV, D)

    def scores_of(label_block):
        return score_factor * jnp.dot(documents, label_block.T, preferred_element_type=jnp.float32)

    def first_pass(running, label_block):
        block_scores = scores_of(label_block)
        new_top = jnp.maximum(running[0], lax.optimization_barrier(jnp.max(block_scores, axis=1)))
        new_total = running[1] * jnp.exp(running[0] - new_top) + lax.optimization_barrier(jnp.sum(jnp.exp(block_scores - new_top[:, None]), axis=1))
        return ((new_top, new_total), None)
    initial = (jnp.full((DOCS,), -jnp.inf, jnp.float32), jnp.zeros((DOCS,), jnp.float32))
    (row_top, row_total), unused = lax.scan(first_pass, initial, blocks)
    log_total = row_top + jnp.log(row_total)

    def second_pass(doc_acc, label_block):
        block_scores = scores_of(label_block)
        probabilities = jnp.exp(block_scores - log_total[:, None]).astype(jnp.bfloat16)
        doc_acc = doc_acc + score_factor * jnp.dot(probabilities, label_block, preferred_element_type=jnp.float32)
        block_grad = score_factor * jnp.dot(probabilities.T, documents, preferred_element_type=jnp.float32)
        return (doc_acc, block_grad)
    soft_doc, soft_label = lax.scan(second_pass, jnp.zeros((DOCS, D), jnp.float32), blocks)
    soft_label = soft_label.reshape(LABELS, D)
    label_ids = (target_owner[:, :, 0] * LAB_DEV + target_row).astype(jnp.int32)
    fetched = jnp.take(labels, label_ids.reshape(-1), axis=0).reshape(DOCS, NEG + 1, D)
    target_scores = score_factor * jnp.einsum('dkf,df->dk', fetched.astype(jnp.float32), documents.astype(jnp.float32))
    positive = target_scores[:, 0]
    margin_gaps = target_scores[:, 1:] - positive[:, None] + 1.0
    doc_loss = log_total - positive + lax.optimization_barrier(jnp.sum(jax.nn.softplus(margin_gaps), axis=1)) / NEG
    weights = jax.nn.sigmoid(margin_gaps) / NEG
    coefficient = jnp.concatenate([-1.0 - lax.optimization_barrier(jnp.sum(weights, axis=1, keepdims=True)), weights], axis=1)
    hard_doc = score_factor * lax.optimization_barrier(jnp.sum(coefficient[:, :, None] * fetched.astype(jnp.float32), axis=1))
    doc_grad = soft_doc + hard_doc
    row_grads = score_factor * coefficient[:, :, None] * documents.astype(jnp.float32)[:, None, :]
    hard_label = jax.ops.segment_sum(row_grads.reshape(DOCS * (NEG + 1), D), label_ids.reshape(-1), num_segments=LABELS)
    label_grad = soft_label + hard_label
    return (doc_loss, doc_grad, label_grad)
```

```python
import functools
import math

import jax
import jax.numpy as jnp
from jax import lax
from jax.experimental import pallas as pl
from jax.experimental.pallas import tpu as pltpu
from jax.sharding import PartitionSpec as P

MESH = pl.DeviceIdType.MESH
F32 = jnp.float32
BF16 = jnp.bfloat16

NX, NYH, NC, NZ, NYL = 4, 2, 2, 4, 2
DP, LB = 16, 8
DEV = DP * LB
SUB = 16
BLK = SUB * LB
GRP = 2 * BLK
DOCS = DP * BLK
D = 768
ROWS = 2048
COLS = 17
TW = 384
MSG = TW + 128
SLOTS = 8
BIG = float(2 ** 23)
FG = 256
C = 4.0 / math.sqrt(D)
TILE = 512

NT = (((1,), (1,)), ((), ()))


def mm(a, b):
    return jnp.dot(a, b, preferred_element_type=F32)


def split(v):
    hi = v.astype(BF16)
    return hi, (v - hi.astype(F32)).astype(BF16)


def kernel(
    docs_ref, labels_ref, ids_ref,
    lg_ref, dg_ref, loss_ref, logt_ref,
    dall, labt, e_ref, u_ref, rc_ref, w_ref, r1_ref, v1_ref, r2_ref, v2_ref, r3_ref,
    idl_ref, idg_ref, keys_ref, rowt_ref, lrow_ref, grow_ref, ch_ref, cl_ref,
    ts_ref, tr_ref, ss_ref, sr_ref, ca_ref, scale_ref, stage_ref,
    own_sem, doc_send, doc_recv, fwd_send, sib_send, sib_recv,
    idl_send, idl_recv, idg_send, idg_recv,
    t1_send, t1_recv, t2_send, t2_recv, t3_send, t3_recv,
    rc_send, rc_recv, rs_send, rs_recv, out_sem,
):
    dp = lax.axis_index("dp")
    lb = lax.axis_index("label")
    x, yh, co = dp // 4, (dp // 2) % 2, dp % 2
    z, yl = lb // 2, lb % 2
    y = yh * 2 + yl
    me = dp * LB + lb

    def dev(x_, yh_, co_, z_, yl_):
        return ((x_ * 2 + yh_) * 2 + co_, z_ * 2 + yl_)

    sib = dev(x, yh, 1 - co, z, yl)
    ypart = dev(x, 1 - yh, co, z, 1 - yl)

    def on_axis(axis, pos):
        if axis == 0:
            return dev(pos, yh, co, z, yl)
        if axis == 1:
            return dev(x, pos // 2, co, z, pos % 2)
        return dev(x, yh, co, pos, yl)

    def remote(src, dst, ssem, rsem, to):
        return pltpu.make_async_remote_copy(
            src_ref=src, dst_ref=dst, send_sem=ssem, recv_sem=rsem, device_id=to, device_id_type=MESH
        )

    barrier = pltpu.get_barrier_semaphore()

    def greet_dp(i, _):
        pl.semaphore_signal(barrier, inc=1, device_id=((dp + i) % DP, lb), device_id_type=MESH)
        return 0

    def greet_lb(i, _):
        pl.semaphore_signal(barrier, inc=1, device_id=(dp, (lb + i) % LB), device_id_type=MESH)
        return 0

    lax.fori_loop(1, DP, greet_dp, 0)
    lax.fori_loop(1, LB, greet_lb, 0)
    pl.semaphore_signal(barrier, inc=1, device_id=ypart, device_id_type=MESH)
    pl.semaphore_wait(barrier, DP - 1 + LB - 1 + 1)

    g_own = x * 2 + yh

    def doc_slot(group, core):
        return dall.at[group * 2 + core]

    own_copy = pltpu.make_async_copy(docs_ref, doc_slot(g_own, co), own_sem)
    own_copy.start()

    def sib_copy(k, src, group):
        return remote(src, doc_slot(group, co), sib_send.at[k], sib_recv.at[k], sib)

    sib_copy(0, docs_ref, g_own).start()
    first_sends = [
        remote(docs_ref, doc_slot(g_own, co), doc_send.at[0], doc_recv.at[1], ypart),
        remote(docs_ref, doc_slot(g_own, co), doc_send.at[1], doc_recv.at[3], on_axis(0, (x + 1) % NX)),
        remote(docs_ref, doc_slot(g_own, co), doc_send.at[2], doc_recv.at[2], on_axis(0, (x + 3) % NX)),
        remote(docs_ref, doc_slot(g_own, co), doc_send.at[3], doc_recv.at[4], on_axis(0, (x + 2) % NX)),
    ]
    for copy in first_sends:
        copy.start()

    def idl_copy(i):
        return remote(ids_ref, idl_ref.at[lb], idl_send.at[i], idl_recv.at[lb], (dp, (lb + i) % LB))

    lax.fori_loop(1, LB, lambda i, _: (idl_copy(i).start(), 0)[1], 0)

    def turn(i, _):
        r = pl.multiple_of(i * 256, 256)
        labt[:, pl.ds(r, 256)] = labels_ref[pl.ds(r, 256), :].T
        return 0

    lax.fori_loop(0, ROWS // 256, turn, 0)
    ts_ref[...] = jnp.zeros_like(ts_ref)

    def idl_sum(i, acc):
        p = (lb + i) % LB
        remote(ids_ref, idl_ref.at[p], idl_send.at[i], idl_recv.at[p], (dp, p)).wait_recv()
        return acc + idl_ref[p]

    idg_ref[dp] = lax.fori_loop(1, LB, idl_sum, ids_ref[...])

    def idg_copy(i):
        return remote(idg_ref.at[dp], idg_ref.at[dp], idg_send.at[i], idg_recv.at[dp], ((dp + i) % DP, lb))

    lax.fori_loop(1, DP, lambda i, _: (idg_copy(i).start(), 0)[1], 0)

    def place(k):
        dx = jnp.where((k == 2) | (k == 5), 1, jnp.where((k == 3) | (k == 6), 3, jnp.where((k == 4) | (k == 7), 2, 0)))
        dy = jnp.where((k == 1) | (k >= 5), 1, 0)
        return ((x + dx) % NX) * 2 + (yh + dy) % 2

    own_copy.wait()

    def score_step(k, _):
        nxt = k + 1

        @pl.when(nxt < 8)
        def _():
            g1 = place(nxt)
            slot = doc_slot(g1, co)
            remote(slot, slot, doc_send.at[0], doc_recv.at[nxt], ypart).wait_recv()
            sib_copy(nxt, slot, g1).start()

            @pl.when(nxt == 1)
            def _():
                remote(slot, slot, fwd_send.at[0], doc_recv.at[6], on_axis(0, (x + 1) % NX)).start()
                remote(slot, slot, fwd_send.at[1], doc_recv.at[5], on_axis(0, (x + 3) % NX)).start()

            @pl.when(nxt == 4)
            def _():
                remote(slot, slot, fwd_send.at[2], doc_recv.at[7], ypart).start()

        g = place(k)
        other = doc_slot(g, 1 - co)
        remote(other, other, sib_send.at[k], sib_recv.at[k], sib).wait_recv()
        block = dall[pl.ds(g * 2, 2)].reshape(GRP, D)
        s = lax.dot_general(labels_ref[...], block, NT, preferred_element_type=F32)
        top = jnp.max(s, axis=0, keepdims=True)
        e = jnp.exp((s - top) * C)
        e_ref[:, pl.ds(pl.multiple_of(g * GRP, GRP), GRP)] = e
        total = jnp.sum(e, axis=0, keepdims=True)
        top = top * C
        for h in range(2):
            ts_ref[g * 2 + h, 0:1, TW:MSG] = top[:, h * BLK:(h + 1) * BLK]
            ts_ref[g * 2 + h, 1:2, TW:MSG] = total[:, h * BLK:(h + 1) * BLK]
        return 0

    lax.fori_loop(0, 8, score_step, 0)

    lane_t = lax.broadcasted_iota(jnp.int32, (LB, TW), 1).astype(F32)
    base = (me * ROWS).astype(F32)

    def find(b, _):
        @pl.when(b != dp)
        def _():
            remote(idg_ref.at[b], idg_ref.at[b], idg_send.at[b], idg_recv.at[b], (b, lb)).wait_recv()

        rel = idg_ref[b] - base
        key = jnp.where((rel >= 0.0) & (rel < float(ROWS)), lane_t * float(ROWS) + rel, BIG)
        for k in range(SLOTS):
            low = jnp.min(key, axis=1, keepdims=True)
            keys_ref[pl.ds(pl.multiple_of((b * SLOTS + k) * 8, 8), 8), :] = jnp.broadcast_to(low, (8, 128))
            key = jnp.where(key == low, BIG, key)
        return 0

    lax.fori_loop(0, DP, find, 0)

    def parts_of(key):
        t = jnp.floor(key * (1.0 / ROWS))
        row = jnp.where(key < BIG, key - t * float(ROWS), -1.0)
        return t, row

    lane_rows = lax.broadcasted_iota(jnp.int32, (256, ROWS), 1).astype(F32)

    def fetch(i, _):
        r = pl.multiple_of(i * 256, 256)
        _, row = parts_of(keys_ref[pl.ds(r, 256), :][:, 0:1])
        pick = jnp.where(lane_rows == row, 1.0, 0.0).astype(BF16)
        lrow_ref[pl.ds(r, 256), :] = mm(pick, labels_ref[...]).astype(BF16)
        return 0

    lax.fori_loop(0, 4, fetch, 0)

    def flip(i, _):
        _, row = parts_of(keys_ref[pl.ds(pl.multiple_of(i * 128, 128), 128), :])
        rowt_ref[:, pl.ds(pl.multiple_of(i * 128, 128), 128)] = row.T[0:8, :]
        return 0

    lax.fori_loop(0, 8, flip, 0)

    lane_doc = lax.broadcasted_iota(jnp.int32, (64, BLK), 1).astype(F32)
    slot_l = (lax.broadcasted_iota(jnp.int32, (64, 1), 0) % 8).astype(F32)

    def doc_pick(key):
        t, _ = parts_of(key)
        d = t - 16.0 * jnp.floor(t * (1.0 / 16.0)) + 16.0 * slot_l
        d = jnp.where(key < BIG, d, -1.0)
        return jnp.where(lane_doc == d, 1.0, 0.0)

    def target(b, _):
        r = pl.multiple_of(b * 64, 64)
        key = keys_ref[pl.ds(r, 64), :][:, 0:1]
        t, _ = parts_of(key)
        found = mm(doc_pick(key).astype(BF16), dall[b])
        grow_ref[pl.ds(r, 64), :] = found.astype(BF16)
        score = C * jnp.sum(found * lrow_ref[pl.ds(r, 64), :].astype(F32), axis=1, keepdims=True)
        acc = jnp.zeros((LB, TW), F32)
        for k in range(SLOTS):
            acc = acc + jnp.where(lane_t == t[k * 8:k * 8 + 8], score[k * 8:k * 8 + 8], 0.0)
        ts_ref[b, :, 0:TW] = acc
        return 0

    lax.fori_loop(0, DP, target, 0)

    def t1_copy(i):
        q = (dp + i) % DP
        return remote(ts_ref.at[q], tr_ref.at[dp], t1_send.at[i], t1_recv.at[dp], (q, lb))

    lax.fori_loop(1, DP, lambda i, _: (t1_copy(i).start(), 0)[1], 0)

    def doc_mm(g, _):
        cols = pl.ds(pl.multiple_of(g * GRP, GRP), GRP)
        part = mm(labt[...], e_ref[:, cols].astype(BF16))
        u_ref[pl.ds(pl.multiple_of(g * GRP, GRP), GRP), :] = part.T
        return 0

    lax.fori_loop(0, 3, doc_mm, 0)

    tr_ref[dp] = ts_ref[dp]

    def t1_wait(i, top):
        q = (dp + i) % DP
        remote(ts_ref.at[q], tr_ref.at[q], t1_send.at[i], t1_recv.at[q], (q, lb)).wait_recv()
        return jnp.maximum(top, tr_ref[q, 0:1, TW:MSG])

    top = lax.fori_loop(1, DP, t1_wait, tr_ref[dp, 0:1, TW:MSG])

    def t1_sum(q, state):
        total, acc = state
        total = total + tr_ref[q, 1:2, TW:MSG] * jnp.exp(tr_ref[q, 0:1, TW:MSG] - top)
        return total, acc + tr_ref[q, :, 0:TW]

    total, acc = lax.fori_loop(0, DP, t1_sum, (jnp.zeros((1, BLK), F32), jnp.zeros((LB, TW), F32)))
    ss_ref[:, 0:TW] = acc
    ss_ref[:, TW:MSG] = jnp.zeros((LB, BLK), F32)
    ss_ref[0:1, TW:MSG] = top
    ss_ref[1:2, TW:MSG] = total

    def t2_copy(i):
        return remote(ss_ref, sr_ref.at[lb], t2_send.at[i], t2_recv.at[lb], (dp, (lb + i) % LB))

    lax.fori_loop(1, LB, lambda i, _: (t2_copy(i).start(), 0)[1], 0)
    lax.fori_loop(3, 6, doc_mm, 0)
    sr_ref[lb] = ss_ref[...]

    def t2_wait(i, top):
        q = (lb + i) % LB
        remote(ss_ref, sr_ref.at[q], t2_send.at[i], t2_recv.at[q], (dp, q)).wait_recv()
        return jnp.maximum(top, sr_ref[q, 0:1, TW:MSG])

    top = lax.fori_loop(1, LB, t2_wait, ss_ref[0:1, TW:MSG])

    def t2_sum(q, state):
        total, acc = state
        total = total + sr_ref[q, 1:2, TW:MSG] * jnp.exp(sr_ref[q, 0:1, TW:MSG] - top)
        return total, acc + sr_ref[q, :, 0:TW]

    total, acc = lax.fori_loop(0, LB, t2_sum, (jnp.zeros((1, BLK), F32), jnp.zeros((LB, TW), F32)))
    log_total = top + jnp.log(total)
    logt_ref[...] = jnp.broadcast_to(log_total, (8, 128))

    lane = lax.broadcasted_iota(jnp.int32, (LB, 128), 1)
    pos = jnp.where(lane < 16, acc[:, 0:128], 0.0)
    for s in (16, 32, 64):
        pos = pos + pltpu.roll(pos, s, 1)
    soft = jnp.zeros((LB, 128), F32)
    weight = jnp.zeros((LB, 128), F32)
    pieces = []
    for v in range(3):
        gap = acc[:, v * 128:(v + 1) * 128] - pos + 1.0
        use = (lane >= 16) if v == 0 else (lane >= 0) if v == 1 else (lane < 16)
        small = jnp.exp(-jnp.abs(gap))
        soft = soft + jnp.where(use, jnp.maximum(gap, 0.0) + jnp.log(1.0 + small), 0.0)
        sig = jnp.where(use, jnp.where(gap >= 0.0, 1.0, small) / (1.0 + small) * (1.0 / 16.0), 0.0)
        weight = weight + sig
        pieces.append(sig)
    for s in (16, 32, 64):
        soft = soft + pltpu.roll(soft, s, 1)
        weight = weight + pltpu.roll(weight, s, 1)
    loss_ref[...] = soft * (1.0 / 16.0) - pos
    pieces[0] = jnp.where(lane < 16, -1.0 - weight, pieces[0])
    for v in range(3):
        ca_ref[dp, :, v * 128:(v + 1) * 128] = pieces[v]
    ca_ref[dp, :, TW:MSG] = jnp.broadcast_to(log_total, (LB, BLK))

    def t3_copy(i):
        return remote(ca_ref.at[dp], ca_ref.at[dp], t3_send.at[i], t3_recv.at[dp], ((dp + i) % DP, lb))

    lax.fori_loop(1, DP, lambda i, _: (t3_copy(i).start(), 0)[1], 0)
    lax.fori_loop(6, 8, doc_mm, 0)

    def t3_wait(i, _):
        q = (dp + i) % DP
        remote(ca_ref.at[q], ca_ref.at[q], t3_send.at[i], t3_recv.at[q], (q, lb)).wait_recv()
        return 0

    lax.fori_loop(1, DP, t3_wait, 0)

    def slot_coef(b, t):
        dense = ca_ref[b, :, 0:TW]
        out = [jnp.sum(jnp.where(lane_t == t[k * 8:k * 8 + 8], dense, 0.0), axis=1, keepdims=True) for k in range(SLOTS)]
        return jnp.concatenate(out, axis=0)

    def core_copy(j):
        block = u_ref.at[pl.ds(pl.multiple_of((j * 2 + 1 - co) * BLK, BLK), BLK), :]
        return remote(block, rc_ref.at[j], rc_send.at[j], rc_recv.at[j], sib)

    def finish(i, _):
        j = i % 8
        b = j * 2 + jnp.where(i < 8, 1 - co, co)
        r = pl.multiple_of(b * 64, 64)
        key = keys_ref[pl.ds(r, 64), :][:, 0:1]
        t, _ = parts_of(key)
        coef = slot_coef(b, t)
        keys_ref[pl.ds(r, 64), 64:128] = jnp.broadcast_to(coef, (64, 64))
        hi, lo = split(coef * lrow_ref[pl.ds(r, 64), :].astype(F32))
        pick = doc_pick(key)
        pick = jnp.concatenate([pick, pick], axis=0).T.astype(BF16)
        hard = mm(pick, jnp.concatenate([hi, lo], axis=0))
        scale = jnp.exp(ts_ref[b, 0:1, TW:MSG] - ca_ref[b, 0:1, TW:MSG])
        scale_ref[:, pl.ds(pl.multiple_of(b * BLK, BLK), BLK)] = jnp.broadcast_to(scale, (8, BLK))
        col = jnp.broadcast_to(scale, (BLK, BLK)).T[:, 0:1]
        rows = pl.ds(pl.multiple_of(b * BLK, BLK), BLK)
        u_ref[rows, :] = C * (u_ref[rows, :] * col + hard)

        @pl.when(i < 8)
        def _():
            core_copy(j).start()

        return 0

    lax.fori_loop(0, 16, finish, 0)

    def gather_units(j, _):
        core_copy(j).wait_recv()
        xx, hh = j // 2, j % 2
        for zz in range(NZ):
            for ll in range(NYL):
                off = (zz * NYL + ll) * SUB
                rows = pl.ds(pl.multiple_of((j * 2 + co) * BLK + off, SUB), SUB)
                u = u_ref[rows, :] + rc_ref[j, off:off + SUB, :]
                yy = hh * 2 + ll
                w_ref[0, xx, yy, zz] = u[:, 0:FG]
                w_ref[1, yy, zz, xx] = u[:, FG:2 * FG]
                w_ref[2, zz, xx, yy] = u[:, 2 * FG:3 * FG]
        return 0

    lax.fori_loop(0, 8, gather_units, 0)

    spot = (x, y, z)
    bufs = ((w_ref, r1_ref), (v1_ref, r2_ref), (v2_ref, r3_ref))

    def rs_copy(step, f, i):
        axis = (f + step) % 3
        here = spot[axis]
        to = (here + i) % 4
        src, dst = bufs[step]
        n = (step * 3 + f) * 4
        return remote(src.at[f, to], dst.at[f, here], rs_send.at[n + i], rs_recv.at[n + here], on_axis(axis, to))

    def rs_wait(step, f, i):
        axis = (f + step) % 3
        frm = (spot[axis] + i) % 4
        src, dst = bufs[step]
        n = (step * 3 + f) * 4
        remote(src.at[f, frm], dst.at[f, frm], rs_send.at[n + i], rs_recv.at[n + frm], on_axis(axis, frm)).wait_recv()

    def rs_start(step):
        for f in range(3):
            for i in (2, 1, 3):
                rs_copy(step, f, i).start()

    def rs_sum(step, f):
        src, dst = bufs[step]
        here = spot[(f + step) % 3]
        for i in (1, 3, 2):
            rs_wait(step, f, i)
        value = src[f, here]
        for i in (1, 2, 3):
            value = value + dst[f, (here + i) % 4]
        return value

    rs_start(0)

    def hard_rows(i, _):
        r = pl.multiple_of(i * 64, 64)
        coef = keys_ref[pl.ds(r, 64), :][:, 64:65]
        hi, lo = split(coef * grow_ref[pl.ds(r, 64), :].astype(F32))
        ch_ref[pl.ds(r, 64), :] = hi
        cl_ref[pl.ds(r, 64), :] = lo
        return 0

    lax.fori_loop(0, 16, hard_rows, 0)

    def out_copy(i):
        return pltpu.make_async_copy(
            stage_ref.at[i % 2], lg_ref.at[pl.ds(pl.multiple_of(i * TILE, TILE), TILE), :], out_sem.at[i]
        )

    def label_mm(i, _):
        r = pl.multiple_of(i * TILE, TILE)
        probs = (e_ref[pl.ds(r, TILE), :] * scale_ref[0:1, :]).astype(BF16)
        value = mm(probs, dall[...].reshape(DOCS, D))
        sub_rows = (lax.broadcasted_iota(jnp.int32, (TILE, DEV * SLOTS), 0) + r).astype(F32)
        pick = jnp.where(sub_rows == rowt_ref[0:1, :], 1.0, 0.0).astype(BF16)
        value = value + mm(pick, ch_ref[...]) + mm(pick, cl_ref[...])

        @pl.when(i >= 2)
        def _():
            out_copy(i - 2).wait()

        stage_ref[i % 2] = C * value
        out_copy(i).start()
        return 0

    lax.fori_loop(0, 2, label_mm, 0)
    for f in range(3):
        v1_ref[f] = rs_sum(0, f)
    rs_start(1)
    lax.fori_loop(2, 3, label_mm, 0)
    for f in range(3):
        v2_ref[f] = rs_sum(1, f)
    rs_start(2)
    lax.fori_loop(3, 4, label_mm, 0)
    for f in range(3):
        dg_ref[:, f * FG:(f + 1) * FG] = rs_sum(2, f)

    out_copy(2).wait()
    out_copy(3).wait()
    for copy in first_sends:
        copy.wait_send()
    for n in range(2):
        remote(docs_ref, doc_slot(g_own, co), fwd_send.at[n], doc_recv.at[5], ypart).wait_send()
    remote(docs_ref, doc_slot(g_own, co), fwd_send.at[2], doc_recv.at[7], ypart).wait_send()

    def ends8(k, _):
        sib_copy(k, docs_ref, g_own).wait_send()
        core_copy(k).wait_send()
        return 0

    lax.fori_loop(0, 8, ends8, 0)

    def ends_lb(i, _):
        idl_copy(i).wait_send()
        t2_copy(i).wait_send()
        return 0

    lax.fori_loop(1, LB, ends_lb, 0)

    def ends_dp(i, _):
        idg_copy(i).wait_send()
        t1_copy(i).wait_send()
        t3_copy(i).wait_send()
        return 0

    lax.fori_loop(1, DP, ends_dp, 0)
    for step in range(3):
        for f in range(3):
            for i in (1, 2, 3):
                rs_copy(step, f, i).wait_send()


def shards(documents, labels, target_owner, target_row):
    lb = lax.axis_index("label")
    ids = (target_owner[:, :, 0] * ROWS + target_row).T.reshape(1, SUB * COLS).astype(F32)
    ids = jnp.pad(ids, ((0, 0), (0, TW - SUB * COLS)), constant_values=-1.0)
    ids = jnp.where(lax.broadcasted_iota(jnp.int32, (LB, TW), 0) == lb, ids, 0.0)
    vm = pl.BlockSpec(memory_space=pltpu.VMEM)
    dma = pltpu.SemaphoreType.DMA
    label_grad, doc_grad, loss, logt = pl.pallas_call(
        kernel,
        out_shape=(
            jax.ShapeDtypeStruct((ROWS, D), F32),
            jax.ShapeDtypeStruct((SUB, D), F32),
            jax.ShapeDtypeStruct((8, 128), F32),
            jax.ShapeDtypeStruct((8, 128), F32),
        ),
        in_specs=[vm, vm, vm],
        out_specs=(pl.BlockSpec(memory_space=pl.ANY), vm, vm, vm),
        scratch_shapes=[
            pltpu.VMEM((DP, BLK, D), BF16),
            pltpu.VMEM((D, ROWS), BF16),
            pltpu.VMEM((ROWS, DOCS), F32),
            pltpu.VMEM((DOCS, D), F32),
            pltpu.VMEM((8, BLK, D), F32),
            pltpu.VMEM((3, 4, 4, 4, SUB, FG), F32),
            pltpu.VMEM((3, 4, 4, 4, SUB, FG), F32),
            pltpu.VMEM((3, 4, 4, SUB, FG), F32),
            pltpu.VMEM((3, 4, 4, SUB, FG), F32),
            pltpu.VMEM((3, 4, SUB, FG), F32),
            pltpu.VMEM((3, 4, SUB, FG), F32),
            pltpu.VMEM((LB, LB, TW), F32),
            pltpu.VMEM((DP, LB, TW), F32),
            pltpu.VMEM((DEV * SLOTS, 128), F32),
            pltpu.VMEM((8, DEV * SLOTS), F32),
            pltpu.VMEM((DEV * SLOTS, D), BF16),
            pltpu.VMEM((DEV * SLOTS, D), BF16),
            pltpu.VMEM((DEV * SLOTS, D), BF16),
            pltpu.VMEM((DEV * SLOTS, D), BF16),
            pltpu.VMEM((DP, LB, MSG), F32),
            pltpu.VMEM((DP, LB, MSG), F32),
            pltpu.VMEM((LB, MSG), F32),
            pltpu.VMEM((LB, LB, MSG), F32),
            pltpu.VMEM((DP, LB, MSG), F32),
            pltpu.VMEM((8, DOCS), F32),
            pltpu.VMEM((2, TILE, D), F32),
            dma,
            dma((4,)), dma((8,)), dma((3,)), dma((8,)), dma((8,)),
            dma((LB,)), dma((LB,)), dma((DP,)), dma((DP,)),
            dma((DP,)), dma((DP,)), dma((LB,)), dma((LB,)), dma((DP,)), dma((DP,)),
            dma((8,)), dma((8,)), dma((36,)), dma((36,)), dma((4,)),
        ],
        compiler_params=pltpu.CompilerParams(
            collective_id=0, has_side_effects=True, vmem_limit_bytes=62 * 1024 * 1024
        ),
        cost_estimate=pl.CostEstimate(
            flops=8 * ROWS * DOCS * D, bytes_accessed=10 * ROWS * D, transcendentals=ROWS * DOCS
        ),
        name="head",
    )(documents, labels, ids)
    doc_loss = (
        lax.dynamic_slice(loss, (lb, 0), (1, SUB)) + lax.dynamic_slice(logt, (0, lb * SUB), (1, SUB))
    ).reshape(SUB)
    return doc_loss, doc_grad, label_grad


def solution(mesh):
    return jax.shard_map(
        shards,
        mesh=mesh,
        in_specs=(
            P("dp", None),
            P(("dp", "label"), None),
            P(("dp", "label"), None, None),
            P(("dp", "label"), None),
        ),
        out_specs=(P(("dp", "label")), P(("dp", "label"), None), P(("dp", "label"), None)),
        check_vma=False,
    )
```

```python
import functools
import math

import jax
import jax.numpy as jnp
from jax import lax
from jax.experimental import pallas as pl
from jax.experimental.pallas import tpu as pltpu
from jax.sharding import PartitionSpec as P

MESH = pl.DeviceIdType.MESH
F32 = jnp.float32
BF16 = jnp.bfloat16

NX, NYH, NC, NZ, NYL = 4, 2, 2, 4, 2
DP, LB = 16, 8
DEV = DP * LB
SUB = 16
BLK = SUB * LB
GRP = 2 * BLK
DOCS = DP * BLK
D = 768
ROWS = 2048
COLS = 17
TW = 384
SLOTS = 8
BIG = float(2 ** 23)
FG = 256
C = 4.0 / math.sqrt(D)
TILE = 256

NT = (((1,), (1,)), ((), ()))


def mm(a, b):
    return jnp.dot(a, b, preferred_element_type=F32)


def split(v):
    hi = v.astype(BF16).astype(F32)
    return hi, v - hi


def kernel(
    docs_ref, labels_hbm, owner_ref, row_ref,
    lg_ref, dg_ref, loss_ref,
    lab, dall, labt, e_ref, u_ref, rc_ref, w_ref, v1_ref, v2_ref, q0_ref, q1_ref, q2_ref,
    ids_ref, idl_ref, idg_ref, keys_ref, skeys_ref, rowt_ref, lrow_ref, slr_ref, grow_ref,
    st_ref, sr_ref, sv_ref, sst_ref, lt_ref,
    ts_ref, tr_ref, tu_ref, tv_ref, ca_ref, scale_ref, tmp_ref, coef_ref, coeft_ref,
    lab_sem, own_sem, doc_send, doc_recv, sib_send, sib_recv,
    idl_send, idl_recv, idg_send, idg_recv,
    s1_send, s1_recv, s2_send, s2_recv, sst_sem, lr_sem,
    t1_send, t1_recv, t2_send, t2_recv, t3_send, t3_recv,
    rc_send, rc_recv, rs_send, rs_recv,
):
    dp = lax.axis_index("dp")
    lb = lax.axis_index("label")
    x, yh, co = dp // 4, (dp // 2) % 2, dp % 2
    z, yl = lb // 2, lb % 2
    y = yh * 2 + yl
    me = dp * LB + lb

    def dev(x_, yh_, co_, z_, yl_):
        return ((x_ * 2 + yh_) * 2 + co_, z_ * 2 + yl_)

    sib = dev(x, yh, 1 - co, z, yl)
    ypart = dev(x, 1 - yh, co, z, 1 - yl)

    def on_axis(axis, pos):
        if axis == 0:
            return dev(pos, yh, co, z, yl)
        if axis == 1:
            return dev(x, pos // 2, co, z, pos % 2)
        return dev(x, yh, co, pos, yl)

    xup, xdown = on_axis(0, (x + 1) % NX), on_axis(0, (x + 3) % NX)

    def mate(i):
        q = (dp + i) % DP
        return q, (q, z * 2 + jnp.where((q // 2) % 2 == yh, yl, 1 - yl))

    def all_in(ref, sem):
        pltpu.make_async_remote_copy(
            src_ref=ref, dst_ref=ref, send_sem=sem, recv_sem=sem, device_id=sib, device_id_type=MESH
        ).wait_recv()

    def all_out(ref, sem):
        pltpu.make_async_remote_copy(
            src_ref=ref, dst_ref=ref, send_sem=sem, recv_sem=sem, device_id=sib, device_id_type=MESH
        ).wait_send()

    def remote(src, dst, ssem, rsem, to):
        return pltpu.make_async_remote_copy(
            src_ref=src, dst_ref=dst, send_sem=ssem, recv_sem=rsem, device_id=to, device_id_type=MESH
        )

    def each(lo, hi, fn):
        def body(i, carry):
            fn(i)
            return carry

        lax.fori_loop(lo, hi, body, 0)

    def at(start, size):
        return pl.ds(pl.multiple_of(start, size), size)

    barrier = pltpu.get_barrier_semaphore()
    each(1, DP, lambda i: pl.semaphore_signal(barrier, inc=1, device_id=mate(i)[1], device_id_type=MESH))
    each(1, LB, lambda i: pl.semaphore_signal(barrier, inc=1, device_id=(dp, (lb + i) % LB), device_id_type=MESH))
    pl.semaphore_signal(barrier, inc=1, device_id=dev(x, 1 - yh, co, z, yl), device_id_type=MESH)
    lab_copy = pltpu.make_async_copy(labels_hbm, lab, lab_sem)
    lab_copy.start()
    g_own = x * 2 + yh

    def doc_slot(group, core):
        return dall.at[group * 2 + core]

    own_copy = pltpu.make_async_copy(docs_ref, doc_slot(g_own, co), own_sem)
    own_copy.start()
    named = (owner_ref[:, 0, :] * ROWS + row_ref[...]).astype(F32)
    high = jnp.floor(named * (1.0 / 4096.0))
    rest = named - 4096.0 * high
    mid = jnp.floor(rest * (1.0 / 64.0))
    digits = jnp.concatenate([high, mid, rest - 64.0 * mid], axis=0).astype(BF16)
    lane = lax.broadcasted_iota(jnp.int32, (COLS, TW), 1)
    spread = mm(digits, jnp.where(lane // SUB == lax.broadcasted_iota(jnp.int32, (COLS, TW), 0), 1.0, 0.0).astype(BF16))
    spread = 4096.0 * spread[0:SUB] + 64.0 * spread[SUB:2 * SUB] + spread[2 * SUB:3 * SUB]
    lane = lax.broadcasted_iota(jnp.int32, (SUB, TW), 1)
    own = jnp.sum(jnp.where(lane % SUB == lax.broadcasted_iota(jnp.int32, (SUB, TW), 0), spread, 0.0), axis=0, keepdims=True)
    own = jnp.where(lane[0:1] < SUB * COLS, own, -1.0)
    ids_ref[...] = jnp.where(lax.broadcasted_iota(jnp.int32, (LB, TW), 0) == lb, own, 0.0)
    pl.semaphore_wait(barrier, DP - 1 + LB - 1 + 1)

    def idl_copy(i):
        return remote(ids_ref, idl_ref.at[lb], idl_send, idl_recv, (dp, (lb + i) % LB))

    each(1, LB, lambda i: idl_copy(i).start())

    def sib_copy(k, src, group):
        return remote(src, doc_slot(group, co), sib_send, sib_recv.at[k], sib)

    sib_copy(0, docs_ref, g_own).start()
    first_sends = [
        remote(docs_ref, doc_slot(g_own, co), doc_send, doc_recv.at[1], ypart),
        remote(docs_ref, doc_slot(g_own, co), doc_send, doc_recv.at[3], xup),
        remote(docs_ref, doc_slot(g_own, co), doc_send, doc_recv.at[2], xdown),
    ]
    for copy in first_sends:
        copy.start()

    def place(k):
        dx = jnp.where((k == 2) | (k == 5), 1, jnp.where((k == 3) | (k == 6), 3, jnp.where((k == 4) | (k == 7), 2, 0)))
        dy = jnp.where((k == 1) | (k >= 5), 1, 0)
        return ((x + dx) % NX) * 2 + (yh + dy) % 2

    def half(ref, h):
        return ref.at[h * (BLK // 2):(h + 1) * (BLK // 2), :]

    def relay_up(slot):
        return remote(slot, slot, doc_send, doc_recv.at[6], xup)

    def relay_down(slot):
        return remote(slot, slot, doc_send, doc_recv.at[5], xdown)

    def relay_far_a(slot):
        return remote(half(slot, 0), half(slot, 0), doc_send, doc_recv.at[4], xdown)

    def relay_far_b(slot):
        return remote(half(slot, 1), half(slot, 1), doc_send, doc_recv.at[8], xup)

    def relay_y(slot):
        return remote(slot, slot, doc_send, doc_recv.at[7], ypart)

    def take(k):
        slot = doc_slot(place(k), co)

        if k != 4:
            remote(slot, slot, doc_send, doc_recv.at[k], ypart).wait_recv()
        else:
            for h in range(2):
                remote(half(slot, h), half(slot, h), doc_send, doc_recv.at[4 + 4 * h], ypart).wait_recv()

        if k == 2:
            relay_far_a(slot).start()
        if k == 3:
            relay_far_b(slot).start()
        if k == 4:
            relay_y(slot).start()
        sib_copy(k, slot, place(k)).start()

    ts_ref[...] = jnp.zeros_like(ts_ref)
    st_ref[...] = jnp.zeros_like(st_ref)
    lab_copy.wait()

    def turn(i):
        labt[:, at(i * 256, 256)] = lab[at(i * 256, 256), :].T

    each(0, ROWS // 256, turn)

    own_copy.wait()

    def raw_cols(p):
        return slice(p * GRP, (p + 1) * GRP)

    CH = 512

    def exp_rows(p, c, top, cols):
        s = lg_ref[c * CH:(c + 1) * CH, raw_cols(p)]
        e = jnp.exp((s - top) * C)
        e_ref[c * CH:(c + 1) * CH, cols] = e
        return jnp.sum(e, axis=0, keepdims=True)

    def keep(g, top, total):
        for h in range(2):
            st_ref[0, pl.ds(g * 2 + h, 1), :] = (top * C)[:, h * BLK:(h + 1) * BLK]
            st_ref[1, pl.ds(g * 2 + h, 1), :] = total[:, h * BLK:(h + 1) * BLK]

    def wait_sib(k):
        other = doc_slot(place(k), 1 - co)
        remote(other, other, sib_send, sib_recv.at[k], sib).wait_recv()

    def score_step(k, p, old_top):
        g = place(k)

        @pl.when(k < 7)
        def _():
            wait_sib(k)

        block = dall[pl.ds(g * 2, 2)].reshape(GRP, D)
        old = place((k + 7) % 8)
        cols = at(old * GRP, GRP)
        top, total = None, 0.0
        for c in range(ROWS // CH):
            s = lax.dot_general(lab[c * CH:(c + 1) * CH, :], block, NT, preferred_element_type=F32)
            lg_ref[c * CH:(c + 1) * CH, raw_cols(p)] = s
            high = jnp.max(s, axis=0, keepdims=True)
            top = high if top is None else jnp.maximum(top, high)
            total = total + exp_rows(1 - p, c, old_top, cols)
        keep(old, old_top, total)
        return top

    def ids_out():
        all_in(idl_ref.at[1:LB], idl_recv)
        idl_ref[lb] = ids_ref[...]
        acc = idl_ref[0]
        for q in range(1, LB):
            acc = acc + idl_ref[q]
        idg_ref[dp] = acc
        each(1, DP, lambda i: idg_copy(i).start())

    def idg_copy(i):
        return remote(idg_ref.at[dp], idg_ref.at[dp], idg_send, idg_recv, mate(i)[1])

    lane_8 = lax.broadcasted_iota(jnp.int32, (LB, 128), 1).astype(F32)
    lane_t = [lane_8 + 128.0 * v for v in range(3)]
    base = (me * ROWS).astype(F32)

    def find():
        all_in(idg_ref.at[1:DP], idg_recv)
        rel = idg_ref[...].reshape(DEV, TW) - base
        lanes = lax.broadcasted_iota(jnp.int32, (DEV, TW), 1).astype(F32)
        key = jnp.where((rel >= 0.0) & (rel < float(ROWS)), lanes * float(ROWS) + rel, BIG)
        for k in range(SLOTS):
            low = jnp.min(key, axis=1, keepdims=True)
            for b in range(DP):
                keys_ref[b % 2, b // 2, k * 8:k * 8 + 8, :] = jnp.broadcast_to(low[b * 8:b * 8 + 8], (8, 128))
            key = jnp.where(key == low, BIG, key)

    def parts_of(key):
        t = jnp.floor(key * (1.0 / ROWS))
        row = jnp.where(key < BIG, key - t * float(ROWS), -1.0)
        return t, row

    def fetch(i):
        lane_rows = lax.broadcasted_iota(jnp.int32, (256, ROWS), 1).astype(F32)
        c, j = i // 2, pl.ds((i % 2) * 4, 4)
        _, row = parts_of(keys_ref[c, j].reshape(256, 128)[:, 0:1])
        pick = jnp.where(lane_rows == row, 1.0, 0.0).astype(BF16)
        lrow_ref[c, j] = mm(pick, lab[...]).astype(BF16).reshape(4, 64, D)

    def named_copy():
        return remote(lrow_ref.at[1 - co], slr_ref, lr_sem.at[0], lr_sem.at[1], sib)

    def keys_copy():
        return remote(keys_ref.at[1 - co], skeys_ref, lr_sem.at[2], lr_sem.at[3], sib)

    def flip(i):
        _, row = parts_of(keys_ref[i // 4, pl.ds((i % 4) * 2, 2)].reshape(128, 128))
        rowt_ref[:, at(i * 128, 128)] = row.T[0:8, :]

    lane_doc = lax.broadcasted_iota(jnp.int32, (64, BLK), 1).astype(F32)
    slot_l = (lax.broadcasted_iota(jnp.int32, (64, BLK), 0) % 8).astype(F32)

    def doc_pick(key):
        t, _ = parts_of(key)
        d = t - 16.0 * jnp.floor(t * (1.0 / 16.0)) + 16.0 * slot_l
        return lane_doc == jnp.where(key < BIG, d, -1.0)

    def target(i):
        out = []
        for q in range(4):
            b = i * 4 + q
            c, j = q % 2, i * 2 + q // 2
            key = keys_ref[c, j]
            t, _ = parts_of(key)
            found = mm(jnp.where(doc_pick(key), 1.0, 0.0).astype(BF16), dall[b])
            score = C * jnp.sum(found * lrow_ref[c, j].astype(F32), axis=1, keepdims=True)
            acc = [jnp.zeros((LB, 128), F32)] * 3
            for k in range(SLOTS):
                for v in range(3):
                    acc[v] = acc[v] + jnp.where(lane_t[v] == t[k * 8:k * 8 + 8], score[k * 8:k * 8 + 8], 0.0)
            out.append((b, c, j, found.astype(BF16), acc))
        for b, c, j, found, acc in out:
            grow_ref[c, j] = found
            for v in range(3):
                ts_ref[b, :, v * 128:(v + 1) * 128] = acc[v]

    def t1_copy(i):
        q, to = mate(i)
        return remote(ts_ref.at[q], tr_ref.at[dp], t1_send, t1_recv, to)


    def s1_copy(i):
        return remote(st_ref, sr_ref.at[lb], s1_send, s1_recv, (dp, (lb + i) % LB))

    def s2_copy(i):
        return remote(sv_ref.at[dp], sv_ref.at[dp], s2_send, s2_recv, mate(i)[1])

    def sst_copy():
        return remote(st_ref.at[0], sst_ref, sst_sem.at[0], sst_sem.at[1], sib)

    def merge(count, ref):
        tops = [ref[q, 0] for q in range(count)]
        top = functools.reduce(jnp.maximum, tops)
        total = 0.0
        for q in range(count):
            total = total + ref[q, 1] * jnp.exp(tops[q] - top)
        return top, total

    def stats_on():
        all_in(sr_ref.at[1:LB], s1_recv)
        sr_ref[lb] = st_ref[...]
        sv_ref[dp, 0], sv_ref[dp, 1] = merge(LB, sr_ref)
        each(1, DP, lambda i: s2_copy(i).start())

    def totals():
        all_in(sv_ref.at[1:DP], s2_recv)
        top, total = merge(DP, sv_ref)
        lt_ref[...] = top + jnp.log(total)

    def doc_part(g):
        part = mm(labt[...], e_ref[:, at(g * GRP, GRP)].astype(BF16))
        u_ref[at(g * GRP, GRP), :] = part.T

    def exp_group(p, g, top):
        total = 0.0
        for c in range(ROWS // CH):
            total = total + exp_rows(p, c, top, at(g * GRP, GRP))
        keep(g, top, total)

    def score_pair(i, top):
        top = score_step(i * 2, 0, top)

        @pl.when(i == 0)
        def _():
            exp_group(0, g_own, top)
            doc_part(g_own)
            ids_out()
            for k in (2, 3, 1):
                take(k)

        @pl.when(i == 1)
        def _():
            slot = doc_slot(place(1), co)
            relay_up(slot).start()
            relay_down(slot).start()

        @pl.when(i == 2)
        def _():
            take(5)
            take(6)
            each(2, 4, fetch)
            named_copy().start()
            keys_copy().start()
            each(0, 8, flip)

        @pl.when(i == 3)
        def _():
            wait_sib(7)
            each(0, 4, target)
            each(1, DP, lambda i: t1_copy(i).start())

        top = score_step(i * 2 + 1, 1, top)

        @pl.when(i == 1)
        def _():
            find()
            each(0, 1, fetch)
            take(4)
            each(1, 2, fetch)

        @pl.when(i == 2)
        def _():
            take(7)

        return top

    lg_ref[:, raw_cols(1)] = jnp.zeros((ROWS, GRP), F32)
    top = lax.fori_loop(0, 4, score_pair, jnp.zeros((1, GRP), F32))
    exp_group(1, place(7), top)

    each(1, LB, lambda i: s1_copy(i).start())
    sst_copy().start()

    def t2_copy(i):
        return remote(tu_ref, tv_ref.at[lb], t2_send, t2_recv, (dp, (lb + i) % LB))

    def t3_copy(i):
        return remote(ca_ref.at[dp], ca_ref.at[dp], t3_send, t3_recv, mate(i)[1])

    def targets_on():
        all_in(tr_ref.at[1:DP], t1_recv)
        tr_ref[dp] = ts_ref[dp]
        acc = tr_ref[0]
        for q in range(1, DP):
            acc = acc + tr_ref[q]
        tu_ref[...] = acc
        each(1, LB, lambda i: t2_copy(i).start())

    def coefficients_on():
        all_in(tv_ref.at[1:LB], t2_recv)
        tv_ref[lb] = tu_ref[...]
        acc = tv_ref[0]
        for q in range(1, LB):
            acc = acc + tv_ref[q]
        lane = lax.broadcasted_iota(jnp.int32, (LB, 128), 1)
        pos = jnp.where(lane < 16, acc[:, 0:128], 0.0)
        for s in (16, 32, 64):
            pos = pos + pltpu.roll(pos, s, 1)
        soft = jnp.zeros((LB, 128), F32)
        weight = jnp.zeros((LB, 128), F32)
        pieces = []
        for v in range(3):
            gap = acc[:, v * 128:(v + 1) * 128] - pos + 1.0
            use = (lane >= 16) if v == 0 else (lane >= 0) if v == 1 else (lane < 16)
            small = jnp.exp(-jnp.abs(gap))
            soft = soft + jnp.where(use, jnp.maximum(gap, 0.0) + jnp.log(1.0 + small), 0.0)
            sig = jnp.where(use, jnp.where(gap >= 0.0, 1.0, small) / (1.0 + small) * (1.0 / 16.0), 0.0)
            weight = weight + sig
            pieces.append(sig)
        for s in (16, 32, 64):
            soft = soft + pltpu.roll(soft, s, 1)
            weight = weight + pltpu.roll(weight, s, 1)
        tmp_ref[...] = soft * (1.0 / 16.0) - pos
        pieces[0] = jnp.where(lane < 16, -1.0 - weight, pieces[0])
        for v in range(3):
            ca_ref[dp, :, v * 128:(v + 1) * 128] = pieces[v]
        each(1, DP, lambda i: t3_copy(i).start())

    def core_copy(j):
        return remote(u_ref.at[at((j * 2 + 1 - co) * BLK, BLK), :], rc_ref.at[j], rc_send, rc_recv, sib)

    def doc_mm(k):
        doc_part(place(k))

        @pl.when(k == 3)
        def _():
            targets_on()
            stats_on()
            for j in range(4):
                core_copy(place(j)).start()

        @pl.when(k == 6)
        def _():
            coefficients_on()

        @pl.when(k > 3)
        def _():
            core_copy(place(k)).start()

    each(1, 8, doc_mm)
    totals()
    all_in(rc_ref, rc_recv)
    sst_copy().wait_recv()

    def column(row):
        return jnp.concatenate([jnp.broadcast_to(row, (BLK, BLK)).T] * (D // BLK), axis=1)

    def merge_cores(i):
        out = []
        for q in range(4):
            j = i * 4 + q
            b = j * 2 + co
            log_total = lt_ref[pl.ds(b, 1), :]
            col = column(jnp.exp(st_ref[0, pl.ds(b, 1), :] - log_total))
            scol = column(jnp.exp(sst_ref[pl.ds(b, 1), :] - log_total))
            out.append((b, u_ref[at(b * BLK, BLK), :] * col + rc_ref[j] * scol))
        for b, value in out:
            u_ref[at(b * BLK, BLK), :] = value

    each(0, 2, merge_cores)
    shifted = pltpu.roll(jnp.broadcast_to(lt_ref[pl.ds(dp, 1), :], (8, BLK)), (BLK - lb * SUB) % BLK, 1)
    loss_ref[...] = tmp_ref[pl.ds(lb, 1), :] + shifted[0:1, :]

    all_in(ca_ref.at[1:DP], t3_recv)

    def slot_coef(b, t):
        out = []
        for k in range(SLOTS):
            hit = [jnp.where(lane_t[v] == t[k * 8:k * 8 + 8], ca_ref[b, :, v * 128:(v + 1) * 128], 0.0) for v in range(3)]
            out.append(jnp.sum(hit[0] + hit[1] + hit[2], axis=1, keepdims=True))
        return jnp.concatenate(out, axis=0)

    def scaled_pick(key, coef):
        hi, lo = split(coef)
        pick = doc_pick(key)
        return [jnp.where(pick, hi, 0.0), jnp.where(pick, lo, 0.0)]

    def finish(i):
        out = []
        for q in range(4):
            j = i * 4 + q
            b = j * 2 + co
            key, skey = keys_ref[co, j], skeys_ref[j]
            coef, scoef = slot_coef(b, parts_of(key)[0]), slot_coef(b, parts_of(skey)[0])
            pick = jnp.concatenate(scaled_pick(key, coef) + scaled_pick(skey, scoef), axis=0).T.astype(BF16)
            named, snamed = lrow_ref[co, j], slr_ref[j]
            hard = mm(pick, jnp.concatenate([named, named, snamed, snamed], axis=0))
            out.append((j, coef, C * (u_ref[at(b * BLK, BLK), :] + hard)))
        for j, coef, value in out:
            coef_ref[co, j] = jnp.broadcast_to(coef, (64, 128))
            xx, hh = j // 2, j % 2
            for zz in range(NZ):
                for ll in range(NYL):
                    off = (zz * NYL + ll) * SUB
                    u = value[off:off + SUB]
                    yy = hh * 2 + ll
                    w_ref[0, xx, yy, zz] = u[:, 0:FG]
                    w_ref[1, yy, zz, xx] = u[:, FG:2 * FG]
                    w_ref[2, zz, xx, yy] = u[:, 2 * FG:3 * FG]

    named_copy().wait_recv()
    keys_copy().wait_recv()
    each(0, 2, finish)

    spot = (x, y, z)
    def ring_msg(f, m):
        h = spot[f]
        up, down = on_axis(f, (h + 1) % 4), on_axis(f, (h + 3) % 4)

        def part(block, which):
            return w_ref.at[f, block % 4, which * 2:which * 2 + 2]

        source = (part(h + 2, 0), part(h + 2, 1), part(h + 3, 1), part(h + 1, 0), q0_ref.at[f, 0], q0_ref.at[f, 1])[m]
        to = (down, up, down, up, down, up)[m]
        return remote(source, q0_ref.at[f, m], rs_send.at[0], rs_recv.at[0 if m < 2 else 1], to)

    def ring_start(msgs):
        for m in msgs:
            for f in range(3):
                ring_msg(f, m).start()

    def ring_relay():
        all_in(q0_ref.at[:, 0:2], rs_recv.at[0])
        for f in range(3):
            h = spot[f]
            for m in range(2):
                block = (h + 3) % 4 if m == 0 else (h + 1) % 4
                q0_ref[f, m] = q0_ref[f, m] + w_ref[f, block, m * 2:m * 2 + 2]
                ring_msg(f, 4 + m).start()

    def ring_done():
        all_in(q0_ref.at[:, 2:6], rs_recv.at[1])
        for f in range(3):
            h = spot[f]
            v1_ref[f, 0:2] = w_ref[f, h, 0:2] + q0_ref[f, 4] + q0_ref[f, 3]
            v1_ref[f, 2:4] = w_ref[f, h, 2:4] + q0_ref[f, 2] + q0_ref[f, 5]

    bufs = {1: (v1_ref, q1_ref), 2: (v2_ref, q2_ref)}

    def straight(step, f, i):
        axis = (f + step) % 3
        to = (spot[axis] + i) % 4
        src, box = bufs[step]
        return remote(src.at[f, to], box.at[f, i - 1], rs_send.at[step], rs_recv.at[step + 1], on_axis(axis, to))

    def straight_start(step):
        for i in (2, 1, 3):
            for f in range(3):
                straight(step, f, i).start()

    def straight_done(step):
        src, box = bufs[step]
        all_in(box, rs_recv.at[step + 1])
        return [src[f, spot[(f + step) % 3]] + box[f, 0] + box[f, 1] + box[f, 2] for f in range(3)]

    ring_start((0, 1))

    def coef_rows(i):
        hi, lo = split(coef_ref[i // 4, pl.ds((i % 4) * 2, 2)].reshape(128, 128).T[0:8, :])
        coeft_ref[0, :, at(i * 128, 128)] = hi
        coeft_ref[1, :, at(i * 128, 128)] = lo

    def other_coef(i):
        out = []
        for q in range(4):
            j = i * 4 + q
            out.append((j, slot_coef(j * 2 + 1 - co, parts_of(keys_ref[1 - co, j])[0])))
        for j, coef in out:
            coef_ref[1 - co, j] = jnp.broadcast_to(coef, (64, 128))

    each(0, 2, other_coef)
    each(0, 8, coef_rows)
    for b in range(DP):
        scale = jnp.exp(st_ref[0, b:b + 1, :] - lt_ref[b:b + 1, :])
        scale_ref[:, b * BLK:(b + 1) * BLK] = jnp.broadcast_to(scale, (8, BLK))

    def label_mm(r):
        probs = (e_ref[at(r * TILE, TILE), :] * scale_ref[0:1, :]).astype(BF16)
        sub_rows = (lax.broadcasted_iota(jnp.int32, (TILE, DEV * SLOTS), 0) + r * TILE).astype(F32)
        pick = sub_rows == rowt_ref[0:1, :]
        named = grow_ref[...].reshape(DEV * SLOTS, D)
        value = mm(probs, dall[...].reshape(DOCS, D))
        for p in range(2):
            value = value + mm(jnp.where(pick, coeft_ref[p, 0:1, :], 0.0).astype(BF16), named)
        lg_ref[at(r * TILE, TILE), :] = C * value

        @pl.when(r == 0)
        def _():
            ring_start((2, 3))

        @pl.when(r == 2)
        def _():
            ring_relay()

        @pl.when(r == 4)
        def _():
            ring_done()
            straight_start(1)

        @pl.when(r == 6)
        def _():
            for f, value in enumerate(straight_done(1)):
                v2_ref[f] = value
            straight_start(2)

    each(0, ROWS // TILE, label_mm)

    for f, value in enumerate(straight_done(2)):
        dg_ref[:, f * FG:(f + 1) * FG] = value

    all_out(dall.at[0:7], doc_send)
    all_out(dall.at[0:8], sib_send)
    all_out(rc_ref, rc_send)
    for copy in (sst_copy(), named_copy(), keys_copy()):
        copy.wait_send()
    all_out(idl_ref.at[1:LB], idl_send)
    all_out(idg_ref.at[1:DP], idg_send)
    all_out(sr_ref.at[1:LB], s1_send)
    all_out(sv_ref.at[1:DP], s2_send)
    all_out(tr_ref.at[1:DP], t1_send)
    all_out(tv_ref.at[1:LB], t2_send)
    all_out(ca_ref.at[1:DP], t3_send)
    all_out(q0_ref, rs_send.at[0])
    all_out(q1_ref, rs_send.at[1])
    all_out(q2_ref, rs_send.at[2])


def ship(lg_in, dg_in, loss_in, lg_out, dg_out, loss_out, sems):
    copies = [pltpu.make_async_copy(lg_in, lg_out, sems.at[0]), pltpu.make_async_copy(dg_in, dg_out, sems.at[1])]
    for copy in copies:
        copy.start()
    loss_out[...] = loss_in[0, 0:SUB]
    for copy in copies:
        copy.wait()


def shards(documents, labels, target_owner, target_row):
    vm = pl.BlockSpec(memory_space=pltpu.VMEM)
    hbm = pl.BlockSpec(memory_space=pl.ANY)
    dma = pltpu.SemaphoreType.DMA
    slots = DEV * SLOTS
    label_grad, doc_grad, loss = pl.pallas_call(
        kernel,
        out_shape=(
            pltpu.VMEM((ROWS, D), F32),
            pltpu.VMEM((SUB, D), F32),
            pltpu.VMEM((1, 128), F32),
        ),
        in_specs=[vm, hbm, vm, vm],
        out_specs=(vm, vm, vm),
        scratch_shapes=[
            pltpu.VMEM((ROWS, D), BF16),
            pltpu.VMEM((DP, BLK, D), BF16),
            pltpu.VMEM((D, ROWS), BF16),
            pltpu.VMEM((ROWS, DOCS), F32),
            pltpu.VMEM((DOCS, D), F32),
            pltpu.VMEM((8, BLK, D), F32),
            pltpu.VMEM((3, 4, 4, 4, SUB, FG), F32),
            pltpu.VMEM((3, 4, 4, SUB, FG), F32),
            pltpu.VMEM((3, 4, SUB, FG), F32),
            pltpu.VMEM((3, 6, 2, 4, SUB, FG), F32),
            pltpu.VMEM((3, 3, 4, SUB, FG), F32),
            pltpu.VMEM((3, 3, SUB, FG), F32),
            pltpu.VMEM((LB, TW), F32),
            pltpu.VMEM((LB, LB, TW), F32),
            pltpu.VMEM((DP, LB, TW), F32),
            pltpu.VMEM((2, 8, 64, 128), F32),
            pltpu.VMEM((8, 64, 128), F32),
            pltpu.VMEM((8, slots), F32),
            pltpu.VMEM((2, 8, 64, D), BF16),
            pltpu.VMEM((8, 64, D), BF16),
            pltpu.VMEM((2, 8, 64, D), BF16),
            pltpu.VMEM((2, DP, BLK), F32),
            pltpu.VMEM((LB, 2, DP, BLK), F32),
            pltpu.VMEM((DP, 2, DP, BLK), F32),
            pltpu.VMEM((DP, BLK), F32),
            pltpu.VMEM((DP, BLK), F32),
            pltpu.VMEM((DP, LB, TW), F32),
            pltpu.VMEM((DP, LB, TW), F32),
            pltpu.VMEM((LB, TW), F32),
            pltpu.VMEM((LB, LB, TW), F32),
            pltpu.VMEM((DP, LB, TW), F32),
            pltpu.VMEM((8, DOCS), F32),
            pltpu.VMEM((LB, 128), F32),
            pltpu.VMEM((2, 8, 64, 128), F32),
            pltpu.VMEM((2, 8, slots), F32),
            dma, dma, dma, dma((9,)), dma, dma((8,)),
            dma, dma, dma, dma,
            dma, dma, dma, dma, dma((2,)), dma((4,)),
            dma, dma, dma, dma, dma, dma,
            dma, dma, dma((3,)), dma((4,)),
        ],
        compiler_params=pltpu.CompilerParams(
            collective_id=0, has_side_effects=True, vmem_limit_bytes=56 * 1024 * 1024
        ),
        cost_estimate=pl.CostEstimate(
            flops=8 * ROWS * DOCS * D, bytes_accessed=10 * ROWS * D, transcendentals=ROWS * DOCS
        ),
        name="head",
    )(documents, labels, target_owner.transpose(0, 2, 1), target_row)
    label_grad, doc_grad, loss = pl.pallas_call(
        ship,
        out_shape=(
            jax.ShapeDtypeStruct((ROWS, D), F32),
            jax.ShapeDtypeStruct((SUB, D), F32),
            jax.ShapeDtypeStruct((SUB,), F32),
        ),
        in_specs=[vm, vm, vm],
        out_specs=(hbm, hbm, vm),
        scratch_shapes=[dma((2,))],
        compiler_params=pltpu.CompilerParams(vmem_limit_bytes=32 * 1024 * 1024),
        name="ship",
    )(label_grad, doc_grad, loss)
    return loss, doc_grad, label_grad


def solution(mesh):
    return jax.shard_map(
        shards,
        mesh=mesh,
        in_specs=(
            P("dp", None),
            P(("dp", "label"), None),
            P(("dp", "label"), None, None),
            P(("dp", "label"), None),
        ),
        out_specs=(P(("dp", "label")), P(("dp", "label"), None), P(("dp", "label"), None)),
        check_vma=False,
    )
```

```python
import functools
import math

import jax
import jax.numpy as jnp
from jax import lax
from jax.experimental import pallas as pl
from jax.experimental.pallas import tpu as pltpu
from jax.sharding import PartitionSpec as P

MESH = pl.DeviceIdType.MESH
F32 = jnp.float32
BF16 = jnp.bfloat16

NX, NYH, NC, NZ, NYL = 4, 2, 2, 4, 2
DP, LB = 16, 8
DEV = DP * LB
SUB = 16
BLK = SUB * LB
GRP = 2 * BLK
DOCS = DP * BLK
D = 768
ROWS = 2048
COLS = 17
TW = 384
SLOTS = 8
BIG = float(2 ** 23)
FG = 256
C = 4.0 / math.sqrt(D)
TILE = 256

NT = (((1,), (1,)), ((), ()))


def mm(a, b):
    return jnp.dot(a, b, preferred_element_type=F32)


def split(v):
    hi = v.astype(BF16).astype(F32)
    return hi, v - hi


def kernel(
    docs_hbm, labels_hbm, owner_hbm, row_hbm,
    lg_ref, dg_ref, loss_ref,
    lab, dall, labt, e_ref, u_ref, rc_ref, w_ref, v1_ref, v2_ref, q0_ref, q1_ref, q2_ref,
    owner_ref, row_ref, ids_ref, idl_ref, idg_ref, keys_ref, skeys_ref, rowt_ref, lrow_ref, slr_ref, grow_ref,
    st_ref, sr_ref, sv_ref, sst_ref, lt_ref,
    ts_ref, tr_ref, tu_ref, tv_ref, ca_ref, scale_ref, tmp_ref, coef_ref, coeft_ref,
    lab_sem, own_sem, in_sem, doc_send, doc_recv, sib_send, sib_recv,
    idl_send, idl_recv, idg_send, idg_recv,
    s1_send, s1_recv, s2_send, s2_recv, sst_sem, lr_sem,
    t1_send, t1_recv, t2_send, t2_recv, t3_send, t3_recv,
    rc_send, rc_recv, rs_send, rs_recv,
):
    dp = lax.axis_index("dp")
    lb = lax.axis_index("label")
    x, yh, co = dp // 4, (dp // 2) % 2, dp % 2
    z, yl = lb // 2, lb % 2
    y = yh * 2 + yl
    me = dp * LB + lb

    def dev(x_, yh_, co_, z_, yl_):
        return ((x_ * 2 + yh_) * 2 + co_, z_ * 2 + yl_)

    sib = dev(x, yh, 1 - co, z, yl)
    ypart = dev(x, 1 - yh, co, z, 1 - yl)

    def on_axis(axis, pos):
        if axis == 0:
            return dev(pos, yh, co, z, yl)
        if axis == 1:
            return dev(x, pos // 2, co, z, pos % 2)
        return dev(x, yh, co, pos, yl)

    xup, xdown = on_axis(0, (x + 1) % NX), on_axis(0, (x + 3) % NX)

    def mate(i):
        q = (dp + i) % DP
        return q, (q, z * 2 + jnp.where((q // 2) % 2 == yh, yl, 1 - yl))

    def all_in(ref, sem):
        pltpu.make_async_remote_copy(
            src_ref=ref, dst_ref=ref, send_sem=sem, recv_sem=sem, device_id=sib, device_id_type=MESH
        ).wait_recv()

    def all_out(ref, sem):
        pltpu.make_async_remote_copy(
            src_ref=ref, dst_ref=ref, send_sem=sem, recv_sem=sem, device_id=sib, device_id_type=MESH
        ).wait_send()

    def remote(src, dst, ssem, rsem, to):
        return pltpu.make_async_remote_copy(
            src_ref=src, dst_ref=dst, send_sem=ssem, recv_sem=rsem, device_id=to, device_id_type=MESH
        )

    def each(lo, hi, fn):
        def body(i, carry):
            fn(i)
            return carry

        lax.fori_loop(lo, hi, body, 0)

    def at(start, size):
        return pl.ds(pl.multiple_of(start, size), size)

    barrier = pltpu.get_barrier_semaphore()
    each(1, DP, lambda i: pl.semaphore_signal(barrier, inc=1, device_id=mate(i)[1], device_id_type=MESH))
    each(1, LB, lambda i: pl.semaphore_signal(barrier, inc=1, device_id=(dp, (lb + i) % LB), device_id_type=MESH))
    pl.semaphore_signal(barrier, inc=1, device_id=dev(x, 1 - yh, co, z, yl), device_id_type=MESH)
    lab_copy = pltpu.make_async_copy(labels_hbm, lab, lab_sem)
    lab_copy.start()
    g_own = x * 2 + yh

    def doc_slot(group, core):
        return dall.at[group * 2 + core]

    own_copy = pltpu.make_async_copy(docs_hbm, doc_slot(g_own, co), own_sem)
    own_copy.start()
    id_copies = [
        pltpu.make_async_copy(owner_hbm, owner_ref, in_sem.at[0]),
        pltpu.make_async_copy(row_hbm, row_ref, in_sem.at[1]),
    ]
    for copy in id_copies:
        copy.start()
    pl.semaphore_wait(barrier, DP - 1 + LB - 1 + 1)

    def sib_copy(k, src, group):
        return remote(src, doc_slot(group, co), sib_send, sib_recv.at[k], sib)

    own_copy.wait()
    sib_copy(0, doc_slot(g_own, co), g_own).start()
    def some(ref, start, size):
        return ref.at[start:start + size, :]

    def half_copy(h, rsem, to):
        block = some(doc_slot(g_own, co), h * 64, 64)
        return remote(block, block, doc_send, doc_recv.at[rsem], to)

    remote(doc_slot(g_own, co), doc_slot(g_own, co), doc_send, doc_recv.at[3], ypart).start()
    half_copy(0, 1, xdown).start()
    half_copy(1, 2, xup).start()

    def place(k):
        dx = jnp.where((k == 1) | (k == 5), 1, jnp.where((k == 2) | (k == 6), 3, jnp.where((k == 4) | (k == 7), 2, 0)))
        dy = jnp.where((k == 3) | (k >= 5), 1, 0)
        return ((x + dx) % NX) * 2 + (yh + dy) % 2

    def relay_up(slot):
        return remote(slot, slot, doc_send, doc_recv.at[6], xup)

    def relay_down(slot):
        return remote(slot, slot, doc_send, doc_recv.at[5], xdown)

    def relay_far(slot, h):
        block = some(slot, h * 64, 64)
        return remote(block, block, doc_send, doc_recv.at[(4, 9)[h]], xup if h else xdown)

    def relay_y(slot):
        return remote(slot, slot, doc_send, doc_recv.at[7], ypart)

    def part_in(k, start, size, rsem):
        block = some(doc_slot(place(k), co), start, size)
        remote(block, block, doc_send, doc_recv.at[rsem], ypart).wait_recv()

    def far():
        part_in(1, 0, 64, 1)
        part_in(2, 64, 64, 2)
        for h in range(2):
            relay_far(doc_slot(place(1 + h), co), h).start()

    def take(k):
        slot = doc_slot(place(k), co)
        if k == 1:
            part_in(1, 64, 64, 12)
        elif k == 2:
            part_in(2, 0, 64, 8)
        elif k == 4:
            part_in(4, 0, 64, 4)
            part_in(4, 64, 64, 9)
            relay_y(slot).start()
        else:
            remote(slot, slot, doc_send, doc_recv.at[k], ypart).wait_recv()
        sib_copy(k, slot, place(k)).start()

    for copy in id_copies:
        copy.wait()
    named = (owner_ref[:, 0, :] * ROWS + row_ref[...]).astype(F32)
    high = jnp.floor(named * (1.0 / 4096.0))
    rest = named - 4096.0 * high
    mid = jnp.floor(rest * (1.0 / 64.0))
    digits = jnp.concatenate([high, mid, rest - 64.0 * mid], axis=0).astype(BF16)
    lane = lax.broadcasted_iota(jnp.int32, (COLS, TW), 1)
    spread = mm(digits, jnp.where(lane // SUB == lax.broadcasted_iota(jnp.int32, (COLS, TW), 0), 1.0, 0.0).astype(BF16))
    spread = 4096.0 * spread[0:SUB] + 64.0 * spread[SUB:2 * SUB] + spread[2 * SUB:3 * SUB]
    lane = lax.broadcasted_iota(jnp.int32, (SUB, TW), 1)
    own = jnp.sum(jnp.where(lane % SUB == lax.broadcasted_iota(jnp.int32, (SUB, TW), 0), spread, 0.0), axis=0, keepdims=True)
    own = jnp.where(lane[0:1] < SUB * COLS, own, -1.0)
    ids_ref[...] = jnp.where(lax.broadcasted_iota(jnp.int32, (LB, TW), 0) == lb, own, 0.0)
    def idl_copy(i):
        return remote(ids_ref, idl_ref.at[lb], idl_send, idl_recv, (dp, (lb + i) % LB))

    each(1, LB, lambda i: idl_copy(i).start())

    ts_ref[...] = jnp.zeros_like(ts_ref)
    st_ref[...] = jnp.zeros_like(st_ref)
    lab_copy.wait()

    def turn(i):
        labt[:, at(i * 256, 256)] = lab[at(i * 256, 256), :].T

    each(0, ROWS // 256, turn)
    half_copy(1, 12, xdown).start()
    half_copy(0, 8, xup).start()


    def raw_cols(p):
        return slice(p * GRP, (p + 1) * GRP)

    CH = 256

    def exp_rows(p, c, top, cols):
        s = lg_ref[c * CH:(c + 1) * CH, raw_cols(p)]
        e = jnp.exp((s - top) * C)
        e_ref[c * CH:(c + 1) * CH, cols] = e
        return jnp.sum(e, axis=0, keepdims=True)

    def keep(g, top, total):
        for h in range(2):
            st_ref[0, pl.ds(g * 2 + h, 1), :] = (top * C)[:, h * BLK:(h + 1) * BLK]
            st_ref[1, pl.ds(g * 2 + h, 1), :] = total[:, h * BLK:(h + 1) * BLK]

    def wait_sib(k):
        other = doc_slot(place(k), 1 - co)
        remote(other, other, sib_send, sib_recv.at[k], sib).wait_recv()

    def score_step(k, p, old_top):
        g = place(k)

        @pl.when(k < 5)
        def _():
            wait_sib(k)

        block = dall[pl.ds(g * 2, 2)].reshape(GRP, D)
        old = place((k + 7) % 8)
        cols = at(old * GRP, GRP)
        top, total = None, 0.0
        for c in range(ROWS // CH):
            s = lax.dot_general(lab[c * CH:(c + 1) * CH, :], block, NT, preferred_element_type=F32)
            lg_ref[c * CH:(c + 1) * CH, raw_cols(p)] = s
            high = jnp.max(s, axis=0, keepdims=True)
            top = high if top is None else jnp.maximum(top, high)
            total = total + exp_rows(1 - p, c, old_top, cols)
        keep(old, old_top, total)
        return top

    def ids_out():
        all_in(idl_ref.at[1:LB], idl_recv)
        idl_ref[lb] = ids_ref[...]
        acc = idl_ref[0]
        for q in range(1, LB):
            acc = acc + idl_ref[q]
        idg_ref[dp] = acc
        each(1, DP, lambda i: idg_copy(i).start())

    def idg_copy(i):
        return remote(idg_ref.at[dp], idg_ref.at[dp], idg_send, idg_recv, mate(i)[1])

    lane_8 = lax.broadcasted_iota(jnp.int32, (LB, 128), 1).astype(F32)
    lane_t = [lane_8 + 128.0 * v for v in range(3)]
    base = (me * ROWS).astype(F32)

    def find():
        all_in(idg_ref.at[1:DP], idg_recv)
        rel = idg_ref[...].reshape(DEV, TW) - base
        lanes = lax.broadcasted_iota(jnp.int32, (DEV, TW), 1).astype(F32)
        key = jnp.where((rel >= 0.0) & (rel < float(ROWS)), lanes * float(ROWS) + rel, BIG)
        for k in range(SLOTS):
            low = jnp.min(key, axis=1, keepdims=True)
            for b in range(DP):
                keys_ref[b % 2, b // 2, k * 8:k * 8 + 8, :] = jnp.broadcast_to(low[b * 8:b * 8 + 8], (8, 128))
            key = jnp.where(key == low, BIG, key)

    def parts_of(key):
        t = jnp.floor(key * (1.0 / ROWS))
        row = jnp.where(key < BIG, key - t * float(ROWS), -1.0)
        return t, row

    def fetch(c):
        lane_rows = lax.broadcasted_iota(jnp.int32, (256, ROWS), 1).astype(F32)
        out = []
        for h in range(2):
            _, row = parts_of(keys_ref[c, h * 4:h * 4 + 4].reshape(256, 128)[:, 0:1])
            pick = jnp.where(lane_rows == row, 1.0, 0.0).astype(BF16)
            out.append(mm(pick, lab[...]).astype(BF16).reshape(4, 64, D))
        for h in range(2):
            lrow_ref[c, h * 4:h * 4 + 4] = out[h]

    def named_copy():
        return remote(lrow_ref.at[1 - co], slr_ref, lr_sem.at[0], lr_sem.at[1], sib)

    def keys_copy():
        return remote(keys_ref.at[1 - co], skeys_ref, lr_sem.at[2], lr_sem.at[3], sib)

    def flip(i):
        _, row = parts_of(keys_ref[i // 4, pl.ds((i % 4) * 2, 2)].reshape(128, 128))
        rowt_ref[:, at(i * 128, 128)] = row.T[0:8, :]

    lane_doc = lax.broadcasted_iota(jnp.int32, (64, BLK), 1).astype(F32)
    slot_l = (lax.broadcasted_iota(jnp.int32, (64, BLK), 0) % 8).astype(F32)

    def doc_pick(key):
        t, _ = parts_of(key)
        d = t - 16.0 * jnp.floor(t * (1.0 / 16.0)) + 16.0 * slot_l
        return lane_doc == jnp.where(key < BIG, d, -1.0)

    def target(i):
        out = []
        for q in range(4):
            b = i * 4 + q
            c, j = q % 2, i * 2 + q // 2
            key = keys_ref[c, j]
            t, _ = parts_of(key)
            found = mm(jnp.where(doc_pick(key), 1.0, 0.0).astype(BF16), dall[b])
            score = C * jnp.sum(found * lrow_ref[c, j].astype(F32), axis=1, keepdims=True)
            slots = jnp.full((LB, 128), -1.0, F32)
            for k in range(SLOTS):
                slots = jnp.where(lane_8 == float(k), score[k * 8:k * 8 + 8], slots)
                slots = jnp.where(lane_8 == float(SLOTS + k), t[k * 8:k * 8 + 8], slots)
            out.append((b, c, j, found.astype(BF16), slots))
        for b, c, j, found, slots in out:
            grow_ref[c, j] = found
            ts_ref[b] = slots

    def t1_copy(i):
        q, to = mate(i)
        return remote(ts_ref.at[q], tr_ref.at[dp], t1_send, t1_recv, to)


    def s1_copy(i):
        return remote(st_ref.at[1], sr_ref.at[lb], s1_send, s1_recv, (dp, (lb + i) % LB))

    def s2_copy(i):
        return remote(sv_ref.at[dp], sv_ref.at[dp], s2_send, s2_recv, mate(i)[1])

    def sst_copy():
        return remote(st_ref.at[0], sst_ref, sst_sem.at[0], sst_sem.at[1], sib)

    def merge(count, ref):
        tops = [ref[q] for q in range(count)]
        top = functools.reduce(jnp.maximum, tops)
        total = 0.0
        for q in range(count):
            total = total + jnp.exp(tops[q] - top)
        return top + jnp.log(total)

    def stats_on():
        all_in(sr_ref.at[1:LB], s1_recv)
        sr_ref[lb] = st_ref[1]
        sv_ref[dp] = merge(LB, sr_ref)
        each(1, DP, lambda i: s2_copy(i).start())

    def totals():
        all_in(sv_ref.at[1:DP], s2_recv)
        lt_ref[...] = merge(DP, sv_ref)

    def core_copy(j):
        return remote(u_ref.at[at((j * 2 + 1 - co) * BLK, BLK), :], rc_ref.at[j], rc_send, rc_recv, sib)

    def doc_part(g):
        part = mm(labt[...], e_ref[:, at(g * GRP, GRP)].astype(BF16))
        u_ref[at(g * GRP, GRP), :] = part.T

    def exp_group(p, g, top):
        total = 0.0
        for c in range(ROWS // CH):
            total = total + exp_rows(p, c, top, at(g * GRP, GRP))
        keep(g, top, total)

    def score_pair(i, top):
        @pl.when(i == 1)
        def _():
            slot = doc_slot(place(3), co)
            relay_up(slot).start()
            relay_down(slot).start()

        top = score_step(i * 2, 0, top)

        @pl.when(i == 0)
        def _():
            exp_group(0, g_own, top)
            doc_part(g_own)
            core_copy(g_own).start()
            far()
            ids_out()
            for k in (1, 2, 3):
                take(k)

        @pl.when(i == 2)
        def _():
            find()
            fetch(0)
            take(5)
            take(6)
            fetch(1)
            take(7)
            each(0, 8, flip)
            for k in (5, 6, 7):
                wait_sib(k)
            each(0, 4, target)
            each(1, DP, lambda i: t1_copy(i).start())

        top = score_step(i * 2 + 1, 1, top)

        @pl.when(i == 1)
        def _():
            take(4)

        return top

    lg_ref[:, raw_cols(1)] = jnp.zeros((ROWS, GRP), F32)
    top = lax.fori_loop(0, 4, score_pair, jnp.zeros((1, GRP), F32))
    exp_group(1, place(7), top)

    st_ref[1] = st_ref[0] + jnp.log(st_ref[1])
    each(1, LB, lambda i: s1_copy(i).start())
    sst_copy().start()

    def t2_copy(i):
        return remote(tu_ref, tv_ref.at[lb], t2_send, t2_recv, (dp, (lb + i) % LB))

    def t3_copy(i):
        return remote(ca_ref.at[dp], ca_ref.at[dp], t3_send, t3_recv, mate(i)[1])

    def targets_on():
        all_in(tr_ref.at[1:DP], t1_recv)
        tr_ref[dp] = ts_ref[dp]
        acc = [jnp.zeros((LB, 128), F32)] * 3
        for q in range(DP):
            slots = tr_ref[q]
            for k in range(SLOTS):
                score, t = slots[:, k:k + 1], slots[:, SLOTS + k:SLOTS + k + 1]
                for v in range(3):
                    acc[v] = acc[v] + jnp.where(lane_t[v] == t, score, 0.0)
        for v in range(3):
            tu_ref[:, v * 128:(v + 1) * 128] = acc[v]
        each(1, LB, lambda i: t2_copy(i).start())

    def coefficients_on():
        all_in(tv_ref.at[1:LB], t2_recv)
        tv_ref[lb] = tu_ref[...]
        acc = tv_ref[0]
        for q in range(1, LB):
            acc = acc + tv_ref[q]
        lane = lax.broadcasted_iota(jnp.int32, (LB, 128), 1)
        pos = jnp.where(lane < 16, acc[:, 0:128], 0.0)
        for s in (16, 32, 64):
            pos = pos + pltpu.roll(pos, s, 1)
        soft = jnp.zeros((LB, 128), F32)
        weight = jnp.zeros((LB, 128), F32)
        pieces = []
        for v in range(3):
            gap = acc[:, v * 128:(v + 1) * 128] - pos + 1.0
            use = (lane >= 16) if v == 0 else (lane >= 0) if v == 1 else (lane < 16)
            small = jnp.exp(-jnp.abs(gap))
            soft = soft + jnp.where(use, jnp.maximum(gap, 0.0) + jnp.log(1.0 + small), 0.0)
            sig = jnp.where(use, jnp.where(gap >= 0.0, 1.0, small) / (1.0 + small) * (1.0 / 16.0), 0.0)
            weight = weight + sig
            pieces.append(sig)
        for s in (16, 32, 64):
            soft = soft + pltpu.roll(soft, s, 1)
            weight = weight + pltpu.roll(weight, s, 1)
        tmp_ref[...] = soft * (1.0 / 16.0) - pos
        pieces[0] = jnp.where(lane < 16, -1.0 - weight, pieces[0])
        for v in range(3):
            ca_ref[dp, :, v * 128:(v + 1) * 128] = pieces[v]
        each(1, DP, lambda i: t3_copy(i).start())

    targets_on()
    named_copy().start()
    keys_copy().start()

    def doc_mm(k):
        doc_part(place(k))

        core_copy(place(k)).start()

        @pl.when(k == 4)
        def _():
            stats_on()
            coefficients_on()

    each(1, 8, doc_mm)
    totals()
    all_in(rc_ref, rc_recv)
    sst_copy().wait_recv()

    def column(row):
        return jnp.concatenate([jnp.broadcast_to(row, (BLK, BLK)).T] * (D // BLK), axis=1)

    def merge_cores(i):
        out = []
        for q in range(4):
            j = i * 4 + q
            b = j * 2 + co
            log_total = lt_ref[pl.ds(b, 1), :]
            col = column(jnp.exp(st_ref[0, pl.ds(b, 1), :] - log_total))
            scol = column(jnp.exp(sst_ref[pl.ds(b, 1), :] - log_total))
            out.append((b, u_ref[at(b * BLK, BLK), :] * col + rc_ref[j] * scol))
        for b, value in out:
            u_ref[at(b * BLK, BLK), :] = value

    each(0, 2, merge_cores)
    shifted = pltpu.roll(jnp.broadcast_to(lt_ref[pl.ds(dp, 1), :], (8, BLK)), (BLK - lb * SUB) % BLK, 1)
    loss_ref[...] = tmp_ref[pl.ds(lb, 1), :] + shifted[0:1, :]

    all_in(ca_ref.at[1:DP], t3_recv)

    def slot_coef(b, t):
        out = []
        for k in range(SLOTS):
            hit = [jnp.where(lane_t[v] == t[k * 8:k * 8 + 8], ca_ref[b, :, v * 128:(v + 1) * 128], 0.0) for v in range(3)]
            out.append(jnp.sum(hit[0] + hit[1] + hit[2], axis=1, keepdims=True))
        return jnp.concatenate(out, axis=0)

    def scaled_pick(key, coef):
        hi, lo = split(coef)
        pick = doc_pick(key)
        return [jnp.where(pick, hi, 0.0), jnp.where(pick, lo, 0.0)]

    def finish(i):
        out = []
        for q in range(4):
            j = i * 4 + q
            b = j * 2 + co
            key, skey = keys_ref[co, j], skeys_ref[j]
            coef, scoef = slot_coef(b, parts_of(key)[0]), slot_coef(b, parts_of(skey)[0])
            pick = jnp.concatenate(scaled_pick(key, coef) + scaled_pick(skey, scoef), axis=0).T.astype(BF16)
            named, snamed = lrow_ref[co, j], slr_ref[j]
            hard = mm(pick, jnp.concatenate([named, named, snamed, snamed], axis=0))
            out.append((j, coef, C * (u_ref[at(b * BLK, BLK), :] + hard)))
        for j, coef, value in out:
            coef_ref[co, j] = jnp.broadcast_to(coef, (64, 128))
            xx, hh = j // 2, j % 2
            for zz in range(NZ):
                for ll in range(NYL):
                    off = (zz * NYL + ll) * SUB
                    u = value[off:off + SUB]
                    yy = hh * 2 + ll
                    w_ref[0, xx, yy, zz] = u[:, 0:FG]
                    w_ref[1, yy, zz, xx] = u[:, FG:2 * FG]
                    w_ref[2, zz, xx, yy] = u[:, 2 * FG:3 * FG]

    named_copy().wait_recv()
    keys_copy().wait_recv()
    each(0, 2, finish)

    spot = (x, y, z)
    def ring_msg(f, m, p=None):
        h = spot[f]
        up, down = on_axis(f, (h + 1) % 4), on_axis(f, (h + 3) % 4)

        def part(block, which):
            if p is None:
                return w_ref.at[f, block % 4, which * 2:which * 2 + 2]
            return w_ref.at[f, block % 4, which * 2 + p]

        box = q0_ref.at[f, m] if p is None else q0_ref.at[f, m, p]
        if m >= 4:
            source = q0_ref.at[f, m - 4, p]
        else:
            source = (part(h + 2, 0), part(h + 2, 1), part(h + 3, 1), part(h + 1, 0))[m]
        to = (down, up, down, up, down, up)[m]
        return remote(source, box, rs_send.at[0], rs_recv.at[2 if m >= 2 else p], to)

    def ring_start(msgs, p=None):
        for m in msgs:
            for f in range(3):
                ring_msg(f, m, p).start()

    def ring_relay(p):
        all_in(q0_ref.at[:, 0:2, p], rs_recv.at[p])
        for f in range(3):
            h = spot[f]
            for m in range(2):
                block = (h + 3) % 4 if m == 0 else (h + 1) % 4
                q0_ref[f, m, p] = q0_ref[f, m, p] + w_ref[f, block, m * 2 + p]
                ring_msg(f, 4 + m, p).start()

    def ring_done():
        all_in(q0_ref.at[:, 2:6], rs_recv.at[2])
        for f in range(3):
            h = spot[f]
            v1_ref[f, 0:2] = w_ref[f, h, 0:2] + q0_ref[f, 4] + q0_ref[f, 3]
            v1_ref[f, 2:4] = w_ref[f, h, 2:4] + q0_ref[f, 2] + q0_ref[f, 5]

    bufs = {1: (v1_ref, q1_ref), 2: (v2_ref, q2_ref)}

    def straight(step, f, i):
        axis = (f + step) % 3
        to = (spot[axis] + i) % 4
        src, box = bufs[step]
        return remote(src.at[f, to], box.at[f, i - 1], rs_send.at[step], rs_recv.at[step + 2], on_axis(axis, to))

    def straight_start(step):
        for i in (2, 1, 3):
            for f in range(3):
                straight(step, f, i).start()

    def straight_done(step):
        src, box = bufs[step]
        all_in(box, rs_recv.at[step + 2])
        return [src[f, spot[(f + step) % 3]] + box[f, 0] + box[f, 1] + box[f, 2] for f in range(3)]

    ring_start((0, 1), 0)

    def coef_rows(i):
        hi, lo = split(coef_ref[i // 4, pl.ds((i % 4) * 2, 2)].reshape(128, 128).T[0:8, :])
        coeft_ref[0, :, at(i * 128, 128)] = hi
        coeft_ref[1, :, at(i * 128, 128)] = lo

    def other_coef(i):
        out = []
        for q in range(4):
            j = i * 4 + q
            out.append((j, slot_coef(j * 2 + 1 - co, parts_of(keys_ref[1 - co, j])[0])))
        for j, coef in out:
            coef_ref[1 - co, j] = jnp.broadcast_to(coef, (64, 128))

    ring_start((0, 1), 1)
    each(0, 2, other_coef)
    each(0, 8, coef_rows)
    for b in range(DP):
        scale = jnp.exp(st_ref[0, b:b + 1, :] - lt_ref[b:b + 1, :])
        scale_ref[:, b * BLK:(b + 1) * BLK] = jnp.broadcast_to(scale, (8, BLK))

    def label_mm(r):
        rows = at(r * TILE, TILE)
        probs = (e_ref[rows, :] * scale_ref[0:1, :]).astype(BF16)
        sub_rows = (lax.broadcasted_iota(jnp.int32, (TILE, DEV * SLOTS), 0) + r * TILE).astype(F32)
        pick = sub_rows == rowt_ref[0:1, :]
        named = grow_ref[...].reshape(DEV * SLOTS, D)
        value = mm(probs, dall[...].reshape(DOCS, D))
        for p in range(2):
            value = value + mm(jnp.where(pick, coeft_ref[p, 0:1, :], 0.0).astype(BF16), named)
        lg_ref[rows, :] = C * value

        @pl.when(r == 0)
        def _():
            ring_start((2, 3))

        @pl.when(r == 1)
        def _():
            ring_relay(0)

        @pl.when(r == 2)
        def _():
            ring_relay(1)

        @pl.when(r == 4)
        def _():
            ring_done()
            straight_start(1)

        @pl.when(r == 6)
        def _():
            for f, value in enumerate(straight_done(1)):
                v2_ref[f] = value
            straight_start(2)

    each(0, ROWS // TILE, label_mm)

    for f, value in enumerate(straight_done(2)):
        dg_ref[:, f * FG:(f + 1) * FG] = value

    all_out(dall.at[0:7], doc_send)
    all_out(dall.at[0:8], sib_send)
    all_out(rc_ref, rc_send)
    for copy in (sst_copy(), named_copy(), keys_copy()):
        copy.wait_send()
    all_out(idl_ref.at[1:LB], idl_send)
    all_out(idg_ref.at[1:DP], idg_send)
    all_out(sr_ref.at[1:LB], s1_send)
    all_out(sv_ref.at[1:DP], s2_send)
    all_out(tr_ref.at[1:DP], t1_send)
    all_out(tv_ref.at[1:LB], t2_send)
    all_out(ca_ref.at[1:DP], t3_send)
    all_out(q0_ref, rs_send.at[0])
    all_out(q1_ref, rs_send.at[1])
    all_out(q2_ref, rs_send.at[2])


def ship(lg_in, dg_in, loss_in, lg_out, dg_out, loss_out, sems):
    copies = [pltpu.make_async_copy(lg_in, lg_out, sems.at[0]), pltpu.make_async_copy(dg_in, dg_out, sems.at[1])]
    for copy in copies:
        copy.start()
    loss_out[...] = loss_in[0, 0:SUB]
    for copy in copies:
        copy.wait()


def shards(documents, labels, target_owner, target_row):
    vm = pl.BlockSpec(memory_space=pltpu.VMEM)
    hbm = pl.BlockSpec(memory_space=pl.ANY)
    dma = pltpu.SemaphoreType.DMA
    slots = DEV * SLOTS
    label_grad, doc_grad, loss = pl.pallas_call(
        kernel,
        out_shape=(
            pltpu.VMEM((ROWS, D), F32),
            pltpu.VMEM((SUB, D), F32),
            pltpu.VMEM((1, 128), F32),
        ),
        in_specs=[hbm, hbm, hbm, hbm],
        out_specs=(vm, vm, vm),
        scratch_shapes=[
            pltpu.VMEM((ROWS, D), BF16),
            pltpu.VMEM((DP, BLK, D), BF16),
            pltpu.VMEM((D, ROWS), BF16),
            pltpu.VMEM((ROWS, DOCS), F32),
            pltpu.VMEM((DOCS, D), F32),
            pltpu.VMEM((8, BLK, D), F32),
            pltpu.VMEM((3, 4, 4, 4, SUB, FG), F32),
            pltpu.VMEM((3, 4, 4, SUB, FG), F32),
            pltpu.VMEM((3, 4, SUB, FG), F32),
            pltpu.VMEM((3, 6, 2, 4, SUB, FG), F32),
            pltpu.VMEM((3, 3, 4, SUB, FG), F32),
            pltpu.VMEM((3, 3, SUB, FG), F32),
            pltpu.VMEM((SUB, 1, COLS), jnp.int32),
            pltpu.VMEM((SUB, COLS), jnp.int32),
            pltpu.VMEM((LB, TW), F32),
            pltpu.VMEM((LB, LB, TW), F32),
            pltpu.VMEM((DP, LB, TW), F32),
            pltpu.VMEM((2, 8, 64, 128), F32),
            pltpu.VMEM((8, 64, 128), F32),
            pltpu.VMEM((8, slots), F32),
            pltpu.VMEM((2, 8, 64, D), BF16),
            pltpu.VMEM((8, 64, D), BF16),
            pltpu.VMEM((2, 8, 64, D), BF16),
            pltpu.VMEM((2, DP, BLK), F32),
            pltpu.VMEM((LB, DP, BLK), F32),
            pltpu.VMEM((DP, DP, BLK), F32),
            pltpu.VMEM((DP, BLK), F32),
            pltpu.VMEM((DP, BLK), F32),
            pltpu.VMEM((DP, LB, 128), F32),
            pltpu.VMEM((DP, LB, 128), F32),
            pltpu.VMEM((LB, TW), F32),
            pltpu.VMEM((LB, LB, TW), F32),
            pltpu.VMEM((DP, LB, TW), F32),
            pltpu.VMEM((8, DOCS), F32),
            pltpu.VMEM((LB, 128), F32),
            pltpu.VMEM((2, 8, 64, 128), F32),
            pltpu.VMEM((2, 8, slots), F32),
            dma, dma, dma((2,)), dma, dma((13,)), dma, dma((8,)),
            dma, dma, dma, dma,
            dma, dma, dma, dma, dma((2,)), dma((4,)),
            dma, dma, dma, dma, dma, dma,
            dma, dma, dma((3,)), dma((5,)),
        ],
        compiler_params=pltpu.CompilerParams(
            collective_id=0, has_side_effects=True, vmem_limit_bytes=56 * 1024 * 1024
        ),
        cost_estimate=pl.CostEstimate(
            flops=8 * ROWS * DOCS * D, bytes_accessed=10 * ROWS * D, transcendentals=ROWS * DOCS
        ),
        name="head",
    )(documents, labels, target_owner.transpose(0, 2, 1), target_row)
    label_grad, doc_grad, loss = pl.pallas_call(
        ship,
        out_shape=(
            jax.ShapeDtypeStruct((ROWS, D), F32),
            jax.ShapeDtypeStruct((SUB, D), F32),
            jax.ShapeDtypeStruct((SUB,), F32),
        ),
        in_specs=[vm, vm, vm],
        out_specs=(hbm, hbm, vm),
        scratch_shapes=[dma((2,))],
        compiler_params=pltpu.CompilerParams(vmem_limit_bytes=32 * 1024 * 1024),
        name="ship",
    )(label_grad, doc_grad, loss)
    return loss, doc_grad, label_grad


def solution(mesh):
    return jax.shard_map(
        shards,
        mesh=mesh,
        in_specs=(
            P("dp", None),
            P(("dp", "label"), None),
            P(("dp", "label"), None, None),
            P(("dp", "label"), None),
        ),
        out_specs=(P(("dp", "label")), P(("dp", "label"), None), P(("dp", "label"), None)),
        check_vma=False,
    )
```

```python
import functools
import math

import jax
import jax.numpy as jnp
from jax import lax
from jax.experimental import pallas as pl
from jax.experimental.pallas import tpu as pltpu
from jax.sharding import PartitionSpec as P

MESH = pl.DeviceIdType.MESH
F32 = jnp.float32
BF16 = jnp.bfloat16

NX, NYH, NC, NZ, NYL = 4, 2, 2, 4, 2
DP, LB = 16, 8
DEV = DP * LB
SUB = 16
BLK = SUB * LB
GRP = 2 * BLK
DOCS = DP * BLK
D = 768
ROWS = 2048
COLS = 17
TW = 384
SLOTS = 8
BIG = float(2 ** 23)
FG = 256
C = 4.0 / math.sqrt(D)
TILE = 256

NT = (((1,), (1,)), ((), ()))


def mm(a, b):
    return jnp.dot(a, b, preferred_element_type=F32)


def split(v):
    hi = v.astype(BF16).astype(F32)
    return hi, v - hi


def kernel(
    docs_hbm, labels_hbm, owner_hbm, row_hbm,
    lg_ref, dg_ref, loss_ref,
    lab, dall, labt, e_ref, u_ref, rc_ref, w_ref, v1_ref, v2_ref, q0_ref, q1_ref, q2_ref,
    owner_ref, row_ref, ids_ref, idl_ref, idg_ref, keys_ref, skeys_ref, rowt_ref, lrow_ref, slr_ref, grow_ref,
    st_ref, sr_ref, sv_ref, sst_ref, lt_ref,
    ts_ref, tr_ref, tu_ref, tv_ref, ca_ref, scale_ref, tmp_ref, coef_ref, coeft_ref,
    lab_sem, own_sem, in_sem, doc_send, doc_recv, sib_send, sib_recv,
    idl_send, idl_recv, idg_send, idg_recv,
    s1_send, s1_recv, s2_send, s2_recv, sst_sem, lr_sem,
    t1_send, t1_recv, t2_send, t2_recv, t3_send, t3_recv,
    rc_send, rc_recv, rs_send, rs_recv,
):
    dp = lax.axis_index("dp")
    lb = lax.axis_index("label")
    x, yh, co = dp // 4, (dp // 2) % 2, dp % 2
    z, yl = lb // 2, lb % 2
    y = yh * 2 + yl
    me = dp * LB + lb

    def dev(x_, yh_, co_, z_, yl_):
        return ((x_ * 2 + yh_) * 2 + co_, z_ * 2 + yl_)

    sib = dev(x, yh, 1 - co, z, yl)
    ypart = dev(x, 1 - yh, co, z, 1 - yl)

    def on_axis(axis, pos):
        if axis == 0:
            return dev(pos, yh, co, z, yl)
        if axis == 1:
            return dev(x, pos // 2, co, z, pos % 2)
        return dev(x, yh, co, pos, yl)

    xup, xdown = on_axis(0, (x + 1) % NX), on_axis(0, (x + 3) % NX)

    def mate(i):
        q = (dp + i) % DP
        return q, (q, z * 2 + jnp.where((q // 2) % 2 == yh, yl, 1 - yl))

    def all_in(ref, sem):
        pltpu.make_async_remote_copy(
            src_ref=ref, dst_ref=ref, send_sem=sem, recv_sem=sem, device_id=sib, device_id_type=MESH
        ).wait_recv()

    def all_out(ref, sem):
        pltpu.make_async_remote_copy(
            src_ref=ref, dst_ref=ref, send_sem=sem, recv_sem=sem, device_id=sib, device_id_type=MESH
        ).wait_send()

    def remote(src, dst, ssem, rsem, to):
        return pltpu.make_async_remote_copy(
            src_ref=src, dst_ref=dst, send_sem=ssem, recv_sem=rsem, device_id=to, device_id_type=MESH
        )

    def each(lo, hi, fn):
        def body(i, carry):
            fn(i)
            return carry

        lax.fori_loop(lo, hi, body, 0)

    def at(start, size):
        return pl.ds(pl.multiple_of(start, size), size)

    barrier = pltpu.get_barrier_semaphore()
    each(1, DP, lambda i: pl.semaphore_signal(barrier, inc=1, device_id=mate(i)[1], device_id_type=MESH))
    each(1, LB, lambda i: pl.semaphore_signal(barrier, inc=1, device_id=(dp, (lb + i) % LB), device_id_type=MESH))
    pl.semaphore_signal(barrier, inc=1, device_id=dev(x, 1 - yh, co, z, yl), device_id_type=MESH)
    lab_copy = pltpu.make_async_copy(labels_hbm, lab, lab_sem)
    lab_copy.start()
    g_own = x * 2 + yh

    def doc_slot(group, core):
        return dall.at[group * 2 + core]

    own_copy = pltpu.make_async_copy(docs_hbm, doc_slot(g_own, co), own_sem)
    own_copy.start()
    id_copies = [
        pltpu.make_async_copy(owner_hbm, owner_ref, in_sem.at[0]),
        pltpu.make_async_copy(row_hbm, row_ref, in_sem.at[1]),
    ]
    for copy in id_copies:
        copy.start()
    pl.semaphore_wait(barrier, DP - 1 + LB - 1 + 1)

    def sib_copy(k, src, group):
        return remote(src, doc_slot(group, co), sib_send, sib_recv.at[k], sib)

    own_copy.wait()
    sib_copy(0, doc_slot(g_own, co), g_own).start()
    def some(ref, start, size):
        return ref.at[start:start + size, :]

    def half_copy(h, rsem, to):
        block = some(doc_slot(g_own, co), h * 64, 64)
        return remote(block, block, doc_send, doc_recv.at[rsem], to)

    remote(doc_slot(g_own, co), doc_slot(g_own, co), doc_send, doc_recv.at[3], ypart).start()
    half_copy(0, 1, xdown).start()
    half_copy(1, 2, xup).start()

    def place(k):
        dx = jnp.where((k == 1) | (k == 5), 1, jnp.where((k == 2) | (k == 6), 3, jnp.where((k == 4) | (k == 7), 2, 0)))
        dy = jnp.where((k == 3) | (k >= 5), 1, 0)
        return ((x + dx) % NX) * 2 + (yh + dy) % 2

    def relay_up(slot):
        return remote(slot, slot, doc_send, doc_recv.at[6], xup)

    def relay_down(slot):
        return remote(slot, slot, doc_send, doc_recv.at[5], xdown)

    def relay_far(slot, h):
        block = some(slot, h * 64, 64)
        return remote(block, block, doc_send, doc_recv.at[(4, 9)[h]], xup if h else xdown)

    def relay_y(slot):
        return remote(slot, slot, doc_send, doc_recv.at[7], ypart)

    def part_in(k, start, size, rsem):
        block = some(doc_slot(place(k), co), start, size)
        remote(block, block, doc_send, doc_recv.at[rsem], ypart).wait_recv()

    def far():
        part_in(1, 0, 64, 1)
        part_in(2, 64, 64, 2)
        for h in range(2):
            relay_far(doc_slot(place(1 + h), co), h).start()

    def take(k):
        slot = doc_slot(place(k), co)
        if k == 1:
            part_in(1, 64, 64, 12)
        elif k == 2:
            part_in(2, 0, 64, 8)
        elif k == 4:
            part_in(4, 0, 64, 4)
            part_in(4, 64, 64, 9)
            relay_y(slot).start()
        else:
            remote(slot, slot, doc_send, doc_recv.at[k], ypart).wait_recv()
        sib_copy(k, slot, place(k)).start()

    for copy in id_copies:
        copy.wait()
    named = (owner_ref[:, 0, :] * ROWS + row_ref[...]).astype(F32)
    high = jnp.floor(named * (1.0 / 4096.0))
    rest = named - 4096.0 * high
    mid = jnp.floor(rest * (1.0 / 64.0))
    digits = jnp.concatenate([high, mid, rest - 64.0 * mid], axis=0).astype(BF16)
    lane = lax.broadcasted_iota(jnp.int32, (COLS, TW), 1)
    spread = mm(digits, jnp.where((lane // SUB + 1) % COLS == lax.broadcasted_iota(jnp.int32, (COLS, TW), 0), 1.0, 0.0).astype(BF16))
    spread = 4096.0 * spread[0:SUB] + 64.0 * spread[SUB:2 * SUB] + spread[2 * SUB:3 * SUB]
    lane = lax.broadcasted_iota(jnp.int32, (SUB, TW), 1)
    own = jnp.sum(jnp.where(lane % SUB == lax.broadcasted_iota(jnp.int32, (SUB, TW), 0), spread, 0.0), axis=0, keepdims=True)
    own = jnp.where(lane[0:1] < SUB * COLS, own, -1.0)
    ids_ref[...] = jnp.where(lax.broadcasted_iota(jnp.int32, (LB, TW), 0) == lb, own, 0.0)
    def idl_copy(i):
        return remote(ids_ref, idl_ref.at[lb], idl_send, idl_recv, (dp, (lb + i) % LB))

    each(1, LB, lambda i: idl_copy(i).start())

    ts_ref[...] = jnp.zeros_like(ts_ref)
    st_ref[...] = jnp.zeros_like(st_ref)
    lab_copy.wait()

    def turn(i):
        labt[:, at(i * 256, 256)] = lab[at(i * 256, 256), :].T

    each(0, ROWS // 256, turn)
    half_copy(1, 12, xdown).start()
    half_copy(0, 8, xup).start()


    def raw_cols(p):
        return slice(p * GRP, (p + 1) * GRP)

    CH = 256

    def exp_rows(p, c, top, cols):
        s = lg_ref[c * CH:(c + 1) * CH, raw_cols(p)]
        e = jnp.exp((s - top) * C)
        e_ref[c * CH:(c + 1) * CH, cols] = e
        return jnp.sum(e, axis=0, keepdims=True)

    def keep(g, top, total):
        for h in range(2):
            st_ref[0, pl.ds(g * 2 + h, 1), :] = (top * C)[:, h * BLK:(h + 1) * BLK]
            st_ref[1, pl.ds(g * 2 + h, 1), :] = total[:, h * BLK:(h + 1) * BLK]

    def wait_sib(k):
        other = doc_slot(place(k), 1 - co)
        remote(other, other, sib_send, sib_recv.at[k], sib).wait_recv()

    def score_step(k, p, old_top):
        g = place(k)

        @pl.when(k < 5)
        def _():
            wait_sib(k)

        block = dall[pl.ds(g * 2, 2)].reshape(GRP, D)
        old = place((k + 7) % 8)
        cols = at(old * GRP, GRP)
        top, total = None, 0.0
        for c in range(ROWS // CH):
            s = lax.dot_general(lab[c * CH:(c + 1) * CH, :], block, NT, preferred_element_type=F32)
            lg_ref[c * CH:(c + 1) * CH, raw_cols(p)] = s
            high = jnp.max(s, axis=0, keepdims=True)
            top = high if top is None else jnp.maximum(top, high)
            total = total + exp_rows(1 - p, c, old_top, cols)
        keep(old, old_top, total)
        return top

    def ids_out():
        all_in(idl_ref.at[1:LB], idl_recv)
        idl_ref[lb] = ids_ref[...]
        acc = idl_ref[0]
        for q in range(1, LB):
            acc = acc + idl_ref[q]
        idg_ref[dp] = acc
        each(1, DP, lambda i: idg_copy(i).start())

    def idg_copy(i):
        return remote(idg_ref.at[dp], idg_ref.at[dp], idg_send, idg_recv, mate(i)[1])

    lane_8 = lax.broadcasted_iota(jnp.int32, (LB, 128), 1).astype(F32)
    lane_t = [lane_8 + 128.0 * v for v in range(3)]
    base = (me * ROWS).astype(F32)

    def find():
        all_in(idg_ref.at[1:DP], idg_recv)
        rel = idg_ref[...].reshape(DEV, TW) - base
        lanes = lax.broadcasted_iota(jnp.int32, (DEV, TW), 1).astype(F32)
        key = jnp.where((rel >= 0.0) & (rel < float(ROWS)), lanes * float(ROWS) + rel, BIG)
        for k in range(SLOTS):
            low = jnp.min(key, axis=1, keepdims=True)
            for b in range(DP):
                keys_ref[b % 2, b // 2, k * 8:k * 8 + 8, :] = jnp.broadcast_to(low[b * 8:b * 8 + 8], (8, 128))
            key = jnp.where(key == low, BIG, key)

    def parts_of(key):
        t = jnp.floor(key * (1.0 / ROWS))
        row = jnp.where(key < BIG, key - t * float(ROWS), -1.0)
        return t, row

    def fetch(c):
        lane_rows = lax.broadcasted_iota(jnp.int32, (256, ROWS), 1).astype(F32)
        out = []
        for h in range(2):
            _, row = parts_of(keys_ref[c, h * 4:h * 4 + 4].reshape(256, 128)[:, 0:1])
            pick = jnp.where(lane_rows == row, 1.0, 0.0).astype(BF16)
            out.append(mm(pick, lab[...]).astype(BF16).reshape(4, 64, D))
        for h in range(2):
            lrow_ref[c, h * 4:h * 4 + 4] = out[h]

    def named_copy():
        return remote(lrow_ref.at[1 - co], slr_ref, lr_sem.at[0], lr_sem.at[1], sib)

    def keys_copy():
        return remote(keys_ref.at[1 - co], skeys_ref, lr_sem.at[2], lr_sem.at[3], sib)

    def flip(i):
        _, row = parts_of(keys_ref[i // 4, pl.ds((i % 4) * 2, 2)].reshape(128, 128))
        rowt_ref[:, at(i * 128, 128)] = row.T[0:8, :]

    lane_doc = lax.broadcasted_iota(jnp.int32, (64, BLK), 1).astype(F32)
    slot_l = (lax.broadcasted_iota(jnp.int32, (64, BLK), 0) % 8).astype(F32)

    def doc_pick(key):
        t, _ = parts_of(key)
        d = t - 16.0 * jnp.floor(t * (1.0 / 16.0)) + 16.0 * slot_l
        return lane_doc == jnp.where(key < BIG, d, -1.0)

    def target(i):
        out = []
        for q in range(4):
            c, j = q % 2, place(i * 2 + q // 2)
            b = j * 2 + c
            key = keys_ref[c, j]
            t, _ = parts_of(key)
            found = mm(jnp.where(doc_pick(key), 1.0, 0.0).astype(BF16), dall[b])
            score = C * jnp.sum(found * lrow_ref[c, j].astype(F32), axis=1, keepdims=True)
            slots = jnp.full((LB, 128), -1.0, F32)
            for k in range(SLOTS):
                slots = jnp.where(lane_8 == float(k), score[k * 8:k * 8 + 8], slots)
                slots = jnp.where(lane_8 == float(SLOTS + k), t[k * 8:k * 8 + 8], slots)
            out.append((b, c, j, found.astype(BF16), slots))
        for b, c, j, found, slots in out:
            grow_ref[c, j] = found
            ts_ref[b] = slots

    def t1_copy(i):
        q, to = mate(i)
        return remote(ts_ref.at[q], tr_ref.at[dp], t1_send, t1_recv, to)


    def s1_copy(i):
        return remote(st_ref.at[1], sr_ref.at[lb], s1_send, s1_recv, (dp, (lb + i) % LB))

    def s2_copy(i):
        return remote(sv_ref.at[dp], sv_ref.at[dp], s2_send, s2_recv, mate(i)[1])

    def sst_copy():
        return remote(st_ref.at[0], sst_ref, sst_sem.at[0], sst_sem.at[1], sib)

    def merge(count, ref):
        tops = [ref[q] for q in range(count)]
        top = functools.reduce(jnp.maximum, tops)
        total = 0.0
        for q in range(count):
            total = total + jnp.exp(tops[q] - top)
        return top + jnp.log(total)

    def stats_on():
        all_in(sr_ref.at[1:LB], s1_recv)
        sr_ref[lb] = st_ref[1]
        sv_ref[dp] = merge(LB, sr_ref)
        each(1, DP, lambda i: s2_copy(i).start())

    def totals():
        all_in(sv_ref.at[1:DP], s2_recv)
        lt_ref[...] = merge(DP, sv_ref)

    def core_copy(j):
        return remote(u_ref.at[at((j * 2 + 1 - co) * BLK, BLK), :], rc_ref.at[j], rc_send, rc_recv, sib)

    def doc_part(g):
        part = mm(labt[...], e_ref[:, at(g * GRP, GRP)].astype(BF16))
        u_ref[at(g * GRP, GRP), :] = part.T

    def exp_group(p, g, top):
        total = 0.0
        for c in range(ROWS // CH):
            total = total + exp_rows(p, c, top, at(g * GRP, GRP))
        keep(g, top, total)

    def score_pair(i, top):
        @pl.when(i == 1)
        def _():
            slot = doc_slot(place(3), co)
            relay_up(slot).start()
            relay_down(slot).start()

        top = score_step(i * 2, 0, top)

        @pl.when(i == 0)
        def _():
            exp_group(0, g_own, top)
            doc_part(g_own)
            core_copy(g_own).start()
            far()
            ids_out()
            for k in (1, 2, 3):
                take(k)

        @pl.when(i == 2)
        def _():
            find()
            fetch(0)
            take(5)
            take(6)
            fetch(1)
            take(7)
            wait_sib(5)

            def targets(i):
                @pl.when(i == 3)
                def _():
                    wait_sib(6)
                    wait_sib(7)

                target(i)

            each(0, 4, targets)
            each(1, DP, lambda i: t1_copy(i).start())
            each(0, 8, flip)

        top = score_step(i * 2 + 1, 1, top)

        @pl.when(i == 1)
        def _():
            take(4)

        return top

    lg_ref[:, raw_cols(1)] = jnp.zeros((ROWS, GRP), F32)
    top = lax.fori_loop(0, 4, score_pair, jnp.zeros((1, GRP), F32))
    exp_group(1, place(7), top)

    st_ref[1] = st_ref[0] + jnp.log(st_ref[1])
    each(1, LB, lambda i: s1_copy(i).start())
    sst_copy().start()

    def t2_copy(i):
        return remote(tu_ref, tv_ref.at[lb], t2_send, t2_recv, (dp, (lb + i) % LB))

    def t3_copy(i):
        return remote(ca_ref.at[dp, :, 0:256], ca_ref.at[dp, :, 0:256], t3_send, t3_recv, mate(i)[1])

    def targets_on():
        all_in(tr_ref.at[1:DP], t1_recv)
        tr_ref[dp] = ts_ref[dp]
        acc = [jnp.zeros((LB, 128), F32)] * 3
        for q in range(DP):
            slots = tr_ref[q]
            for k in range(SLOTS):
                score, t = slots[:, k:k + 1], slots[:, SLOTS + k:SLOTS + k + 1]
                for v in range(3):
                    acc[v] = acc[v] + jnp.where(lane_t[v] == t, score, 0.0)
        for v in range(3):
            tu_ref[:, v * 128:(v + 1) * 128] = acc[v]
        each(1, LB, lambda i: t2_copy(i).start())

    def spread_16(value):
        for shift in (16, 32, 64):
            value = value + pltpu.roll(value, shift, 1)
        return value

    def positives():
        for q in range(DP):
            ca_ref[q, :, 256:384] = -1.0 - spread_16(ca_ref[q, :, 0:128] + ca_ref[q, :, 128:256])

    def coefficients_on():
        all_in(tv_ref.at[1:LB], t2_recv)
        tv_ref[lb] = tu_ref[...]
        acc = tv_ref[0]
        for q in range(1, LB):
            acc = acc + tv_ref[q]
        lane = lax.broadcasted_iota(jnp.int32, (LB, 128), 1)
        pos = spread_16(jnp.where(lane < SUB, acc[:, 256:384], 0.0))
        soft = jnp.zeros((LB, 128), F32)
        for v in range(2):
            gap = acc[:, v * 128:(v + 1) * 128] - pos + 1.0
            small = jnp.exp(-jnp.abs(gap))
            soft = soft + jnp.maximum(gap, 0.0) + jnp.log(1.0 + small)
            ca_ref[dp, :, v * 128:(v + 1) * 128] = jnp.where(gap >= 0.0, 1.0, small) / (1.0 + small) * (1.0 / 16.0)
        tmp_ref[...] = spread_16(soft) * (1.0 / 16.0) - pos
        each(1, DP, lambda i: t3_copy(i).start())

    targets_on()
    named_copy().start()
    keys_copy().start()

    def doc_mm(k):
        doc_part(place(k))

        core_copy(place(k)).start()

        @pl.when(k == 4)
        def _():
            stats_on()
            coefficients_on()

    each(1, 8, doc_mm)
    totals()
    all_in(rc_ref, rc_recv)
    sst_copy().wait_recv()

    def column(row):
        return jnp.concatenate([jnp.broadcast_to(row, (BLK, BLK)).T] * (D // BLK), axis=1)

    def merge_cores(i):
        out = []
        for q in range(4):
            j = i * 4 + q
            b = j * 2 + co
            log_total = lt_ref[pl.ds(b, 1), :]
            col = column(jnp.exp(st_ref[0, pl.ds(b, 1), :] - log_total))
            scol = column(jnp.exp(sst_ref[pl.ds(b, 1), :] - log_total))
            out.append((b, u_ref[at(b * BLK, BLK), :] * col + rc_ref[j] * scol))
        for b, value in out:
            u_ref[at(b * BLK, BLK), :] = value

    each(0, 2, merge_cores)
    shifted = pltpu.roll(jnp.broadcast_to(lt_ref[pl.ds(dp, 1), :], (8, BLK)), (BLK - lb * SUB) % BLK, 1)
    loss_ref[...] = tmp_ref[pl.ds(lb, 1), :] + shifted[0:1, :]

    all_in(ca_ref.at[1:DP, :, 0:256], t3_recv)
    positives()

    def slot_coef(b, t):
        out = []
        for k in range(SLOTS):
            hit = [jnp.where(lane_t[v] == t[k * 8:k * 8 + 8], ca_ref[b, :, v * 128:(v + 1) * 128], 0.0) for v in range(3)]
            out.append(jnp.sum(hit[0] + hit[1] + hit[2], axis=1, keepdims=True))
        return jnp.concatenate(out, axis=0)

    def scaled_pick(key, coef):
        hi, lo = split(coef)
        pick = doc_pick(key)
        return [jnp.where(pick, hi, 0.0), jnp.where(pick, lo, 0.0)]

    def finish(i):
        out = []
        for q in range(4):
            j = i * 4 + q
            b = j * 2 + co
            key, skey = keys_ref[co, j], skeys_ref[j]
            coef, scoef = slot_coef(b, parts_of(key)[0]), slot_coef(b, parts_of(skey)[0])
            pick = jnp.concatenate(scaled_pick(key, coef) + scaled_pick(skey, scoef), axis=0).T.astype(BF16)
            named, snamed = lrow_ref[co, j], slr_ref[j]
            hard = mm(pick, jnp.concatenate([named, named, snamed, snamed], axis=0))
            out.append((j, coef, C * (u_ref[at(b * BLK, BLK), :] + hard)))
        for j, coef, value in out:
            coef_ref[co, j] = jnp.broadcast_to(coef, (64, 128))
            xx, hh = j // 2, j % 2
            for zz in range(NZ):
                for ll in range(NYL):
                    off = (zz * NYL + ll) * SUB
                    u = value[off:off + SUB]
                    yy = hh * 2 + ll
                    w_ref[0, xx, yy, zz] = u[:, 0:FG]
                    w_ref[1, yy, zz, xx] = u[:, FG:2 * FG]
                    w_ref[2, zz, xx, yy] = u[:, 2 * FG:3 * FG]

    named_copy().wait_recv()
    keys_copy().wait_recv()
    each(0, 2, finish)

    spot = (x, y, z)
    def ring_msg(f, m, p=None):
        h = spot[f]
        up, down = on_axis(f, (h + 1) % 4), on_axis(f, (h + 3) % 4)

        def part(block, which):
            if p is None:
                return w_ref.at[f, block % 4, which * 2:which * 2 + 2]
            return w_ref.at[f, block % 4, which * 2 + p]

        box = q0_ref.at[f, m] if p is None else q0_ref.at[f, m, p]
        if m >= 4:
            source = q0_ref.at[f, m - 4, p]
        else:
            source = (part(h + 2, 0), part(h + 2, 1), part(h + 3, 1), part(h + 1, 0))[m]
        to = (down, up, down, up, down, up)[m]
        return remote(source, box, rs_send.at[0], rs_recv.at[2 if m >= 2 else p], to)

    def ring_start(msgs, p=None):
        for m in msgs:
            for f in range(3):
                ring_msg(f, m, p).start()

    def ring_relay(p):
        all_in(q0_ref.at[:, 0:2, p], rs_recv.at[p])
        for f in range(3):
            h = spot[f]
            for m in range(2):
                block = (h + 3) % 4 if m == 0 else (h + 1) % 4
                q0_ref[f, m, p] = q0_ref[f, m, p] + w_ref[f, block, m * 2 + p]
                ring_msg(f, 4 + m, p).start()

    def ring_done():
        all_in(q0_ref.at[:, 2:6], rs_recv.at[2])
        for f in range(3):
            h = spot[f]
            v1_ref[f, 0:2] = w_ref[f, h, 0:2] + q0_ref[f, 4] + q0_ref[f, 3]
            v1_ref[f, 2:4] = w_ref[f, h, 2:4] + q0_ref[f, 2] + q0_ref[f, 5]

    bufs = {1: (v1_ref, q1_ref), 2: (v2_ref, q2_ref)}

    def straight(step, f, i):
        axis = (f + step) % 3
        to = (spot[axis] + i) % 4
        src, box = bufs[step]
        return remote(src.at[f, to], box.at[f, i - 1], rs_send.at[step], rs_recv.at[step + 2], on_axis(axis, to))

    def straight_start(step):
        for i in (2, 1, 3):
            for f in range(3):
                straight(step, f, i).start()

    def straight_done(step):
        src, box = bufs[step]
        all_in(box, rs_recv.at[step + 2])
        return [src[f, spot[(f + step) % 3]] + box[f, 0] + box[f, 1] + box[f, 2] for f in range(3)]

    ring_start((0, 1), 0)

    def coef_rows(i):
        hi, lo = split(coef_ref[i // 4, pl.ds((i % 4) * 2, 2)].reshape(128, 128).T[0:8, :])
        coeft_ref[0, :, at(i * 128, 128)] = hi
        coeft_ref[1, :, at(i * 128, 128)] = lo

    def other_coef(i):
        out = []
        for q in range(4):
            j = i * 4 + q
            out.append((j, slot_coef(j * 2 + 1 - co, parts_of(keys_ref[1 - co, j])[0])))
        for j, coef in out:
            coef_ref[1 - co, j] = jnp.broadcast_to(coef, (64, 128))

    ring_start((0, 1), 1)
    each(0, 2, other_coef)
    each(0, 8, coef_rows)
    for b in range(DP):
        scale = jnp.exp(st_ref[0, b:b + 1, :] - lt_ref[b:b + 1, :])
        scale_ref[:, b * BLK:(b + 1) * BLK] = jnp.broadcast_to(scale, (8, BLK))

    def label_mm(r):
        rows = at(r * TILE, TILE)
        probs = (e_ref[rows, :] * scale_ref[0:1, :]).astype(BF16)
        sub_rows = (lax.broadcasted_iota(jnp.int32, (TILE, DEV * SLOTS), 0) + r * TILE).astype(F32)
        pick = sub_rows == rowt_ref[0:1, :]
        named = grow_ref[...].reshape(DEV * SLOTS, D)
        value = mm(probs, dall[...].reshape(DOCS, D))
        for p in range(2):
            value = value + mm(jnp.where(pick, coeft_ref[p, 0:1, :], 0.0).astype(BF16), named)
        lg_ref[rows, :] = C * value

        @pl.when(r == 0)
        def _():
            ring_start((2, 3))

        @pl.when(r == 1)
        def _():
            ring_relay(0)

        @pl.when(r == 2)
        def _():
            ring_relay(1)

        @pl.when(r == 4)
        def _():
            ring_done()
            straight_start(1)

        @pl.when(r == 6)
        def _():
            for f, value in enumerate(straight_done(1)):
                v2_ref[f] = value
            straight_start(2)

    each(0, ROWS // TILE, label_mm)

    for f, value in enumerate(straight_done(2)):
        dg_ref[:, f * FG:(f + 1) * FG] = value

    all_out(dall.at[0:7], doc_send)
    all_out(dall.at[0:8], sib_send)
    all_out(rc_ref, rc_send)
    for copy in (sst_copy(), named_copy(), keys_copy()):
        copy.wait_send()
    all_out(idl_ref.at[1:LB], idl_send)
    all_out(idg_ref.at[1:DP], idg_send)
    all_out(sr_ref.at[1:LB], s1_send)
    all_out(sv_ref.at[1:DP], s2_send)
    all_out(tr_ref.at[1:DP], t1_send)
    all_out(tv_ref.at[1:LB], t2_send)
    all_out(ca_ref.at[1:DP, :, 0:256], t3_send)
    all_out(q0_ref, rs_send.at[0])
    all_out(q1_ref, rs_send.at[1])
    all_out(q2_ref, rs_send.at[2])


def ship(lg_in, dg_in, loss_in, lg_out, dg_out, loss_out, sems):
    copies = [pltpu.make_async_copy(lg_in, lg_out, sems.at[0]), pltpu.make_async_copy(dg_in, dg_out, sems.at[1])]
    for copy in copies:
        copy.start()
    loss_out[...] = loss_in[0, 0:SUB]
    for copy in copies:
        copy.wait()


def shards(documents, labels, target_owner, target_row):
    vm = pl.BlockSpec(memory_space=pltpu.VMEM)
    hbm = pl.BlockSpec(memory_space=pl.ANY)
    dma = pltpu.SemaphoreType.DMA
    slots = DEV * SLOTS
    label_grad, doc_grad, loss = pl.pallas_call(
        kernel,
        out_shape=(
            pltpu.VMEM((ROWS, D), F32),
            pltpu.VMEM((SUB, D), F32),
            pltpu.VMEM((1, 128), F32),
        ),
        in_specs=[hbm, hbm, hbm, hbm],
        out_specs=(vm, vm, vm),
        scratch_shapes=[
            pltpu.VMEM((ROWS, D), BF16),
            pltpu.VMEM((DP, BLK, D), BF16),
            pltpu.VMEM((D, ROWS), BF16),
            pltpu.VMEM((ROWS, DOCS), F32),
            pltpu.VMEM((DOCS, D), F32),
            pltpu.VMEM((8, BLK, D), F32),
            pltpu.VMEM((3, 4, 4, 4, SUB, FG), F32),
            pltpu.VMEM((3, 4, 4, SUB, FG), F32),
            pltpu.VMEM((3, 4, SUB, FG), F32),
            pltpu.VMEM((3, 6, 2, 4, SUB, FG), F32),
            pltpu.VMEM((3, 3, 4, SUB, FG), F32),
            pltpu.VMEM((3, 3, SUB, FG), F32),
            pltpu.VMEM((SUB, 1, COLS), jnp.int32),
            pltpu.VMEM((SUB, COLS), jnp.int32),
            pltpu.VMEM((LB, TW), F32),
            pltpu.VMEM((LB, LB, TW), F32),
            pltpu.VMEM((DP, LB, TW), F32),
            pltpu.VMEM((2, 8, 64, 128), F32),
            pltpu.VMEM((8, 64, 128), F32),
            pltpu.VMEM((8, slots), F32),
            pltpu.VMEM((2, 8, 64, D), BF16),
            pltpu.VMEM((8, 64, D), BF16),
            pltpu.VMEM((2, 8, 64, D), BF16),
            pltpu.VMEM((2, DP, BLK), F32),
            pltpu.VMEM((LB, DP, BLK), F32),
            pltpu.VMEM((DP, DP, BLK), F32),
            pltpu.VMEM((DP, BLK), F32),
            pltpu.VMEM((DP, BLK), F32),
            pltpu.VMEM((DP, LB, 128), F32),
            pltpu.VMEM((DP, LB, 128), F32),
            pltpu.VMEM((LB, TW), F32),
            pltpu.VMEM((LB, LB, TW), F32),
            pltpu.VMEM((DP, LB, TW), F32),
            pltpu.VMEM((8, DOCS), F32),
            pltpu.VMEM((LB, 128), F32),
            pltpu.VMEM((2, 8, 64, 128), F32),
            pltpu.VMEM((2, 8, slots), F32),
            dma, dma, dma((2,)), dma, dma((13,)), dma, dma((8,)),
            dma, dma, dma, dma,
            dma, dma, dma, dma, dma((2,)), dma((4,)),
            dma, dma, dma, dma, dma, dma,
            dma, dma, dma((3,)), dma((5,)),
        ],
        compiler_params=pltpu.CompilerParams(
            collective_id=0, has_side_effects=True, vmem_limit_bytes=56 * 1024 * 1024
        ),
        cost_estimate=pl.CostEstimate(
            flops=8 * ROWS * DOCS * D, bytes_accessed=10 * ROWS * D, transcendentals=ROWS * DOCS
        ),
        name="head",
    )(documents, labels, target_owner.transpose(0, 2, 1), target_row)
    label_grad, doc_grad, loss = pl.pallas_call(
        ship,
        out_shape=(
            jax.ShapeDtypeStruct((ROWS, D), F32),
            jax.ShapeDtypeStruct((SUB, D), F32),
            jax.ShapeDtypeStruct((SUB,), F32),
        ),
        in_specs=[vm, vm, vm],
        out_specs=(hbm, hbm, vm),
        scratch_shapes=[dma((2,))],
        compiler_params=pltpu.CompilerParams(vmem_limit_bytes=32 * 1024 * 1024),
        name="ship",
    )(label_grad, doc_grad, loss)
    return loss, doc_grad, label_grad


def solution(mesh):
    return jax.shard_map(
        shards,
        mesh=mesh,
        in_specs=(
            P("dp", None),
            P(("dp", "label"), None),
            P(("dp", "label"), None, None),
            P(("dp", "label"), None),
        ),
        out_specs=(P(("dp", "label")), P(("dp", "label"), None), P(("dp", "label"), None)),
        check_vma=False,
    )
```

```python
import functools
import math

import jax
import jax.numpy as jnp
from jax import lax
from jax.experimental import pallas as pl
from jax.experimental.pallas import tpu as pltpu
from jax.sharding import PartitionSpec as P

MESH = pl.DeviceIdType.MESH
F32 = jnp.float32
BF16 = jnp.bfloat16

NX, NYH, NC, NZ, NYL = 4, 2, 2, 4, 2
DP, LB = 16, 8
DEV = DP * LB
SUB = 16
BLK = SUB * LB
GRP = 2 * BLK
DOCS = DP * BLK
D = 768
ROWS = 2048
COLS = 17
TW = 384
SLOTS = 8
BIG = float(2 ** 23)
FG = 256
C = 4.0 / math.sqrt(D)
TILE = 256

NT = (((1,), (1,)), ((), ()))


def mm(a, b):
    return jnp.dot(a, b, preferred_element_type=F32)


def split(v):
    hi = v.astype(BF16).astype(F32)
    return hi, v - hi


def kernel(
    docs_hbm, labels_hbm, owner_hbm, row_hbm,
    lg_ref, dg_ref, loss_ref,
    lab, dall, labt, e_ref, u_ref, rc_ref, w_ref, v1_ref, v2_ref, q0_ref, q1_ref, q2_ref,
    owner_ref, row_ref, ids_ref, idl_ref, idg_ref, keys_ref, skeys_ref, rowt_ref, lrow_ref, slr_ref, grow_ref,
    st_ref, sr_ref, sv_ref, sst_ref, lt_ref,
    ts_ref, tr_ref, tu_ref, tv_ref, ca_ref, scale_ref, tmp_ref, coef_ref, coeft_ref,
    lab_sem, own_sem, in_sem, doc_send, doc_recv, sib_send, sib_recv,
    idl_send, idl_recv, idg_send, idg_recv,
    s1_send, s1_recv, s2_send, s2_recv, sst_sem, lr_sem,
    t1_send, t1_recv, t2_send, t2_recv, t3_send, t3_recv,
    rc_send, rc_recv, rs_send, rs_recv,
):
    dp = lax.axis_index("dp")
    lb = lax.axis_index("label")
    x, yh, co = dp // 4, (dp // 2) % 2, dp % 2
    z, yl = lb // 2, lb % 2
    y = yh * 2 + yl
    me = dp * LB + lb

    def dev(x_, yh_, co_, z_, yl_):
        return ((x_ * 2 + yh_) * 2 + co_, z_ * 2 + yl_)

    sib = dev(x, yh, 1 - co, z, yl)
    ypart = dev(x, 1 - yh, co, z, 1 - yl)

    def on_axis(axis, pos):
        if axis == 0:
            return dev(pos, yh, co, z, yl)
        if axis == 1:
            return dev(x, pos // 2, co, z, pos % 2)
        return dev(x, yh, co, pos, yl)

    xup, xdown = on_axis(0, (x + 1) % NX), on_axis(0, (x + 3) % NX)

    def mate(i):
        q = (dp + i) % DP
        return q, (q, z * 2 + jnp.where((q // 2) % 2 == yh, yl, 1 - yl))

    def all_in(ref, sem):
        pltpu.make_async_remote_copy(
            src_ref=ref, dst_ref=ref, send_sem=sem, recv_sem=sem, device_id=sib, device_id_type=MESH
        ).wait_recv()

    def all_out(ref, sem):
        pltpu.make_async_remote_copy(
            src_ref=ref, dst_ref=ref, send_sem=sem, recv_sem=sem, device_id=sib, device_id_type=MESH
        ).wait_send()

    def remote(src, dst, ssem, rsem, to):
        return pltpu.make_async_remote_copy(
            src_ref=src, dst_ref=dst, send_sem=ssem, recv_sem=rsem, device_id=to, device_id_type=MESH
        )

    def each(lo, hi, fn):
        def body(i, carry):
            fn(i)
            return carry

        lax.fori_loop(lo, hi, body, 0)

    def at(start, size):
        return pl.ds(pl.multiple_of(start, size), size)

    barrier = pltpu.get_barrier_semaphore()
    each(1, DP, lambda i: pl.semaphore_signal(barrier, inc=1, device_id=mate(i)[1], device_id_type=MESH))
    each(1, LB, lambda i: pl.semaphore_signal(barrier, inc=1, device_id=(dp, (lb + i) % LB), device_id_type=MESH))
    pl.semaphore_signal(barrier, inc=1, device_id=dev(x, 1 - yh, co, z, yl), device_id_type=MESH)
    lab_copy = pltpu.make_async_copy(labels_hbm, lab, lab_sem)
    lab_copy.start()
    g_own = x * 2 + yh

    def doc_slot(group, core):
        return dall.at[group * 2 + core]

    own_copy = pltpu.make_async_copy(docs_hbm, doc_slot(g_own, co), own_sem)
    own_copy.start()
    id_copies = [
        pltpu.make_async_copy(owner_hbm, owner_ref, in_sem.at[0]),
        pltpu.make_async_copy(row_hbm, row_ref, in_sem.at[1]),
    ]
    for copy in id_copies:
        copy.start()
    pl.semaphore_wait(barrier, DP - 1 + LB - 1 + 1)

    def sib_copy(k, src, group):
        return remote(src, doc_slot(group, co), sib_send, sib_recv.at[k], sib)

    own_copy.wait()
    sib_copy(0, doc_slot(g_own, co), g_own).start()
    def some(ref, start, size):
        return ref.at[start:start + size, :]

    def half_copy(h, rsem, to):
        block = some(doc_slot(g_own, co), h * 64, 64)
        return remote(block, block, doc_send, doc_recv.at[rsem], to)

    remote(doc_slot(g_own, co), doc_slot(g_own, co), doc_send, doc_recv.at[3], ypart).start()
    half_copy(0, 1, xdown).start()
    half_copy(1, 2, xup).start()

    def place(k):
        dx = jnp.where((k == 1) | (k == 5), 1, jnp.where((k == 2) | (k == 6), 3, jnp.where((k == 4) | (k == 7), 2, 0)))
        dy = jnp.where((k == 3) | (k >= 5), 1, 0)
        return ((x + dx) % NX) * 2 + (yh + dy) % 2

    def relay_up(slot):
        return remote(slot, slot, doc_send, doc_recv.at[6], xup)

    def relay_down(slot):
        return remote(slot, slot, doc_send, doc_recv.at[5], xdown)

    def relay_far(slot, h):
        block = some(slot, h * 64, 64)
        return remote(block, block, doc_send, doc_recv.at[(4, 9)[h]], xup if h else xdown)

    def relay_y(slot):
        return remote(slot, slot, doc_send, doc_recv.at[7], ypart)

    def part_in(k, start, size, rsem):
        block = some(doc_slot(place(k), co), start, size)
        remote(block, block, doc_send, doc_recv.at[rsem], ypart).wait_recv()

    def far():
        part_in(1, 0, 64, 1)
        part_in(2, 64, 64, 2)
        for h in range(2):
            relay_far(doc_slot(place(1 + h), co), h).start()

    def take(k):
        slot = doc_slot(place(k), co)
        if k == 1:
            part_in(1, 64, 64, 12)
        elif k == 2:
            part_in(2, 0, 64, 8)
        elif k == 4:
            part_in(4, 0, 64, 4)
            part_in(4, 64, 64, 9)
            relay_y(slot).start()
        else:
            remote(slot, slot, doc_send, doc_recv.at[k], ypart).wait_recv()
        sib_copy(k, slot, place(k)).start()

    for copy in id_copies:
        copy.wait()
    named = (owner_ref[:, 0, :] * ROWS + row_ref[...]).astype(F32)
    high = jnp.floor(named * (1.0 / 4096.0))
    rest = named - 4096.0 * high
    mid = jnp.floor(rest * (1.0 / 64.0))
    digits = jnp.concatenate([high, mid, rest - 64.0 * mid], axis=0).astype(BF16)
    lane = lax.broadcasted_iota(jnp.int32, (COLS, TW), 1)
    spread = mm(digits, jnp.where((lane // SUB + 1) % COLS == lax.broadcasted_iota(jnp.int32, (COLS, TW), 0), 1.0, 0.0).astype(BF16))
    spread = 4096.0 * spread[0:SUB] + 64.0 * spread[SUB:2 * SUB] + spread[2 * SUB:3 * SUB]
    lane = lax.broadcasted_iota(jnp.int32, (SUB, TW), 1)
    own = jnp.sum(jnp.where(lane % SUB == lax.broadcasted_iota(jnp.int32, (SUB, TW), 0), spread, 0.0), axis=0, keepdims=True)
    own = jnp.where(lane[0:1] < SUB * COLS, own, -1.0)
    ids_ref[...] = jnp.where(lax.broadcasted_iota(jnp.int32, (LB, TW), 0) == lb, own, 0.0)
    def idl_copy(i):
        return remote(ids_ref, idl_ref.at[lb], idl_send, idl_recv, (dp, (lb + i) % LB))

    each(1, LB, lambda i: idl_copy(i).start())

    ts_ref[...] = jnp.zeros_like(ts_ref)
    st_ref[...] = jnp.zeros_like(st_ref)
    lab_copy.wait()

    def turn(i):
        labt[:, at(i * 256, 256)] = lab[at(i * 256, 256), :].T

    each(0, ROWS // 256, turn)
    half_copy(1, 12, xdown).start()
    half_copy(0, 8, xup).start()


    def raw_cols(p):
        return slice(p * GRP, (p + 1) * GRP)

    CH = 256

    def exp_rows(p, c, top, cols):
        s = lg_ref[c * CH:(c + 1) * CH, raw_cols(p)]
        e = jnp.exp((s - top) * C)
        e_ref[c * CH:(c + 1) * CH, cols] = e
        return jnp.sum(e, axis=0, keepdims=True)

    def keep(g, top, total):
        for h in range(2):
            st_ref[0, pl.ds(g * 2 + h, 1), :] = (top * C)[:, h * BLK:(h + 1) * BLK]
            st_ref[1, pl.ds(g * 2 + h, 1), :] = total[:, h * BLK:(h + 1) * BLK]

    def wait_sib(k):
        other = doc_slot(place(k), 1 - co)
        remote(other, other, sib_send, sib_recv.at[k], sib).wait_recv()

    def score_step(k, p, old_top):
        g = place(k)

        @pl.when(k < 5)
        def _():
            wait_sib(k)

        block = dall[pl.ds(g * 2, 2)].reshape(GRP, D)
        old = place((k + 7) % 8)
        cols = at(old * GRP, GRP)
        top, total = None, 0.0
        for c in range(ROWS // CH):
            s = lax.dot_general(lab[c * CH:(c + 1) * CH, :], block, NT, preferred_element_type=F32)
            lg_ref[c * CH:(c + 1) * CH, raw_cols(p)] = s
            high = jnp.max(s, axis=0, keepdims=True)
            top = high if top is None else jnp.maximum(top, high)
            total = total + exp_rows(1 - p, c, old_top, cols)
        keep(old, old_top, total)
        return top

    def ids_out():
        all_in(idl_ref.at[1:LB], idl_recv)
        idl_ref[lb] = ids_ref[...]
        acc = idl_ref[0]
        for q in range(1, LB):
            acc = acc + idl_ref[q]
        idg_ref[dp] = acc
        each(1, DP, lambda i: idg_copy(i).start())

    def idg_copy(i):
        return remote(idg_ref.at[dp], idg_ref.at[dp], idg_send, idg_recv, mate(i)[1])

    lane_8 = lax.broadcasted_iota(jnp.int32, (LB, 128), 1).astype(F32)
    lane_t = [lane_8 + 128.0 * v for v in range(3)]
    base = (me * ROWS).astype(F32)

    def find():
        all_in(idg_ref.at[1:DP], idg_recv)
        rel = idg_ref[...].reshape(DEV, TW) - base
        lanes = lax.broadcasted_iota(jnp.int32, (DEV, TW), 1).astype(F32)
        key = jnp.where((rel >= 0.0) & (rel < float(ROWS)), lanes * float(ROWS) + rel, BIG)
        for k in range(SLOTS):
            low = jnp.min(key, axis=1, keepdims=True)
            for b in range(DP):
                keys_ref[b % 2, b // 2, k * 8:k * 8 + 8, :] = jnp.broadcast_to(low[b * 8:b * 8 + 8], (8, 128))
            key = jnp.where(key == low, BIG, key)

    def parts_of(key):
        t = jnp.floor(key * (1.0 / ROWS))
        row = jnp.where(key < BIG, key - t * float(ROWS), -1.0)
        return t, row

    def fetch(c):
        lane_rows = lax.broadcasted_iota(jnp.int32, (256, ROWS), 1).astype(F32)
        out = []
        for h in range(2):
            _, row = parts_of(keys_ref[c, h * 4:h * 4 + 4].reshape(256, 128)[:, 0:1])
            pick = jnp.where(lane_rows == row, 1.0, 0.0).astype(BF16)
            out.append(mm(pick, lab[...]).astype(BF16).reshape(4, 64, D))
        for h in range(2):
            lrow_ref[c, h * 4:h * 4 + 4] = out[h]

    def named_copy():
        return remote(lrow_ref.at[1 - co], slr_ref, lr_sem.at[0], lr_sem.at[1], sib)

    def keys_copy():
        return remote(keys_ref.at[1 - co], skeys_ref, lr_sem.at[2], lr_sem.at[3], sib)

    def flip(i):
        _, row = parts_of(keys_ref[i // 4, pl.ds((i % 4) * 2, 2)].reshape(128, 128))
        rowt_ref[:, at(i * 128, 128)] = row.T[0:8, :]

    lane_doc = lax.broadcasted_iota(jnp.int32, (64, BLK), 1).astype(F32)
    slot_l = (lax.broadcasted_iota(jnp.int32, (64, BLK), 0) % 8).astype(F32)

    def doc_pick(key):
        t, _ = parts_of(key)
        d = t - 16.0 * jnp.floor(t * (1.0 / 16.0)) + 16.0 * slot_l
        return lane_doc == jnp.where(key < BIG, d, -1.0)

    def target(i):
        out = []
        for q in range(4):
            c, j = q % 2, place(i * 2 + q // 2)
            b = j * 2 + c
            key = keys_ref[c, j]
            t, _ = parts_of(key)
            found = mm(jnp.where(doc_pick(key), 1.0, 0.0).astype(BF16), dall[b])
            score = C * jnp.sum(found * lrow_ref[c, j].astype(F32), axis=1, keepdims=True)
            slots = jnp.full((LB, 128), -1.0, F32)
            for k in range(SLOTS):
                slots = jnp.where(lane_8 == float(k), score[k * 8:k * 8 + 8], slots)
                slots = jnp.where(lane_8 == float(SLOTS + k), t[k * 8:k * 8 + 8], slots)
            out.append((b, c, j, found.astype(BF16), slots))
        for b, c, j, found, slots in out:
            grow_ref[c, j] = found
            ts_ref[b] = slots

    def t1_copy(i):
        q, to = mate(i)
        return remote(ts_ref.at[q], tr_ref.at[dp], t1_send, t1_recv, to)


    def s1_copy(i):
        return remote(st_ref.at[1], sr_ref.at[lb], s1_send, s1_recv, (dp, (lb + i) % LB))

    def s2_copy(i):
        return remote(sv_ref.at[dp], sv_ref.at[dp], s2_send, s2_recv, mate(i)[1])

    def sst_copy():
        return remote(st_ref.at[0], sst_ref, sst_sem.at[0], sst_sem.at[1], sib)

    def merge(count, ref):
        tops = [ref[q] for q in range(count)]
        top = functools.reduce(jnp.maximum, tops)
        total = 0.0
        for q in range(count):
            total = total + jnp.exp(tops[q] - top)
        return top + jnp.log(total)

    def stats_on():
        all_in(sr_ref.at[1:LB], s1_recv)
        sr_ref[lb] = st_ref[1]
        sv_ref[dp] = merge(LB, sr_ref)
        each(1, DP, lambda i: s2_copy(i).start())

    def totals():
        all_in(sv_ref.at[1:DP], s2_recv)
        lt_ref[...] = merge(DP, sv_ref)

    def core_copy(j):
        return remote(u_ref.at[at((j * 2 + 1 - co) * BLK, BLK), :], rc_ref.at[j], rc_send, rc_recv, sib)

    def doc_part(g):
        part = mm(labt[...], e_ref[:, at(g * GRP, GRP)].astype(BF16))
        u_ref[at(g * GRP, GRP), :] = part.T

    def exp_group(p, g, top):
        total = 0.0
        for c in range(ROWS // CH):
            total = total + exp_rows(p, c, top, at(g * GRP, GRP))
        keep(g, top, total)

    def score_pair(i, top):
        @pl.when(i == 1)
        def _():
            slot = doc_slot(place(3), co)
            relay_up(slot).start()
            relay_down(slot).start()

        top = score_step(i * 2, 0, top)

        @pl.when(i == 0)
        def _():
            exp_group(0, g_own, top)
            doc_part(g_own)
            core_copy(g_own).start()
            far()
            ids_out()
            for k in (1, 2, 3):
                take(k)

        @pl.when(i == 2)
        def _():
            find()
            fetch(0)
            take(5)
            take(6)
            fetch(1)
            take(7)
            wait_sib(5)

            def targets(i):
                @pl.when(i == 3)
                def _():
                    wait_sib(6)
                    wait_sib(7)

                target(i)

            each(0, 4, targets)
            each(1, DP, lambda i: t1_copy(i).start())
            each(0, 8, flip)

        top = score_step(i * 2 + 1, 1, top)

        @pl.when(i == 1)
        def _():
            take(4)

        return top

    lg_ref[:, raw_cols(1)] = jnp.zeros((ROWS, GRP), F32)
    top = lax.fori_loop(0, 4, score_pair, jnp.zeros((1, GRP), F32))
    exp_group(1, place(7), top)

    st_ref[1] = st_ref[0] + jnp.log(st_ref[1])
    each(1, LB, lambda i: s1_copy(i).start())
    sst_copy().start()

    def t2_copy(i):
        return remote(tu_ref, tv_ref.at[lb], t2_send, t2_recv, (dp, (lb + i) % LB))

    def t3_copy(i):
        return remote(ca_ref.at[dp, :, 0:256], ca_ref.at[dp, :, 0:256], t3_send, t3_recv, mate(i)[1])

    def targets_on():
        all_in(tr_ref.at[1:DP], t1_recv)
        tr_ref[dp] = ts_ref[dp]
        acc = [jnp.zeros((LB, 128), F32)] * 3
        for q in range(DP):
            slots = tr_ref[q]
            for k in range(SLOTS):
                score, t = slots[:, k:k + 1], slots[:, SLOTS + k:SLOTS + k + 1]
                for v in range(3):
                    acc[v] = acc[v] + jnp.where(lane_t[v] == t, score, 0.0)
        for v in range(3):
            tu_ref[:, v * 128:(v + 1) * 128] = acc[v]
        each(1, LB, lambda i: t2_copy(i).start())

    def spread_16(value):
        for shift in (16, 32, 64):
            value = value + pltpu.roll(value, shift, 1)
        return value

    def positives():
        for q in range(DP):
            ca_ref[q, :, 256:384] = -1.0 - spread_16(ca_ref[q, :, 0:128] + ca_ref[q, :, 128:256])

    def coefficients_on():
        all_in(tv_ref.at[1:LB], t2_recv)
        tv_ref[lb] = tu_ref[...]
        acc = tv_ref[0]
        for q in range(1, LB):
            acc = acc + tv_ref[q]
        lane = lax.broadcasted_iota(jnp.int32, (LB, 128), 1)
        pos = spread_16(jnp.where(lane < SUB, acc[:, 256:384], 0.0))
        soft = jnp.zeros((LB, 128), F32)
        for v in range(2):
            gap = acc[:, v * 128:(v + 1) * 128] - pos + 1.0
            small = jnp.exp(-jnp.abs(gap))
            soft = soft + jnp.maximum(gap, 0.0) + jnp.log(1.0 + small)
            ca_ref[dp, :, v * 128:(v + 1) * 128] = jnp.where(gap >= 0.0, 1.0, small) / (1.0 + small) * (1.0 / 16.0)
        tmp_ref[...] = spread_16(soft) * (1.0 / 16.0) - pos
        each(1, DP, lambda i: t3_copy(i).start())

    targets_on()
    named_copy().start()
    keys_copy().start()

    def doc_mm(k):
        doc_part(place(k))

        core_copy(place(k)).start()

        @pl.when(k == 4)
        def _():
            stats_on()
            coefficients_on()

    each(1, 8, doc_mm)
    totals()
    all_in(rc_ref, rc_recv)
    sst_copy().wait_recv()

    def column(row):
        return jnp.concatenate([jnp.broadcast_to(row, (BLK, BLK)).T] * (D // BLK), axis=1)

    def merge_cores(i):
        out = []
        for q in range(4):
            j = i * 4 + q
            b = j * 2 + co
            log_total = lt_ref[pl.ds(b, 1), :]
            col = column(jnp.exp(st_ref[0, pl.ds(b, 1), :] - log_total))
            scol = column(jnp.exp(sst_ref[pl.ds(b, 1), :] - log_total))
            out.append((b, u_ref[at(b * BLK, BLK), :] * col + rc_ref[j] * scol))
        for b, value in out:
            u_ref[at(b * BLK, BLK), :] = value

    each(0, 2, merge_cores)
    shifted = pltpu.roll(jnp.broadcast_to(lt_ref[pl.ds(dp, 1), :], (8, BLK)), (BLK - lb * SUB) % BLK, 1)
    loss_ref[...] = tmp_ref[pl.ds(lb, 1), :] + shifted[0:1, :]

    all_in(ca_ref.at[1:DP, :, 0:256], t3_recv)
    positives()

    def slot_coef(b, t):
        out = []
        for k in range(SLOTS):
            hit = [jnp.where(lane_t[v] == t[k * 8:k * 8 + 8], ca_ref[b, :, v * 128:(v + 1) * 128], 0.0) for v in range(3)]
            out.append(jnp.sum(hit[0] + hit[1] + hit[2], axis=1, keepdims=True))
        return jnp.concatenate(out, axis=0)

    def scaled_pick(key, coef):
        hi, lo = split(coef)
        pick = doc_pick(key)
        return [jnp.where(pick, hi, 0.0), jnp.where(pick, lo, 0.0)]

    def finish(i):
        out = []
        for q in range(4):
            j = i * 4 + q
            b = j * 2 + co
            key, skey = keys_ref[co, j], skeys_ref[j]
            coef, scoef = slot_coef(b, parts_of(key)[0]), slot_coef(b, parts_of(skey)[0])
            pick = jnp.concatenate(scaled_pick(key, coef) + scaled_pick(skey, scoef), axis=0).T.astype(BF16)
            named, snamed = lrow_ref[co, j], slr_ref[j]
            hard = mm(pick, jnp.concatenate([named, named, snamed, snamed], axis=0))
            out.append((j, coef, C * (u_ref[at(b * BLK, BLK), :] + hard)))
        for j, coef, value in out:
            coef_ref[co, j] = jnp.broadcast_to(coef, (64, 128))
            xx, hh = j // 2, j % 2
            for zz in range(NZ):
                for ll in range(NYL):
                    off = (zz * NYL + ll) * SUB
                    u = value[off:off + SUB]
                    yy = hh * 2 + ll
                    w_ref[0, xx, yy, zz] = u[:, 0:FG]
                    w_ref[1, yy, zz, xx] = u[:, FG:2 * FG]
                    w_ref[2, zz, xx, yy] = u[:, 2 * FG:3 * FG]

    named_copy().wait_recv()
    keys_copy().wait_recv()
    each(0, 2, finish)

    spot = (x, y, z)
    def ring_msg(f, m, p=None):
        h = spot[f]
        up, down = on_axis(f, (h + 1) % 4), on_axis(f, (h + 3) % 4)

        def part(block, which):
            if p is None:
                return w_ref.at[f, block % 4, which * 2:which * 2 + 2]
            return w_ref.at[f, block % 4, which * 2 + p]

        box = q0_ref.at[f, m] if p is None else q0_ref.at[f, m, p]
        if m >= 4:
            source = q0_ref.at[f, m - 4, p]
        else:
            source = (part(h + 2, 0), part(h + 2, 1), part(h + 3, 1), part(h + 1, 0))[m]
        to = (down, up, down, up, down, up)[m]
        return remote(source, box, rs_send.at[0], rs_recv.at[2 if m >= 2 else p], to)

    def ring_start(msgs, p=None):
        for m in msgs:
            for f in range(3):
                ring_msg(f, m, p).start()

    def ring_relay(p):
        all_in(q0_ref.at[:, 0:2, p], rs_recv.at[p])
        for f in range(3):
            h = spot[f]
            for m in range(2):
                block = (h + 3) % 4 if m == 0 else (h + 1) % 4
                q0_ref[f, m, p] = q0_ref[f, m, p] + w_ref[f, block, m * 2 + p]
                ring_msg(f, 4 + m, p).start()

    def ring_done():
        all_in(q0_ref.at[:, 2:6], rs_recv.at[2])
        for f in range(3):
            h = spot[f]
            v1_ref[f, 0:2] = w_ref[f, h, 0:2] + q0_ref[f, 4] + q0_ref[f, 3]
            v1_ref[f, 2:4] = w_ref[f, h, 2:4] + q0_ref[f, 2] + q0_ref[f, 5]

    bufs = {1: (v1_ref, q1_ref), 2: (v2_ref, q2_ref)}

    def straight(step, f, i):
        axis = (f + step) % 3
        to = (spot[axis] + i) % 4
        src, box = bufs[step]
        return remote(src.at[f, to], box.at[f, i - 1], rs_send.at[step], rs_recv.at[step + 2], on_axis(axis, to))

    def straight_start(step):
        for i in (2, 1, 3):
            for f in range(3):
                straight(step, f, i).start()

    def straight_done(step):
        src, box = bufs[step]
        all_in(box, rs_recv.at[step + 2])
        return [src[f, spot[(f + step) % 3]] + box[f, 0] + box[f, 1] + box[f, 2] for f in range(3)]

    ring_start((0, 1), 0)

    def coef_rows(i):
        hi, lo = split(coef_ref[i // 4, pl.ds((i % 4) * 2, 2)].reshape(128, 128).T[0:8, :])
        coeft_ref[0, :, at(i * 128, 128)] = hi
        coeft_ref[1, :, at(i * 128, 128)] = lo

    def other_coef(i):
        out = []
        for q in range(4):
            j = i * 4 + q
            out.append((j, slot_coef(j * 2 + 1 - co, parts_of(keys_ref[1 - co, j])[0])))
        for j, coef in out:
            coef_ref[1 - co, j] = jnp.broadcast_to(coef, (64, 128))

    ring_start((0, 1), 1)
    each(0, 2, other_coef)
    each(0, 8, coef_rows)
    for b in range(DP):
        scale = jnp.exp(st_ref[0, b:b + 1, :] - lt_ref[b:b + 1, :])
        scale_ref[:, b * BLK:(b + 1) * BLK] = jnp.broadcast_to(scale, (8, BLK))

    def label_mm(r):
        rows = at(r * TILE, TILE)
        probs = (e_ref[rows, :] * scale_ref[0:1, :]).astype(BF16)
        sub_rows = (lax.broadcasted_iota(jnp.int32, (TILE, DEV * SLOTS), 0) + r * TILE).astype(F32)
        pick = sub_rows == rowt_ref[0:1, :]
        named = grow_ref[...].reshape(DEV * SLOTS, D)
        value = mm(probs, dall[...].reshape(DOCS, D))
        for p in range(2):
            value = value + mm(jnp.where(pick, coeft_ref[p, 0:1, :], 0.0).astype(BF16), named)
        lg_ref[rows, :] = C * value

        @pl.when(r == 0)
        def _():
            ring_start((2, 3))

        @pl.when(r == 1)
        def _():
            ring_relay(0)
            ring_relay(1)

        @pl.when(r == 4)
        def _():
            ring_done()
            straight_start(1)

        @pl.when(r == 6)
        def _():
            for f, value in enumerate(straight_done(1)):
                v2_ref[f] = value
            straight_start(2)

    each(0, ROWS // TILE, label_mm)

    for f, value in enumerate(straight_done(2)):
        dg_ref[:, f * FG:(f + 1) * FG] = value

    all_out(dall.at[0:7], doc_send)
    all_out(dall.at[0:8], sib_send)
    all_out(rc_ref, rc_send)
    for copy in (sst_copy(), named_copy(), keys_copy()):
        copy.wait_send()
    all_out(idl_ref.at[1:LB], idl_send)
    all_out(idg_ref.at[1:DP], idg_send)
    all_out(sr_ref.at[1:LB], s1_send)
    all_out(sv_ref.at[1:DP], s2_send)
    all_out(tr_ref.at[1:DP], t1_send)
    all_out(tv_ref.at[1:LB], t2_send)
    all_out(ca_ref.at[1:DP, :, 0:256], t3_send)
    all_out(q0_ref, rs_send.at[0])
    all_out(q1_ref, rs_send.at[1])
    all_out(q2_ref, rs_send.at[2])


def ship(lg_in, dg_in, loss_in, lg_out, dg_out, loss_out, sems):
    copies = [pltpu.make_async_copy(lg_in, lg_out, sems.at[0]), pltpu.make_async_copy(dg_in, dg_out, sems.at[1])]
    for copy in copies:
        copy.start()
    loss_out[...] = loss_in[0, 0:SUB]
    for copy in copies:
        copy.wait()


def shards(documents, labels, target_owner, target_row):
    vm = pl.BlockSpec(memory_space=pltpu.VMEM)
    hbm = pl.BlockSpec(memory_space=pl.ANY)
    dma = pltpu.SemaphoreType.DMA
    slots = DEV * SLOTS
    label_grad, doc_grad, loss = pl.pallas_call(
        kernel,
        out_shape=(
            pltpu.VMEM((ROWS, D), F32),
            pltpu.VMEM((SUB, D), F32),
            pltpu.VMEM((1, 128), F32),
        ),
        in_specs=[hbm, hbm, hbm, hbm],
        out_specs=(vm, vm, vm),
        scratch_shapes=[
            pltpu.VMEM((ROWS, D), BF16),
            pltpu.VMEM((DP, BLK, D), BF16),
            pltpu.VMEM((D, ROWS), BF16),
            pltpu.VMEM((ROWS, DOCS), F32),
            pltpu.VMEM((DOCS, D), F32),
            pltpu.VMEM((8, BLK, D), F32),
            pltpu.VMEM((3, 4, 4, 4, SUB, FG), F32),
            pltpu.VMEM((3, 4, 4, SUB, FG), F32),
            pltpu.VMEM((3, 4, SUB, FG), F32),
            pltpu.VMEM((3, 6, 2, 4, SUB, FG), F32),
            pltpu.VMEM((3, 3, 4, SUB, FG), F32),
            pltpu.VMEM((3, 3, SUB, FG), F32),
            pltpu.VMEM((SUB, 1, COLS), jnp.int32),
            pltpu.VMEM((SUB, COLS), jnp.int32),
            pltpu.VMEM((LB, TW), F32),
            pltpu.VMEM((LB, LB, TW), F32),
            pltpu.VMEM((DP, LB, TW), F32),
            pltpu.VMEM((2, 8, 64, 128), F32),
            pltpu.VMEM((8, 64, 128), F32),
            pltpu.VMEM((8, slots), F32),
            pltpu.VMEM((2, 8, 64, D), BF16),
            pltpu.VMEM((8, 64, D), BF16),
            pltpu.VMEM((2, 8, 64, D), BF16),
            pltpu.VMEM((2, DP, BLK), F32),
            pltpu.VMEM((LB, DP, BLK), F32),
            pltpu.VMEM((DP, DP, BLK), F32),
            pltpu.VMEM((DP, BLK), F32),
            pltpu.VMEM((DP, BLK), F32),
            pltpu.VMEM((DP, LB, 128), F32),
            pltpu.VMEM((DP, LB, 128), F32),
            pltpu.VMEM((LB, TW), F32),
            pltpu.VMEM((LB, LB, TW), F32),
            pltpu.VMEM((DP, LB, TW), F32),
            pltpu.VMEM((8, DOCS), F32),
            pltpu.VMEM((LB, 128), F32),
            pltpu.VMEM((2, 8, 64, 128), F32),
            pltpu.VMEM((2, 8, slots), F32),
            dma, dma, dma((2,)), dma, dma((13,)), dma, dma((8,)),
            dma, dma, dma, dma,
            dma, dma, dma, dma, dma((2,)), dma((4,)),
            dma, dma, dma, dma, dma, dma,
            dma, dma, dma((3,)), dma((5,)),
        ],
        compiler_params=pltpu.CompilerParams(
            collective_id=0, has_side_effects=True, vmem_limit_bytes=56 * 1024 * 1024
        ),
        cost_estimate=pl.CostEstimate(
            flops=8 * ROWS * DOCS * D, bytes_accessed=10 * ROWS * D, transcendentals=ROWS * DOCS
        ),
        name="head",
    )(documents, labels, target_owner.transpose(0, 2, 1), target_row)
    label_grad, doc_grad, loss = pl.pallas_call(
        ship,
        out_shape=(
            jax.ShapeDtypeStruct((ROWS, D), F32),
            jax.ShapeDtypeStruct((SUB, D), F32),
            jax.ShapeDtypeStruct((SUB,), F32),
        ),
        in_specs=[vm, vm, vm],
        out_specs=(hbm, hbm, vm),
        scratch_shapes=[dma((2,))],
        compiler_params=pltpu.CompilerParams(vmem_limit_bytes=32 * 1024 * 1024),
        name="ship",
    )(label_grad, doc_grad, loss)
    return loss, doc_grad, label_grad


def solution(mesh):
    return jax.shard_map(
        shards,
        mesh=mesh,
        in_specs=(
            P("dp", None),
            P(("dp", "label"), None),
            P(("dp", "label"), None, None),
            P(("dp", "label"), None),
        ),
        out_specs=(P(("dp", "label")), P(("dp", "label"), None), P(("dp", "label"), None)),
        check_vma=False,
    )
```

```python
import functools
import math

import jax
import jax.numpy as jnp
from jax import lax
from jax.experimental import pallas as pl
from jax.experimental.pallas import tpu as pltpu
from jax.sharding import PartitionSpec as P

MESH = pl.DeviceIdType.MESH
F32 = jnp.float32
BF16 = jnp.bfloat16

NX, NYH, NC, NZ, NYL = 4, 2, 2, 4, 2
DP, LB = 16, 8
DEV = DP * LB
SUB = 16
BLK = SUB * LB
GRP = 2 * BLK
DOCS = DP * BLK
D = 768
ROWS = 2048
COLS = 17
TW = 384
SLOTS = 8
BIG = float(2 ** 23)
FG = 256
C = 4.0 / math.sqrt(D)
TILE = 256

NT = (((1,), (1,)), ((), ()))


def mm(a, b):
    return jnp.dot(a, b, preferred_element_type=F32)


def split(v):
    hi = v.astype(BF16).astype(F32)
    return hi, v - hi


def kernel(
    docs_hbm, labels_hbm, owner_hbm, row_hbm,
    lg_ref, dg_ref, loss_ref,
    lab, dall, labt, e_ref, u_ref, rc_ref, w_ref, v1_ref, v2_ref, q0_ref, q1_ref, q2_ref,
    owner_ref, row_ref, ids_ref, idl_ref, idg_ref, keys_ref, skeys_ref, rowt_ref, lrow_ref, slr_ref, grow_ref,
    st_ref, sr_ref, sv_ref, sst_ref, lt_ref,
    ts_ref, tr_ref, tu_ref, tv_ref, ca_ref, scale_ref, tmp_ref, coef_ref, coeft_ref,
    lab_sem, own_sem, in_sem, doc_send, doc_recv, sib_send, sib_recv,
    idl_send, idl_recv, idg_send, idg_recv,
    s1_send, s1_recv, s2_send, s2_recv, sst_sem, lr_sem,
    t1_send, t1_recv, t2_send, t2_recv, t3_send, t3_recv,
    rc_send, rc_recv, rs_send, rs_recv,
):
    dp = lax.axis_index("dp")
    lb = lax.axis_index("label")
    x, yh, co = dp // 4, (dp // 2) % 2, dp % 2
    z, yl = lb // 2, lb % 2
    y = yh * 2 + yl
    me = dp * LB + lb

    def dev(x_, yh_, co_, z_, yl_):
        return ((x_ * 2 + yh_) * 2 + co_, z_ * 2 + yl_)

    sib = dev(x, yh, 1 - co, z, yl)
    ypart = dev(x, 1 - yh, co, z, 1 - yl)

    def on_axis(axis, pos):
        if axis == 0:
            return dev(pos, yh, co, z, yl)
        if axis == 1:
            return dev(x, pos // 2, co, z, pos % 2)
        return dev(x, yh, co, pos, yl)

    xup, xdown = on_axis(0, (x + 1) % NX), on_axis(0, (x + 3) % NX)

    def mate(i):
        q = (dp + i) % DP
        return q, (q, z * 2 + jnp.where((q // 2) % 2 == yh, yl, 1 - yl))

    def all_in(ref, sem):
        pltpu.make_async_remote_copy(
            src_ref=ref, dst_ref=ref, send_sem=sem, recv_sem=sem, device_id=sib, device_id_type=MESH
        ).wait_recv()

    def all_out(ref, sem):
        pltpu.make_async_remote_copy(
            src_ref=ref, dst_ref=ref, send_sem=sem, recv_sem=sem, device_id=sib, device_id_type=MESH
        ).wait_send()

    def remote(src, dst, ssem, rsem, to):
        return pltpu.make_async_remote_copy(
            src_ref=src, dst_ref=dst, send_sem=ssem, recv_sem=rsem, device_id=to, device_id_type=MESH
        )

    def each(lo, hi, fn):
        def body(i, carry):
            fn(i)
            return carry

        lax.fori_loop(lo, hi, body, 0)

    def at(start, size):
        return pl.ds(pl.multiple_of(start, size), size)

    barrier = pltpu.get_barrier_semaphore()
    each(1, DP, lambda i: pl.semaphore_signal(barrier, inc=1, device_id=mate(i)[1], device_id_type=MESH))
    each(1, LB, lambda i: pl.semaphore_signal(barrier, inc=1, device_id=(dp, (lb + i) % LB), device_id_type=MESH))
    pl.semaphore_signal(barrier, inc=1, device_id=dev(x, 1 - yh, co, z, yl), device_id_type=MESH)
    lab_copy = pltpu.make_async_copy(labels_hbm, lab, lab_sem)
    lab_copy.start()
    g_own = x * 2 + yh

    def doc_slot(group, core):
        return dall.at[group * 2 + core]

    own_copy = pltpu.make_async_copy(docs_hbm, doc_slot(g_own, co), own_sem)
    own_copy.start()
    id_copies = [
        pltpu.make_async_copy(owner_hbm, owner_ref, in_sem.at[0]),
        pltpu.make_async_copy(row_hbm, row_ref, in_sem.at[1]),
    ]
    for copy in id_copies:
        copy.start()
    pl.semaphore_wait(barrier, DP - 1 + LB - 1 + 1)

    def sib_copy(k, src, group):
        return remote(src, doc_slot(group, co), sib_send, sib_recv.at[k], sib)

    own_copy.wait()
    sib_copy(0, doc_slot(g_own, co), g_own).start()
    def some(ref, start, size):
        return ref.at[start:start + size, :]

    def half_copy(h, rsem, to):
        block = some(doc_slot(g_own, co), h * 64, 64)
        return remote(block, block, doc_send, doc_recv.at[rsem], to)

    remote(doc_slot(g_own, co), doc_slot(g_own, co), doc_send, doc_recv.at[3], ypart).start()
    half_copy(0, 1, xdown).start()
    half_copy(1, 2, xup).start()

    def place(k):
        dx = jnp.where((k == 1) | (k == 5), 1, jnp.where((k == 2) | (k == 6), 3, jnp.where((k == 4) | (k == 7), 2, 0)))
        dy = jnp.where((k == 3) | (k >= 5), 1, 0)
        return ((x + dx) % NX) * 2 + (yh + dy) % 2

    def relay_up(slot):
        return remote(slot, slot, doc_send, doc_recv.at[6], xup)

    def relay_down(slot):
        return remote(slot, slot, doc_send, doc_recv.at[5], xdown)

    def relay_far(slot, h):
        block = some(slot, h * 64, 64)
        return remote(block, block, doc_send, doc_recv.at[(4, 9)[h]], xup if h else xdown)

    def relay_y(slot):
        return remote(slot, slot, doc_send, doc_recv.at[7], ypart)

    def part_in(k, start, size, rsem):
        block = some(doc_slot(place(k), co), start, size)
        remote(block, block, doc_send, doc_recv.at[rsem], ypart).wait_recv()

    def far():
        part_in(1, 0, 64, 1)
        part_in(2, 64, 64, 2)
        for h in range(2):
            relay_far(doc_slot(place(1 + h), co), h).start()

    def take(k):
        slot = doc_slot(place(k), co)
        if k == 1:
            part_in(1, 64, 64, 12)
        elif k == 2:
            part_in(2, 0, 64, 8)
        elif k == 4:
            part_in(4, 0, 64, 4)
            part_in(4, 64, 64, 9)
            relay_y(slot).start()
        else:
            remote(slot, slot, doc_send, doc_recv.at[k], ypart).wait_recv()
        sib_copy(k, slot, place(k)).start()

    for copy in id_copies:
        copy.wait()
    named = (owner_ref[:, 0, :] * ROWS + row_ref[...]).astype(F32)
    high = jnp.floor(named * (1.0 / 4096.0))
    rest = named - 4096.0 * high
    mid = jnp.floor(rest * (1.0 / 64.0))
    digits = jnp.concatenate([high, mid, rest - 64.0 * mid], axis=0).astype(BF16)
    lane = lax.broadcasted_iota(jnp.int32, (COLS, TW), 1)
    spread = mm(digits, jnp.where((lane // SUB + 1) % COLS == lax.broadcasted_iota(jnp.int32, (COLS, TW), 0), 1.0, 0.0).astype(BF16))
    spread = 4096.0 * spread[0:SUB] + 64.0 * spread[SUB:2 * SUB] + spread[2 * SUB:3 * SUB]
    lane = lax.broadcasted_iota(jnp.int32, (SUB, TW), 1)
    own = jnp.sum(jnp.where(lane % SUB == lax.broadcasted_iota(jnp.int32, (SUB, TW), 0), spread, 0.0), axis=0, keepdims=True)
    own = jnp.where(lane[0:1] < SUB * COLS, own, -1.0)
    ids_ref[...] = jnp.where(lax.broadcasted_iota(jnp.int32, (LB, TW), 0) == lb, own, 0.0)
    def idl_copy(i):
        return remote(ids_ref, idl_ref.at[lb], idl_send, idl_recv, (dp, (lb + i) % LB))

    each(1, LB, lambda i: idl_copy(i).start())

    ts_ref[...] = jnp.zeros_like(ts_ref)
    st_ref[...] = jnp.zeros_like(st_ref)
    lab_copy.wait()

    def turn(i):
        labt[:, at(i * 256, 256)] = lab[at(i * 256, 256), :].T

    each(0, ROWS // 256, turn)
    half_copy(1, 12, xdown).start()
    half_copy(0, 8, xup).start()


    def raw_cols(p):
        return slice(p * GRP, (p + 1) * GRP)

    CH = 256

    def exp_rows(p, c, top, cols):
        s = lg_ref[c * CH:(c + 1) * CH, raw_cols(p)]
        e = jnp.exp((s - top) * C)
        e_ref[c * CH:(c + 1) * CH, cols] = e
        return jnp.sum(e, axis=0, keepdims=True)

    def keep(g, top, total):
        for h in range(2):
            st_ref[0, pl.ds(g * 2 + h, 1), :] = (top * C)[:, h * BLK:(h + 1) * BLK]
            st_ref[1, pl.ds(g * 2 + h, 1), :] = total[:, h * BLK:(h + 1) * BLK]

    def wait_sib(k):
        other = doc_slot(place(k), 1 - co)
        remote(other, other, sib_send, sib_recv.at[k], sib).wait_recv()

    def score_step(k, p, old_top):
        g = place(k)

        @pl.when(k < 5)
        def _():
            wait_sib(k)

        block = dall[pl.ds(g * 2, 2)].reshape(GRP, D)
        old = place((k + 7) % 8)
        cols = at(old * GRP, GRP)
        top, total = None, 0.0
        for c in range(ROWS // CH):
            s = lax.dot_general(lab[c * CH:(c + 1) * CH, :], block, NT, preferred_element_type=F32)
            lg_ref[c * CH:(c + 1) * CH, raw_cols(p)] = s
            high = jnp.max(s, axis=0, keepdims=True)
            top = high if top is None else jnp.maximum(top, high)
            total = total + exp_rows(1 - p, c, old_top, cols)
        keep(old, old_top, total)
        return top

    def ids_out():
        all_in(idl_ref.at[1:LB], idl_recv)
        idl_ref[lb] = ids_ref[...]
        acc = idl_ref[0]
        for q in range(1, LB):
            acc = acc + idl_ref[q]
        idg_ref[dp] = acc
        each(1, DP, lambda i: idg_copy(i).start())

    def idg_copy(i):
        return remote(idg_ref.at[dp], idg_ref.at[dp], idg_send, idg_recv, mate(i)[1])

    lane_8 = lax.broadcasted_iota(jnp.int32, (LB, 128), 1).astype(F32)
    lane_t = [lane_8 + 128.0 * v for v in range(3)]
    base = (me * ROWS).astype(F32)

    def find():
        all_in(idg_ref.at[1:DP], idg_recv)
        rel = idg_ref[...].reshape(DEV, TW) - base
        lanes = lax.broadcasted_iota(jnp.int32, (DEV, TW), 1).astype(F32)
        key = jnp.where((rel >= 0.0) & (rel < float(ROWS)), lanes * float(ROWS) + rel, BIG)
        for k in range(SLOTS):
            low = jnp.min(key, axis=1, keepdims=True)
            for b in range(DP):
                keys_ref[b % 2, b // 2, k * 8:k * 8 + 8, :] = jnp.broadcast_to(low[b * 8:b * 8 + 8], (8, 128))
            key = jnp.where(key == low, BIG, key)

    def parts_of(key):
        t = jnp.floor(key * (1.0 / ROWS))
        row = jnp.where(key < BIG, key - t * float(ROWS), -1.0)
        return t, row

    def fetch(c):
        lane_rows = lax.broadcasted_iota(jnp.int32, (256, ROWS), 1).astype(F32)
        out = []
        for h in range(2):
            _, row = parts_of(keys_ref[c, h * 4:h * 4 + 4].reshape(256, 128)[:, 0:1])
            pick = jnp.where(lane_rows == row, 1.0, 0.0).astype(BF16)
            out.append(mm(pick, lab[...]).astype(BF16).reshape(4, 64, D))
        for h in range(2):
            lrow_ref[c, h * 4:h * 4 + 4] = out[h]

    def named_copy():
        return remote(lrow_ref.at[1 - co], slr_ref, lr_sem.at[0], lr_sem.at[1], sib)

    def keys_copy():
        return remote(keys_ref.at[1 - co], skeys_ref, lr_sem.at[2], lr_sem.at[3], sib)

    def flip(i):
        _, row = parts_of(keys_ref[i // 4, pl.ds((i % 4) * 2, 2)].reshape(128, 128))
        rowt_ref[:, at(i * 128, 128)] = row.T[0:8, :]

    lane_doc = lax.broadcasted_iota(jnp.int32, (64, BLK), 1).astype(F32)
    slot_l = (lax.broadcasted_iota(jnp.int32, (64, BLK), 0) % 8).astype(F32)

    def doc_pick(key):
        t, _ = parts_of(key)
        d = t - 16.0 * jnp.floor(t * (1.0 / 16.0)) + 16.0 * slot_l
        return lane_doc == jnp.where(key < BIG, d, -1.0)

    def target(i):
        out = []
        for q in range(4):
            c, j = q % 2, place(i * 2 + q // 2)
            b = j * 2 + c
            key = keys_ref[c, j]
            t, _ = parts_of(key)
            found = mm(jnp.where(doc_pick(key), 1.0, 0.0).astype(BF16), dall[b])
            score = C * jnp.sum(found * lrow_ref[c, j].astype(F32), axis=1, keepdims=True)
            slots = jnp.full((LB, 128), -1.0, F32)
            for k in range(SLOTS):
                slots = jnp.where(lane_8 == float(k), score[k * 8:k * 8 + 8], slots)
                slots = jnp.where(lane_8 == float(SLOTS + k), t[k * 8:k * 8 + 8], slots)
            out.append((b, c, j, found.astype(BF16), slots))
        for b, c, j, found, slots in out:
            grow_ref[c, j] = found
            ts_ref[b] = slots

    def t1_copy(i):
        q, to = mate(i)
        return remote(ts_ref.at[q], tr_ref.at[dp], t1_send, t1_recv, to)


    def s1_copy(i):
        return remote(st_ref.at[1], sr_ref.at[lb], s1_send, s1_recv, (dp, (lb + i) % LB))

    def s2_copy(i):
        return remote(sv_ref.at[dp], sv_ref.at[dp], s2_send, s2_recv, mate(i)[1])

    def sst_copy():
        return remote(st_ref.at[0], sst_ref, sst_sem.at[0], sst_sem.at[1], sib)

    def merge(count, ref):
        tops = [ref[q] for q in range(count)]
        top = functools.reduce(jnp.maximum, tops)
        total = 0.0
        for q in range(count):
            total = total + jnp.exp(tops[q] - top)
        return top + jnp.log(total)

    def stats_on():
        all_in(sr_ref.at[1:LB], s1_recv)
        sr_ref[lb] = st_ref[1]
        sv_ref[dp] = merge(LB, sr_ref)
        each(1, DP, lambda i: s2_copy(i).start())

    def totals():
        all_in(sv_ref.at[1:DP], s2_recv)
        lt_ref[...] = merge(DP, sv_ref)

    def core_copy(j):
        return remote(u_ref.at[at((j * 2 + 1 - co) * BLK, BLK), :], rc_ref.at[j], rc_send, rc_recv, sib)

    def doc_part(g):
        part = mm(labt[...], e_ref[:, at(g * GRP, GRP)].astype(BF16))
        u_ref[at(g * GRP, GRP), :] = part.T

    def exp_group(p, g, top):
        total = 0.0
        for c in range(ROWS // CH):
            total = total + exp_rows(p, c, top, at(g * GRP, GRP))
        keep(g, top, total)

    def score_pair(i, top):
        @pl.when(i == 1)
        def _():
            slot = doc_slot(place(3), co)
            relay_up(slot).start()
            relay_down(slot).start()

        top = score_step(i * 2, 0, top)

        @pl.when(i == 0)
        def _():
            exp_group(0, g_own, top)
            doc_part(g_own)
            core_copy(g_own).start()
            far()
            ids_out()
            for k in (1, 2, 3):
                take(k)

        @pl.when(i == 1)
        def _():
            take(4)

        @pl.when(i == 2)
        def _():
            find()
            fetch(0)
            take(5)
            take(6)
            fetch(1)
            take(7)
            wait_sib(5)

            def targets(i):
                @pl.when(i == 3)
                def _():
                    wait_sib(6)
                    wait_sib(7)

                target(i)

            each(0, 4, targets)
            each(1, DP, lambda i: t1_copy(i).start())
            each(0, 8, flip)

        top = score_step(i * 2 + 1, 1, top)

        return top

    lg_ref[:, raw_cols(1)] = jnp.zeros((ROWS, GRP), F32)
    top = lax.fori_loop(0, 4, score_pair, jnp.zeros((1, GRP), F32))
    exp_group(1, place(7), top)

    st_ref[1] = st_ref[0] + jnp.log(st_ref[1])
    each(1, LB, lambda i: s1_copy(i).start())
    sst_copy().start()

    def t2_copy(i):
        return remote(tu_ref, tv_ref.at[lb], t2_send, t2_recv, (dp, (lb + i) % LB))

    def t3_copy(i):
        return remote(ca_ref.at[dp, :, 0:256], ca_ref.at[dp, :, 0:256], t3_send, t3_recv, mate(i)[1])

    def targets_on():
        all_in(tr_ref.at[1:DP], t1_recv)
        tr_ref[dp] = ts_ref[dp]
        acc = [jnp.zeros((LB, 128), F32)] * 3
        for q in range(DP):
            slots = tr_ref[q]
            for k in range(SLOTS):
                score, t = slots[:, k:k + 1], slots[:, SLOTS + k:SLOTS + k + 1]
                for v in range(3):
                    acc[v] = acc[v] + jnp.where(lane_t[v] == t, score, 0.0)
        for v in range(3):
            tu_ref[:, v * 128:(v + 1) * 128] = acc[v]
        each(1, LB, lambda i: t2_copy(i).start())

    def spread_16(value):
        for shift in (16, 32, 64):
            value = value + pltpu.roll(value, shift, 1)
        return value

    def positives():
        for q in range(DP):
            ca_ref[q, :, 256:384] = -1.0 - spread_16(ca_ref[q, :, 0:128] + ca_ref[q, :, 128:256])

    def coefficients_on():
        all_in(tv_ref.at[1:LB], t2_recv)
        tv_ref[lb] = tu_ref[...]
        acc = tv_ref[0]
        for q in range(1, LB):
            acc = acc + tv_ref[q]
        lane = lax.broadcasted_iota(jnp.int32, (LB, 128), 1)
        pos = spread_16(jnp.where(lane < SUB, acc[:, 256:384], 0.0))
        soft = jnp.zeros((LB, 128), F32)
        for v in range(2):
            gap = acc[:, v * 128:(v + 1) * 128] - pos + 1.0
            small = jnp.exp(-jnp.abs(gap))
            soft = soft + jnp.maximum(gap, 0.0) + jnp.log(1.0 + small)
            ca_ref[dp, :, v * 128:(v + 1) * 128] = jnp.where(gap >= 0.0, 1.0, small) / (1.0 + small) * (1.0 / 16.0)
        tmp_ref[...] = spread_16(soft) * (1.0 / 16.0) - pos
        each(1, DP, lambda i: t3_copy(i).start())

    targets_on()
    named_copy().start()
    keys_copy().start()

    def doc_mm(k):
        doc_part(place(k))

        core_copy(place(k)).start()

        @pl.when(k == 4)
        def _():
            stats_on()
            coefficients_on()

    each(1, 8, doc_mm)
    totals()
    all_in(rc_ref, rc_recv)
    sst_copy().wait_recv()

    def column(row):
        return jnp.concatenate([jnp.broadcast_to(row, (BLK, BLK)).T] * (D // BLK), axis=1)

    def merge_cores(i):
        out = []
        for q in range(4):
            j = i * 4 + q
            b = j * 2 + co
            log_total = lt_ref[pl.ds(b, 1), :]
            col = column(jnp.exp(st_ref[0, pl.ds(b, 1), :] - log_total))
            scol = column(jnp.exp(sst_ref[pl.ds(b, 1), :] - log_total))
            out.append((b, u_ref[at(b * BLK, BLK), :] * col + rc_ref[j] * scol))
        for b, value in out:
            u_ref[at(b * BLK, BLK), :] = value

    each(0, 2, merge_cores)
    shifted = pltpu.roll(jnp.broadcast_to(lt_ref[pl.ds(dp, 1), :], (8, BLK)), (BLK - lb * SUB) % BLK, 1)
    loss_ref[...] = tmp_ref[pl.ds(lb, 1), :] + shifted[0:1, :]

    all_in(ca_ref.at[1:DP, :, 0:256], t3_recv)
    positives()

    def slot_coef(b, t):
        out = []
        for k in range(SLOTS):
            hit = [jnp.where(lane_t[v] == t[k * 8:k * 8 + 8], ca_ref[b, :, v * 128:(v + 1) * 128], 0.0) for v in range(3)]
            out.append(jnp.sum(hit[0] + hit[1] + hit[2], axis=1, keepdims=True))
        return jnp.concatenate(out, axis=0)

    def scaled_pick(key, coef):
        hi, lo = split(coef)
        pick = doc_pick(key)
        return [jnp.where(pick, hi, 0.0), jnp.where(pick, lo, 0.0)]

    def finish(i):
        out = []
        for q in range(4):
            j = i * 4 + q
            b = j * 2 + co
            key, skey = keys_ref[co, j], skeys_ref[j]
            coef, scoef = slot_coef(b, parts_of(key)[0]), slot_coef(b, parts_of(skey)[0])
            pick = jnp.concatenate(scaled_pick(key, coef) + scaled_pick(skey, scoef), axis=0).T.astype(BF16)
            named, snamed = lrow_ref[co, j], slr_ref[j]
            hard = mm(pick, jnp.concatenate([named, named, snamed, snamed], axis=0))
            out.append((j, coef, C * (u_ref[at(b * BLK, BLK), :] + hard)))
        for j, coef, value in out:
            coef_ref[co, j] = jnp.broadcast_to(coef, (64, 128))
            xx, hh = j // 2, j % 2
            for zz in range(NZ):
                for ll in range(NYL):
                    off = (zz * NYL + ll) * SUB
                    u = value[off:off + SUB]
                    yy = hh * 2 + ll
                    w_ref[0, xx, yy, zz] = u[:, 0:FG]
                    w_ref[1, yy, zz, xx] = u[:, FG:2 * FG]
                    w_ref[2, zz, xx, yy] = u[:, 2 * FG:3 * FG]

    named_copy().wait_recv()
    keys_copy().wait_recv()
    each(0, 2, finish)

    spot = (x, y, z)
    def ring_msg(f, m, p=None):
        h = spot[f]
        up, down = on_axis(f, (h + 1) % 4), on_axis(f, (h + 3) % 4)

        def part(block, which):
            if p is None:
                return w_ref.at[f, block % 4, which * 2:which * 2 + 2]
            return w_ref.at[f, block % 4, which * 2 + p]

        box = q0_ref.at[f, m] if p is None else q0_ref.at[f, m, p]
        if m >= 4:
            source = q0_ref.at[f, m - 4, p]
        else:
            source = (part(h + 2, 0), part(h + 2, 1), part(h + 3, 1), part(h + 1, 0))[m]
        to = (down, up, down, up, down, up)[m]
        return remote(source, box, rs_send.at[0], rs_recv.at[2 if m >= 2 else p], to)

    def ring_start(msgs, p=None):
        for m in msgs:
            for f in range(3):
                ring_msg(f, m, p).start()

    def ring_relay(p):
        all_in(q0_ref.at[:, 0:2, p], rs_recv.at[p])
        for f in range(3):
            h = spot[f]
            for m in range(2):
                block = (h + 3) % 4 if m == 0 else (h + 1) % 4
                q0_ref[f, m, p] = q0_ref[f, m, p] + w_ref[f, block, m * 2 + p]
                ring_msg(f, 4 + m, p).start()

    def ring_done():
        all_in(q0_ref.at[:, 2:6], rs_recv.at[2])
        for f in range(3):
            h = spot[f]
            v1_ref[f, 0:2] = w_ref[f, h, 0:2] + q0_ref[f, 4] + q0_ref[f, 3]
            v1_ref[f, 2:4] = w_ref[f, h, 2:4] + q0_ref[f, 2] + q0_ref[f, 5]

    bufs = {1: (v1_ref, q1_ref), 2: (v2_ref, q2_ref)}

    def straight(step, f, i):
        axis = (f + step) % 3
        to = (spot[axis] + i) % 4
        src, box = bufs[step]
        return remote(src.at[f, to], box.at[f, i - 1], rs_send.at[step], rs_recv.at[step + 2], on_axis(axis, to))

    def straight_start(step):
        for i in (2, 1, 3):
            for f in range(3):
                straight(step, f, i).start()

    def straight_done(step):
        src, box = bufs[step]
        all_in(box, rs_recv.at[step + 2])
        return [src[f, spot[(f + step) % 3]] + box[f, 0] + box[f, 1] + box[f, 2] for f in range(3)]

    ring_start((0, 1), 0)

    def coef_rows(i):
        hi, lo = split(coef_ref[i // 4, pl.ds((i % 4) * 2, 2)].reshape(128, 128).T[0:8, :])
        coeft_ref[0, :, at(i * 128, 128)] = hi
        coeft_ref[1, :, at(i * 128, 128)] = lo

    def other_coef(i):
        out = []
        for q in range(4):
            j = i * 4 + q
            out.append((j, slot_coef(j * 2 + 1 - co, parts_of(keys_ref[1 - co, j])[0])))
        for j, coef in out:
            coef_ref[1 - co, j] = jnp.broadcast_to(coef, (64, 128))

    ring_start((0, 1), 1)
    each(0, 2, other_coef)
    each(0, 8, coef_rows)
    for b in range(DP):
        scale = jnp.exp(st_ref[0, b:b + 1, :] - lt_ref[b:b + 1, :])
        scale_ref[:, b * BLK:(b + 1) * BLK] = jnp.broadcast_to(scale, (8, BLK))

    def label_mm(r):
        rows = at(r * TILE, TILE)
        probs = (e_ref[rows, :] * scale_ref[0:1, :]).astype(BF16)
        sub_rows = (lax.broadcasted_iota(jnp.int32, (TILE, DEV * SLOTS), 0) + r * TILE).astype(F32)
        pick = sub_rows == rowt_ref[0:1, :]
        named = grow_ref[...].reshape(DEV * SLOTS, D)
        value = mm(probs, dall[...].reshape(DOCS, D))
        for p in range(2):
            value = value + mm(jnp.where(pick, coeft_ref[p, 0:1, :], 0.0).astype(BF16), named)
        lg_ref[rows, :] = C * value

        @pl.when(r == 0)
        def _():
            ring_start((2, 3))

        @pl.when(r == 1)
        def _():
            ring_relay(0)

        @pl.when(r == 2)
        def _():
            ring_relay(1)

        @pl.when(r == 4)
        def _():
            ring_done()
            straight_start(1)

        @pl.when(r == 6)
        def _():
            for f, value in enumerate(straight_done(1)):
                v2_ref[f] = value
            straight_start(2)

    each(0, ROWS // TILE, label_mm)

    for f, value in enumerate(straight_done(2)):
        dg_ref[:, f * FG:(f + 1) * FG] = value

    all_out(dall.at[0:7], doc_send)
    all_out(dall.at[0:8], sib_send)
    all_out(rc_ref, rc_send)
    for copy in (sst_copy(), named_copy(), keys_copy()):
        copy.wait_send()
    all_out(idl_ref.at[1:LB], idl_send)
    all_out(idg_ref.at[1:DP], idg_send)
    all_out(sr_ref.at[1:LB], s1_send)
    all_out(sv_ref.at[1:DP], s2_send)
    all_out(tr_ref.at[1:DP], t1_send)
    all_out(tv_ref.at[1:LB], t2_send)
    all_out(ca_ref.at[1:DP, :, 0:256], t3_send)
    all_out(q0_ref, rs_send.at[0])
    all_out(q1_ref, rs_send.at[1])
    all_out(q2_ref, rs_send.at[2])


def ship(lg_in, dg_in, loss_in, lg_out, dg_out, loss_out, sems):
    copies = [pltpu.make_async_copy(lg_in, lg_out, sems.at[0]), pltpu.make_async_copy(dg_in, dg_out, sems.at[1])]
    for copy in copies:
        copy.start()
    loss_out[...] = loss_in[0, 0:SUB]
    for copy in copies:
        copy.wait()


def shards(documents, labels, target_owner, target_row):
    vm = pl.BlockSpec(memory_space=pltpu.VMEM)
    hbm = pl.BlockSpec(memory_space=pl.ANY)
    dma = pltpu.SemaphoreType.DMA
    slots = DEV * SLOTS
    label_grad, doc_grad, loss = pl.pallas_call(
        kernel,
        out_shape=(
            pltpu.VMEM((ROWS, D), F32),
            pltpu.VMEM((SUB, D), F32),
            pltpu.VMEM((1, 128), F32),
        ),
        in_specs=[hbm, hbm, hbm, hbm],
        out_specs=(vm, vm, vm),
        scratch_shapes=[
            pltpu.VMEM((ROWS, D), BF16),
            pltpu.VMEM((DP, BLK, D), BF16),
            pltpu.VMEM((D, ROWS), BF16),
            pltpu.VMEM((ROWS, DOCS), F32),
            pltpu.VMEM((DOCS, D), F32),
            pltpu.VMEM((8, BLK, D), F32),
            pltpu.VMEM((3, 4, 4, 4, SUB, FG), F32),
            pltpu.VMEM((3, 4, 4, SUB, FG), F32),
            pltpu.VMEM((3, 4, SUB, FG), F32),
            pltpu.VMEM((3, 6, 2, 4, SUB, FG), F32),
            pltpu.VMEM((3, 3, 4, SUB, FG), F32),
            pltpu.VMEM((3, 3, SUB, FG), F32),
            pltpu.VMEM((SUB, 1, COLS), jnp.int32),
            pltpu.VMEM((SUB, COLS), jnp.int32),
            pltpu.VMEM((LB, TW), F32),
            pltpu.VMEM((LB, LB, TW), F32),
            pltpu.VMEM((DP, LB, TW), F32),
            pltpu.VMEM((2, 8, 64, 128), F32),
            pltpu.VMEM((8, 64, 128), F32),
            pltpu.VMEM((8, slots), F32),
            pltpu.VMEM((2, 8, 64, D), BF16),
            pltpu.VMEM((8, 64, D), BF16),
            pltpu.VMEM((2, 8, 64, D), BF16),
            pltpu.VMEM((2, DP, BLK), F32),
            pltpu.VMEM((LB, DP, BLK), F32),
            pltpu.VMEM((DP, DP, BLK), F32),
            pltpu.VMEM((DP, BLK), F32),
            pltpu.VMEM((DP, BLK), F32),
            pltpu.VMEM((DP, LB, 128), F32),
            pltpu.VMEM((DP, LB, 128), F32),
            pltpu.VMEM((LB, TW), F32),
            pltpu.VMEM((LB, LB, TW), F32),
            pltpu.VMEM((DP, LB, TW), F32),
            pltpu.VMEM((8, DOCS), F32),
            pltpu.VMEM((LB, 128), F32),
            pltpu.VMEM((2, 8, 64, 128), F32),
            pltpu.VMEM((2, 8, slots), F32),
            dma, dma, dma((2,)), dma, dma((13,)), dma, dma((8,)),
            dma, dma, dma, dma,
            dma, dma, dma, dma, dma((2,)), dma((4,)),
            dma, dma, dma, dma, dma, dma,
            dma, dma, dma((3,)), dma((5,)),
        ],
        compiler_params=pltpu.CompilerParams(
            collective_id=0, has_side_effects=True, vmem_limit_bytes=56 * 1024 * 1024
        ),
        cost_estimate=pl.CostEstimate(
            flops=8 * ROWS * DOCS * D, bytes_accessed=10 * ROWS * D, transcendentals=ROWS * DOCS
        ),
        name="head",
    )(documents, labels, target_owner.transpose(0, 2, 1), target_row)
    label_grad, doc_grad, loss = pl.pallas_call(
        ship,
        out_shape=(
            jax.ShapeDtypeStruct((ROWS, D), F32),
            jax.ShapeDtypeStruct((SUB, D), F32),
            jax.ShapeDtypeStruct((SUB,), F32),
        ),
        in_specs=[vm, vm, vm],
        out_specs=(hbm, hbm, vm),
        scratch_shapes=[dma((2,))],
        compiler_params=pltpu.CompilerParams(vmem_limit_bytes=32 * 1024 * 1024),
        name="ship",
    )(label_grad, doc_grad, loss)
    return loss, doc_grad, label_grad


def solution(mesh):
    return jax.shard_map(
        shards,
        mesh=mesh,
        in_specs=(
            P("dp", None),
            P(("dp", "label"), None),
            P(("dp", "label"), None, None),
            P(("dp", "label"), None),
        ),
        out_specs=(P(("dp", "label")), P(("dp", "label"), None), P(("dp", "label"), None)),
        check_vma=False,
    )
```
